32 devices in a mesh: groups: 2 (over x), sites: 16 (over z, y, core).
Axes of the slice: x: 2, y: 2, z: 4, core: 2. Of those that a mesh axis runs over, the one named last changes fastest.
Arguments:
- state: float32 [64, 128, 128], P(('groups', 'sites')), parts along dimension 0
- left_tensor: float32 [64, 128, 128], P(('groups', 'sites')), parts along dimension 0
- right_tensor: float32 [64, 128, 128], P(('groups', 'sites')), parts along dimension 0
- onsite: float32 [64, 128, 128], P(('groups', 'sites')), parts along dimension 0, may hold values from -6 to 6
- left_env: float32 [256, 8, 128, 128], P(('groups', 'sites')), parts along dimension 0
- right_env: float32 [256, 8, 128, 128], P(('groups', 'sites')), parts along dimension 0
- mpo_bond: float32 [256, 8], P(('groups', 'sites')), parts along dimension 0
- sectors: int32 [8, 8], P('groups'), parts along dimension 0, may hold values from 0 to 7, each once within a row
- flow: int32 [8, 8], P('groups'), parts along dimension 0, may hold values from 0 to 7, each once within a row
Outputs:
- new_state: float32 [64, 128, 128], P(('groups', 'sites')), parts along dimension 0
- energy: float32 [32], P(('groups', 'sites')), parts along dimension 0
The draws below stay inside these ranges and needn't reach their ends.
There are 2 independent parts, one for each index of `groups`. The reference program is written for one: setup_inputs(seed, part) draws one part's arguments, and reference() takes and returns one part's arrays. A program takes and returns all parts, laid end to end along the dimension named above; each array names one. Nothing has to cross between parts.
Inputs may be any that keep to these rules, and one draw needn't show every extreme that they name: Each row of sectors names every sector once. Each row of flow names every sector once.
All inputs are finite; a program needn't handle non-finite values.
Results may differ from the reference program's by a relative error of at most 0.0003.
Values sent between devices are 32-bit elements; how exact they have to be, the bound alone decides.
No kernel may reach another device: no remote copies, remote signals or barrier semaphores. Data moves between devices by JAX's collectives and lax.ppermute only.
A program may use at most 128 MiB of HBM per device.

```python
import math
import jax
import jax.numpy as jnp
from jax import lax

Q = 8
B = 128
GROUP = 4
TERMS_DEV = 8
K = 32
PARTITIONS = 4


def near_identity(key):
    rows = PARTITIONS * Q
    noise = jax.random.normal(key, (rows, B, B), jnp.float32)
    eye = jnp.eye(B, dtype=jnp.float32)
    return (eye + 0.2 * noise / math.sqrt(B)) / math.sqrt(1.04)


def env_terms(key):
    key_noise, key_diag = jax.random.split(key)
    rows = PARTITIONS * K
    noise = jax.random.normal(key_noise, (rows, Q, B, B), jnp.float32)
    sym = (noise + jnp.swapaxes(noise, -1, -2)) / (2.0 * math.sqrt(B))
    diag = jax.random.uniform(key_diag, (rows, Q, 1, 1), jnp.float32, 0.5, 1.5)
    eye = jnp.eye(B, dtype=jnp.float32)
    return (diag * eye + sym) * K ** (-0.25)


def draw_state(key, part):
    key = jax.random.fold_in(key, 11)
    key_main = jax.random.fold_in(key, 0)
    rows = PARTITIONS * Q
    sector = (jnp.arange(rows, dtype=jnp.int32) % Q).astype(jnp.float32)
    ramp = jnp.sqrt(1.0 + 2.0 * sector / (Q - 1))[:, None, None]
    main = jax.random.normal(key_main, (rows, B, B), jnp.float32)
    return main * ramp


def draw_left_tensor(key, part):
    key = jax.random.fold_in(key, 12)
    return near_identity(key)


def draw_right_tensor(key, part):
    key = jax.random.fold_in(key, 13)
    return near_identity(key)


def draw_left_env(key, part):
    key = jax.random.fold_in(key, 14)
    return env_terms(key)


def draw_right_env(key, part):
    key = jax.random.fold_in(key, 15)
    return env_terms(key)


def draw_mpo_bond(key, part):
    key = jax.random.fold_in(key, 16)
    rows = PARTITIONS * K
    noise = jax.random.normal(key, (rows, TERMS_DEV), jnp.float32)
    place = jnp.arange(rows, dtype=jnp.int32) % TERMS_DEV
    eye = (place[:, None] == jnp.arange(TERMS_DEV, dtype=jnp.int32)[None, :]).astype(jnp.float32)
    return (eye + 0.5 * noise / math.sqrt(TERMS_DEV)) / math.sqrt(1.25)


def block_levels(own_key, extent, pieces, low, high):
    level, own = 1.0, jax.random.fold_in(own_key, 6)
    for axis_at, parts in pieces:
        draws = jnp.exp(jax.random.uniform(jax.random.fold_in(own, axis_at), (parts,), jnp.float32, low / len(pieces), high / len(pieces)))
        level = level * jnp.repeat(draws, extent[axis_at] // parts).reshape([-1 if axis == axis_at else 1 for axis in range(len(extent))])
    return level


def bell_draw(key, shape, spread, reach, shards=(), kind=jnp.bfloat16):
    loudness = block_levels(key, shape, shards, -0.22, 0.18) if shards else 1.0
    result = jax.random.normal(key, shape, jnp.float32) * spread * loudness
    return jnp.minimum(jnp.maximum(result, -reach), reach).astype(kind)


def setup_inputs(seed: int = 0, part: int = 0) -> dict:
    arg_keys = jax.random.split(jax.random.key(seed), 10)
    part_keys = jax.random.split(jax.random.fold_in(arg_keys[9], part), 10)
    return {
        "state": draw_state(jax.random.fold_in(jax.random.fold_in(arg_keys[9], part), 71), part),
        "left_tensor": draw_left_tensor(jax.random.fold_in(jax.random.fold_in(arg_keys[9], part), 71), part),
        "right_tensor": draw_right_tensor(jax.random.fold_in(jax.random.fold_in(arg_keys[9], part), 71), part),
        "onsite": bell_draw(part_keys[3], (PARTITIONS * Q, B, B), 1.0, 6.0, ((0, 16),), jnp.float32),
        "left_env": draw_left_env(jax.random.fold_in(jax.random.fold_in(arg_keys[9], part), 71), part),
        "right_env": draw_right_env(jax.random.fold_in(jax.random.fold_in(arg_keys[9], part), 71), part),
        "mpo_bond": draw_mpo_bond(jax.random.fold_in(jax.random.fold_in(arg_keys[9], part), 71), part),
        "sectors": jax.vmap(lambda own: jax.random.permutation(own, Q))(jax.random.split(part_keys[7], PARTITIONS)).reshape((PARTITIONS, Q)).astype(jnp.int32),
        "flow": jax.vmap(lambda own: jax.random.permutation(own, Q))(jax.random.split(part_keys[8], PARTITIONS)).reshape((PARTITIONS, Q)).astype(jnp.int32),
    }


HIGH = lax.Precision.HIGHEST

def sector_onehot(row, width):
    return (row[:, None] == jnp.arange(width, dtype=jnp.int32)[None, :]).astype(jnp.float32)

def left_moved(tensors, env):
    temp = jnp.einsum('kaij,ajl->kail', env, tensors, precision=HIGH)
    return jnp.einsum('aji,kajl->kail', tensors, temp, precision=HIGH)

def right_moved(tensors, env):
    temp = jnp.einsum('aij,kajl->kail', tensors, env, precision=HIGH)
    return jnp.einsum('kaij,alj->kail', temp, tensors, precision=HIGH)

def mix_terms(moved, bonds, onehot):
    shaped = moved.reshape((GROUP, TERMS_DEV) + moved.shape[1:])
    mixed = jnp.einsum('gmn,gmaij->gnaij', bonds, shaped, precision=HIGH).reshape(moved.shape)
    return jnp.einsum('ab,naij->nbij', onehot, mixed, precision=HIGH)

def apply_ham(full_vec, left_use, right_sel):
    temp = jnp.einsum('kaij,ajl->kail', left_use, full_vec, precision=HIGH)
    return jnp.einsum('kail,kalm->aim', temp, right_sel, precision=HIGH)

def ritz_update(alpha1, alpha2, beta, first_vec, second_vec):
    energy = (alpha1 + alpha2) / 2.0 - jnp.sqrt(((alpha1 - alpha2) / 2.0) ** 2 + beta * beta)
    height = jnp.sqrt(beta * beta + (energy - alpha1) ** 2)
    scale = math.sqrt(Q * B * B)
    return (scale * (beta / height * first_vec + (energy - alpha1) / height * second_vec), energy)

def reference(state, left_tensor, right_tensor, onsite, left_env, right_env, mpo_bond, sectors, flow):
    blocks = state.reshape(PARTITIONS, Q, B, B)
    lefts = left_tensor.reshape(PARTITIONS, Q, B, B)
    rights = right_tensor.reshape(PARTITIONS, Q, B, B)
    diags = onsite.reshape(PARTITIONS, Q, B, B)
    lenv = left_env.reshape(PARTITIONS, K, Q, B, B)
    renv = right_env.reshape(PARTITIONS, K, Q, B, B)
    bonds = mpo_bond.reshape(PARTITIONS, GROUP, TERMS_DEV, TERMS_DEV)

    def take(array, where):
        return lax.dynamic_index_in_dim(array, where, 0, keepdims=False)

    def partition_step(index):
        before = jnp.maximum(index - 1, 0).astype(jnp.int32)
        after = jnp.minimum(index + 1, PARTITIONS - 1).astype(jnp.int32)
        from_left = mix_terms(left_moved(take(lefts, before), take(lenv, before)), take(bonds, before), sector_onehot(take(flow, before), Q))
        from_right = mix_terms(right_moved(take(rights, after), take(renv, after)), take(bonds, after), sector_onehot(take(flow, after), Q))
        left_use = jnp.where(index == 0, take(lenv, index), from_left)
        right_use = jnp.where(index == PARTITIONS - 1, take(renv, index), from_right)
        right_sel = jnp.einsum('ac,kcij->kaij', sector_onehot(take(sectors, index), Q), right_use, precision=HIGH)
        vector = take(blocks, index)
        diag = take(diags, index)
        norm_sq = jnp.sum(vector * vector)
        first_vec = vector / jnp.sqrt(norm_sq)
        image = apply_ham(first_vec, left_use, right_sel) + diag * first_vec
        alpha1 = jnp.sum(first_vec * image)
        resid = image - alpha1 * first_vec
        beta = jnp.sqrt(jnp.sum(resid * resid) + 1e-06)
        second_vec = resid / beta
        second = apply_ham(second_vec, left_use, right_sel) + diag * second_vec
        alpha2 = jnp.sum(second_vec * second)
        return ritz_update(alpha1, alpha2, beta, first_vec, second_vec)
    new_blocks, energies = lax.map(partition_step, jnp.arange(PARTITIONS, dtype=jnp.int32))
    return (new_blocks.reshape(PARTITIONS * Q, B, B), jnp.repeat(energies, GROUP))
```

```python
import math

import jax
import jax.numpy as jnp
from jax import lax
from jax.sharding import PartitionSpec as P

GROUP = 4
CHUNKS = (2, 2, 2, 1, 1)

HIGH = lax.Precision.HIGH
HIGHEST = lax.Precision.HIGHEST


def shift(block, distance):
    devices = range(lax.axis_size("sites"))
    route = [(i - distance, i) for i in devices if i - distance in devices]
    return lax.ppermute(block, "sites", route)


def partner(block, mask):
    route = [(i, i ^ mask) for i in range(lax.axis_size("sites"))]
    return lax.ppermute(block, "sites", route)


def group_gather(local, member):
    whole = local
    for bit in range(GROUP.bit_length() - 1):
        other = partner(whole, 1 << bit)
        lower = member >> bit & 1 == 0
        whole = jnp.where(
            lower, jnp.concatenate([whole, other], 0), jnp.concatenate([other, whole], 0)
        )
    return whole


def group_total(value):
    first, second, third = partner(value, 1), partner(value, 2), partner(value, 3)
    return (value + first) + (second + third)


def inverse(row):
    labels = jnp.arange(row.shape[0], dtype=jnp.int32)
    return jnp.sum(jnp.where(row[None, :] == labels[:, None], labels[None, :], 0), axis=1)


def row_of(table, index):
    return lax.dynamic_index_in_dim(table, jnp.clip(index, 0, table.shape[0] - 1), 0, False)


def pick(env, order):
    return jnp.stack(
        [lax.dynamic_index_in_dim(env, order[j], 1, False) for j in range(order.shape[0])], 0
    )


def weighted(env_left, env_right, bond, middle):
    mixed = jnp.einsum("mn,snij->smij", bond, env_right, precision=HIGHEST)
    temp = jnp.einsum("smij,sjl->smil", env_left, middle, precision=HIGH)
    return mixed, jnp.einsum("smil,smlk->sik", temp, mixed, precision=HIGH)


def on_device(
    state, left_tensor, right_tensor, onsite, left_env, right_env, mpo_bond, sectors, flow
):
    position = lax.axis_index("sites")
    partition = position // GROUP
    member = position % GROUP
    first = partition == 0
    last = partition == lax.axis_size("sites") // GROUP - 1
    own, size = state.shape[0], state.shape[1]
    terms, total = left_env.shape[0], left_env.shape[1]
    eye = jnp.eye(size, dtype=jnp.float32)

    here = inverse(row_of(flow, partition))
    joined = row_of(sectors, partition)
    send_left = here
    send_right = here[row_of(sectors, partition - 1)]
    pos_left = inverse(row_of(flow, partition - 1))
    pos_right = inverse(row_of(flow, partition + 1))[joined]

    bond_rows = jnp.pad(mpo_bond, ((0, 0), (0, size - mpo_bond.shape[1])))
    note = lambda tensor: jnp.concatenate([tensor.reshape(own * size, size), bond_rows], 0)
    from_left = shift(note(left_tensor), GROUP)
    from_right = shift(note(right_tensor), -GROUP)

    starts = [sum(CHUNKS[:i]) for i in range(len(CHUNKS))]
    got = []
    for i, (begin, width) in enumerate(zip(starts, CHUNKS)):
        to_right, to_left = send_left[begin : begin + width], send_right[begin : begin + width]
        if i >= 2:
            to_right, _ = lax.optimization_barrier((to_right, got[i - 2][0]))
            to_left, _ = lax.optimization_barrier((to_left, got[i - 2][1]))
        got.append(
            (shift(pick(left_env, to_right), GROUP), shift(pick(right_env, to_left), -GROUP))
        )

    def edge(flag, block):
        tensor = jnp.where(flag, eye, block[: own * size].reshape(own, size, size))
        small = jnp.eye(terms, dtype=jnp.float32)
        return tensor, jnp.where(flag, small, block[own * size :, : mpo_bond.shape[1]])

    tensor_left, bond_left = edge(first, from_left)
    tensor_right, bond_right = edge(last, from_right)
    bond = jnp.einsum("mn,kn->mk", bond_left, bond_right, precision=HIGHEST)
    gathered = group_gather(jnp.stack([state, tensor_left, tensor_right], 1), member)
    vector = gathered[:, 0]
    outer_left = jnp.take(gathered[:, 1], pos_left, axis=0)
    outer_right = jnp.take(gathered[:, 2], pos_right, axis=0)
    diagonal = lax.dynamic_update_slice_in_dim(
        jnp.zeros_like(vector), onsite, member * own, 0
    )

    def inward(block, a, b):
        return jnp.einsum(
            "sil,slm->sim",
            jnp.einsum("sij,sjl->sil", a, block, precision=HIGHEST),
            b,
            precision=HIGHEST,
        )

    norm_sq = jnp.sum(vector * vector)
    first_vec = vector / jnp.sqrt(norm_sq)
    middle = inward(first_vec, outer_left, outer_right)
    back_left, back_right = jnp.swapaxes(outer_left, 1, 2), jnp.swapaxes(outer_right, 1, 2)

    kept, images = [], []
    for i, (begin, width) in enumerate(zip(starts, CHUNKS)):
        at = slice(begin, begin + width)
        own_left = jnp.moveaxis(left_env[:, at], 1, 0)
        use_left = jnp.where(first, own_left, got[i][0])
        use_right = jnp.where(last, pick(right_env, joined[at]), got[i][1])
        mixed, core = weighted(use_left, use_right, bond, middle[at])
        kept.append((use_left, mixed))
        part = inward(core, back_left[at], back_right[at]) + diagonal[at] * first_vec[at]
        images.append(group_total(part))
    image = jnp.concatenate(images, 0)
    alpha1 = jnp.sum(first_vec * image)
    resid = image - alpha1 * first_vec
    beta = jnp.sqrt(jnp.sum(resid * resid) + 1e-06)
    second_vec = resid / beta
    middle = inward(second_vec, outer_left, outer_right)
    share = jnp.sum(diagonal * second_vec * second_vec)
    for (begin, width), (use_left, mixed) in zip(zip(starts, CHUNKS), kept):
        at = slice(begin, begin + width)
        temp = jnp.einsum("smij,sjl->smil", use_left, middle[at], precision=HIGH)
        core = jnp.einsum("smil,smlk->sik", temp, mixed, precision=HIGH)
        share = share + jnp.sum(middle[at] * core)
    alpha2 = group_total(share)

    energy = (alpha1 + alpha2) / 2.0 - jnp.sqrt(((alpha1 - alpha2) / 2.0) ** 2 + beta * beta)
    height = jnp.sqrt(beta * beta + (energy - alpha1) ** 2)
    scale = math.sqrt(total * size * size)
    mine = lambda block: lax.dynamic_slice_in_dim(block, member * own, own, 0)
    new_state = scale * (
        beta / height * mine(first_vec) + (energy - alpha1) / height * mine(second_vec)
    )
    return (new_state, jnp.reshape(energy, (1,)))


def solution(mesh):
    return jax.shard_map(
        on_device,
        mesh=mesh,
        in_specs=(
            P(("groups", "sites"), None, None),
            P(("groups", "sites"), None, None),
            P(("groups", "sites"), None, None),
            P(("groups", "sites"), None, None),
            P(("groups", "sites"), None, None, None),
            P(("groups", "sites"), None, None, None),
            P(("groups", "sites"), None),
            P("groups", None),
            P("groups", None),
        ),
        out_specs=(P(("groups", "sites"), None, None), P(("groups", "sites"))),
        check_vma=False,
    )
```

```python
import functools
import math

import jax
import jax.numpy as jnp
from jax import lax
from jax.experimental import pallas as pl
from jax.experimental.pallas import tpu as pltpu
from jax.sharding import PartitionSpec as P

GROUP = 4
VMEM_LIMIT = 48 * 1024 * 1024

HIGHEST = lax.Precision.HIGHEST


def shift(block, distance):
    devices = range(lax.axis_size("sites"))
    route = [(i - distance, i) for i in devices if i - distance in devices]
    return lax.ppermute(block, "sites", route)


def partner(block, mask):
    route = [(i, i ^ mask) for i in range(lax.axis_size("sites"))]
    return lax.ppermute(block, "sites", route)


def inverse(row):
    labels = jnp.arange(row.shape[0], dtype=jnp.int32)
    return jnp.sum(jnp.where(row[None, :] == labels[:, None], labels[None, :], 0), axis=1)


def row_of(table, index):
    return lax.dynamic_index_in_dim(table, jnp.clip(index, 0, table.shape[0] - 1), 0, False)


def halves(value):
    high = value.astype(jnp.bfloat16)
    return high, (value - high.astype(jnp.float32)).astype(jnp.bfloat16)


def split_left(value):
    return jnp.concatenate(halves(value), axis=1)


def split_right(value):
    high, low = halves(value)
    return jnp.concatenate(
        [
            jnp.concatenate([high, low], axis=1),
            jnp.concatenate([high, jnp.zeros_like(low)], axis=1),
        ],
        axis=0,
    )


def fold(wide):
    half = wide.shape[1] // 2
    return wide[:, :half] + wide[:, half:]


def product(left, right):
    return fold(jnp.dot(split_left(left), split_right(right), preferred_element_type=jnp.float32))


def core_of(env_split, mixed_split, middle_split, terms):
    size = mixed_split.shape[0] // terms
    temp = fold(jnp.dot(env_split, middle_split, preferred_element_type=jnp.float32))
    high, low = halves(temp)
    wide = lambda part: jnp.concatenate(
        [part[m * size : (m + 1) * size] for m in range(terms)], axis=1
    )
    out = jnp.dot(
        jnp.concatenate([wide(high), wide(low)], axis=0),
        mixed_split,
        preferred_element_type=jnp.float32,
    )
    return fold(out[:size]) + out[size:, :size]


def prepare_kernel(own, table, pieces, vec_out, middle_out, left_out, right_out, back_out):
    total, size = vec_out.shape[0], vec_out.shape[1]
    row = lax.broadcasted_iota(jnp.int32, (size, size), 0)
    col = lax.broadcasted_iota(jnp.int32, (size, size), 1)
    eye = (row == col).astype(jnp.float32)
    member = table[2]

    def block(sector, kind):
        return pieces[(sector // own) ^ member, sector % own, kind]

    square = jnp.zeros((size, size), jnp.float32)
    for j in range(total):
        value = block(jnp.int32(j), 0)
        square = square + value * value
    norm = jnp.sqrt(jnp.sum(square))

    def body(j, carry):
        vec = block(j, 0) / norm
        left = jnp.where(table[0] == 1, eye, block(table[3 + j], 1))
        right = jnp.where(table[1] == 1, eye, block(table[3 + total + j], 2))
        vec_out[j] = vec
        left_out[j] = split_left(left)
        right_out[j] = split_right(right)
        back_out[j, 0] = jnp.transpose(left)
        back_out[j, 1] = jnp.transpose(right)
        middle_out[j] = split_right(product(product(left, vec), right))
        return carry

    lax.fori_loop(0, total, body, 0)


def first_kernel(
    own, table, bond, left_got, left_own, right_got, right_own, middle, vec, back, onsite,
    env_out, mixed_out, part_out,
):
    step = pl.program_id(0)
    terms, size = left_got.shape[0], left_got.shape[-1]
    first, last, member = table[0] == 1, table[1] == 1, table[2]

    def store_left(ref):
        for m in range(terms):
            env_out[0, m * size : (m + 1) * size] = split_left(ref[m, 0])

    def store_right(ref):
        for m in range(terms):
            total = bond[m, 0] * ref[0, 0]
            for k in range(1, terms):
                total = total + bond[m, k] * ref[k, 0]
            mixed_out[0, m * size : (m + 1) * size] = split_left(total)

    pl.when(first)(lambda: store_left(left_own))
    pl.when(jnp.logical_not(first))(lambda: store_left(left_got))
    pl.when(last)(lambda: store_right(right_own))
    pl.when(jnp.logical_not(last))(lambda: store_right(right_got))
    core = core_of(env_out[0], mixed_out[0], middle[0], terms)
    part = product(product(back[0, 0], core), back[0, 1])
    mine = (step // own == member).astype(jnp.float32)
    part_out[0] = part + (mine * onsite[0]) * vec[0]


def second_kernel(
    own, table, part0, part1, part2, part3, vec, left, right, onsite, env_hbm, mixed_hbm,
    second_out, share_out, env, mixed, middle, work, sems,
):
    total, size = vec.shape[0], vec.shape[1]
    terms = mixed.shape[1] // size
    member = table[2]

    def copies(j):
        return (
            pltpu.make_async_copy(env_hbm.at[j], env.at[j], sems.at[0, j]),
            pltpu.make_async_copy(mixed_hbm.at[j], mixed.at[j], sems.at[1, j]),
        )

    for j in range(total):
        for copy in copies(j):
            copy.start()

    dot = jnp.zeros((size, size), jnp.float32)
    for j in range(total):
        image = (part0[j] + part1[j]) + (part2[j] + part3[j])
        work[j] = image
        dot = dot + vec[j] * image
    alpha1 = jnp.sum(dot)
    square = jnp.zeros((size, size), jnp.float32)
    for j in range(total):
        resid = work[j] - alpha1 * vec[j]
        work[j] = resid
        square = square + resid * resid
    beta = jnp.sqrt(jnp.full((8, 128), jnp.sum(square) + 1e-06, jnp.float32))
    scale = 1.0 / beta[0:1, :]

    def inward(j, carry):
        value = work[j] * scale
        work[j] = value
        temp = fold(jnp.dot(left[j], split_right(value), preferred_element_type=jnp.float32))
        moved = fold(
            jnp.dot(split_left(temp), right[j], preferred_element_type=jnp.float32)
        )
        middle[j] = moved
        return carry

    lax.fori_loop(0, total, inward, 0)

    def outward(j, carry):
        for copy in copies(j):
            copy.wait()
        value = middle[j]
        core = core_of(env[j], mixed[j], split_right(value), terms)
        return carry + value * core

    share = lax.fori_loop(0, total, outward, jnp.zeros((size, size), jnp.float32))
    for i in range(own):
        mine = work[member * own + i]
        second_out[i] = mine
        share = share + (onsite[i] * mine) * mine
    share_out[0] = jnp.full((8, 128), jnp.sum(share), jnp.float32)
    share_out[1] = jnp.full((8, 128), alpha1, jnp.float32)
    share_out[2] = beta


def final_kernel(own, count, table, share0, share1, share2, share3, vec, second, out, energy_out):
    member = table[2]
    alpha2 = (share0[0] + share1[0]) + (share2[0] + share3[0])
    alpha1, beta = share0[1], share0[2]
    energy = (alpha1 + alpha2) / 2.0 - jnp.sqrt(((alpha1 - alpha2) / 2.0) ** 2 + beta * beta)
    height = jnp.sqrt(beta * beta + (energy - alpha1) ** 2)
    scale = math.sqrt(count)
    weight1 = (scale * (beta / height))[0:1]
    weight2 = (scale * ((energy - alpha1) / height))[0:1]
    for i in range(own):
        out[i] = weight1 * vec[member * own + i] + weight2 * second[i]
    energy_out[...] = energy


def on_device(
    state, left_tensor, right_tensor, onsite, left_env, right_env, mpo_bond, sectors, flow
):
    position = lax.axis_index("sites")
    partition = position // GROUP
    member = position % GROUP
    first = partition == 0
    last = partition == lax.axis_size("sites") // GROUP - 1
    own, size = state.shape[0], state.shape[1]
    terms, total = left_env.shape[0], left_env.shape[1]
    f32, bf16 = jnp.float32, jnp.bfloat16

    bond_rows = jnp.pad(mpo_bond, ((0, 0), (0, size - mpo_bond.shape[1])))
    note = lambda tensor: jnp.concatenate([tensor.reshape(own * size, size), bond_rows], 0)
    from_left = shift(note(left_tensor), GROUP)
    from_right = shift(note(right_tensor), -GROUP)
    left_got = shift(left_env, GROUP)
    right_got = shift(right_env, -GROUP)

    joined = row_of(sectors, partition)
    pos_left = inverse(row_of(flow, partition - 1))
    pos_right = inverse(row_of(flow, partition + 1))[joined]
    as_int = lambda value: jnp.reshape(value.astype(jnp.int32), (1,))
    table = jnp.concatenate(
        [as_int(first), as_int(last), as_int(member), pos_left, pos_right, joined]
    )

    small = jnp.eye(terms, dtype=f32)
    bond_left = jnp.where(first, small, from_left[own * size :, : mpo_bond.shape[1]])
    bond_right = jnp.where(last, small, from_right[own * size :, : mpo_bond.shape[1]])
    bond = jnp.sum(bond_left[:, None, :] * bond_right[None, :, :], axis=2)

    tensors = lambda block: block[: own * size].reshape(own, size, size)
    stacked = jnp.stack([state, tensors(from_left), tensors(from_right)], 1)
    pieces = jnp.stack([stacked] + [partner(stacked, mask) for mask in (1, 2, 3)], 0)

    params = pltpu.CompilerParams(vmem_limit_bytes=VMEM_LIMIT)
    smem = pl.BlockSpec(memory_space=pltpu.SMEM)
    vmem = pl.BlockSpec(memory_space=pltpu.VMEM)
    anywhere = pl.BlockSpec(memory_space=pl.ANY)
    shape = jax.ShapeDtypeStruct

    vec, middle, left, right, back = pl.pallas_call(
        functools.partial(prepare_kernel, own),
        in_specs=[smem, vmem],
        out_specs=[vmem] * 5,
        out_shape=[
            shape((total, size, size), f32),
            shape((total, 2 * size, 2 * size), bf16),
            shape((total, size, 2 * size), bf16),
            shape((total, 2 * size, 2 * size), bf16),
            shape((total, 2, size, size), f32),
        ],
        compiler_params=params,
        name="prepare",
    )(table, pieces)

    env_block = (terms, 1, size, size)
    at_left_got = lambda j, t: (0, jnp.where(t[0] == 1, 0, t[3 + j]), 0, 0)
    at_left_own = lambda j, t: (0, jnp.where(t[0] == 1, j, 0), 0, 0)
    at_right_got = lambda j, t: (0, jnp.where(t[1] == 1, 0, t[3 + total + j]), 0, 0)
    at_right_own = lambda j, t: (0, jnp.where(t[1] == 1, t[3 + 2 * total + j], 0), 0, 0)
    by_sector = lambda *dims: pl.BlockSpec((1, *dims), lambda j, t: (j,) + (0,) * len(dims))
    env, mixed, part = pl.pallas_call(
        functools.partial(first_kernel, own),
        grid_spec=pltpu.PrefetchScalarGridSpec(
            num_scalar_prefetch=1,
            grid=(total,),
            in_specs=[
                smem,
                pl.BlockSpec(env_block, at_left_got),
                pl.BlockSpec(env_block, at_left_own),
                pl.BlockSpec(env_block, at_right_got),
                pl.BlockSpec(env_block, at_right_own),
                by_sector(2 * size, 2 * size),
                by_sector(size, size),
                by_sector(2, size, size),
                pl.BlockSpec((1, size, size), lambda j, t: (j % own, 0, 0)),
            ],
            out_specs=[
                by_sector(terms * size, 2 * size),
                by_sector(terms * size, 2 * size),
                by_sector(size, size),
            ],
        ),
        out_shape=[
            shape((total, terms * size, 2 * size), bf16),
            shape((total, terms * size, 2 * size), bf16),
            shape((total, size, size), f32),
        ],
        compiler_params=params,
        name="first_matvec",
    )(table, bond, left_got, left_env, right_got, right_env, middle, vec, back, onsite)

    parts = [part] + [partner(part, mask) for mask in (1, 2, 3)]
    second, share = pl.pallas_call(
        functools.partial(second_kernel, own),
        in_specs=[smem] + [vmem] * 8 + [anywhere] * 2,
        out_specs=[vmem] * 2,
        out_shape=[shape((own, size, size), f32), shape((3, 8, 128), f32)],
        scratch_shapes=[
            pltpu.VMEM((total, terms * size, 2 * size), bf16),
            pltpu.VMEM((total, terms * size, 2 * size), bf16),
            pltpu.VMEM((total, size, size), f32),
            pltpu.VMEM((total, size, size), f32),
            pltpu.SemaphoreType.DMA((2, total)),
        ],
        compiler_params=params,
        name="second_matvec",
    )(table, *parts, vec, left, right, onsite, env, mixed)

    shares = [share] + [partner(share[:1], mask) for mask in (1, 2, 3)]
    new_state, energy = pl.pallas_call(
        functools.partial(final_kernel, own, total * size * size),
        in_specs=[smem] + [vmem] * 6,
        out_specs=[vmem] * 2,
        out_shape=[shape((own, size, size), f32), shape((8, 128), f32)],
        compiler_params=params,
        name="ritz_update",
    )(table, *shares, vec, second)
    return (new_state, energy[0, :1])


def solution(mesh):
    return jax.shard_map(
        on_device,
        mesh=mesh,
        in_specs=(
            P(("groups", "sites"), None, None),
            P(("groups", "sites"), None, None),
            P(("groups", "sites"), None, None),
            P(("groups", "sites"), None, None),
            P(("groups", "sites"), None, None, None),
            P(("groups", "sites"), None, None, None),
            P(("groups", "sites"), None),
            P("groups", None),
            P("groups", None),
        ),
        out_specs=(P(("groups", "sites"), None, None), P(("groups", "sites"))),
        check_vma=False,
    )
```

```python
import functools
import math

import jax
import jax.numpy as jnp
from jax import lax
from jax.experimental import pallas as pl
from jax.experimental.pallas import tpu as pltpu
from jax.sharding import PartitionSpec as P

GROUP = 4
CHUNKS = (4, 3, 1)
MIB = 1024 * 1024


def shift(block, distance):
    devices = range(lax.axis_size("sites"))
    route = [(i - distance, i) for i in devices if i - distance in devices]
    return lax.ppermute(block, "sites", route)


def partner(block, mask):
    route = [(i, i ^ mask) for i in range(lax.axis_size("sites"))]
    return lax.ppermute(block, "sites", route)


def gather(block):
    across = partner(block, 2)
    beside = partner(jnp.stack([block, across], 0), 1)
    return jnp.stack([block, beside[0], across, beside[1]], 0)


def total_of(block):
    pair = block + partner(block, 1)
    return pair + partner(pair, 2)


def halves(value):
    high = value.astype(jnp.bfloat16)
    return high, (value - high.astype(jnp.float32)).astype(jnp.bfloat16)


def split_left(value):
    return jnp.concatenate(halves(value), axis=1)


def split_right(value):
    high, low = halves(value)
    return jnp.concatenate(
        [
            jnp.concatenate([high, low], axis=1),
            jnp.concatenate([high, jnp.zeros_like(low)], axis=1),
        ],
        axis=0,
    )


def fold(wide):
    half = wide.shape[1] // 2
    return wide[:, :half] + wide[:, half:]


def product(left, right):
    return fold(jnp.dot(split_left(left), split_right(right), preferred_element_type=jnp.float32))


def core_of(env_split, mixed_split, middle_split, terms):
    size = mixed_split.shape[0] // terms
    temp = fold(jnp.dot(env_split, middle_split, preferred_element_type=jnp.float32))
    high, low = halves(temp)
    wide = lambda part: jnp.concatenate(
        [part[m * size : (m + 1) * size] for m in range(terms)], axis=1
    )
    out = jnp.dot(
        jnp.concatenate([wide(high), wide(low)], axis=0),
        mixed_split,
        preferred_element_type=jnp.float32,
    )
    return fold(out[:size]) + out[size:, :size]


def pick(table, left_env, right_env, to_right, to_left, sems, begin, width):
    terms, total, size = left_env.shape[:3]
    first, last = table[0] == 1, table[1] == 1

    def copies(side, env, base, out):
        return [
            pltpu.make_async_copy(
                env.at[:, begin + s if base is None else table[base + begin + s]],
                out.at[pl.ds(s * terms * size, terms * size)].reshape(terms, size, size),
                sems.at[side, begin + s],
            )
            for s in range(width)
        ]

    def start(flag, usual, edge):
        pl.when(jnp.logical_not(flag))(lambda: [copy.start() for copy in usual] and None)
        pl.when(flag)(lambda: [copy.start() for copy in edge] and None)

    right = copies(0, left_env, 3 + 3 * total, to_right)
    left = copies(1, right_env, 3 + 4 * total, to_left)
    start(last, right, copies(0, right_env, 3 + 2 * total, to_right))
    start(first, left, copies(1, left_env, None, to_left))
    return right + left


def open_kernel(
    chunks, parts, place_hbm, sectors_hbm, flow_hbm, bond_hbm, left_tensor, right_tensor,
    left_env, right_env, table, *refs,
):
    outs, refs = refs[: 2 * len(chunks)], refs[2 * len(chunks) :]
    place, sectors, flow, order, bond, small, sems, more, some = refs
    own, size = left_tensor.shape[0], left_tensor.shape[1]
    terms, total = left_env.shape[0], left_env.shape[1]
    width = chunks[0]
    base = width * terms * size
    copies = [
        pltpu.make_async_copy(tensor.at[i], out.at[pl.ds(base + i * size, size)], more.at[side, i])
        for side, (tensor, out) in enumerate(((left_tensor, outs[0]), (right_tensor, outs[1])))
        for i in range(own)
    ]
    inputs = ((place_hbm, place), (sectors_hbm, sectors), (flow_hbm, flow), (bond_hbm, bond))
    loads = [pltpu.make_async_copy(a, b, some.at[i]) for i, (a, b) in enumerate(inputs)]
    for copy in loads + copies:
        copy.start()
    for copy in loads:
        copy.wait()
    partition = place[0] // GROUP
    before = jnp.maximum(partition - 1, 0)
    after = jnp.minimum(partition + 1, parts - 1)
    table[0] = (partition == 0).astype(jnp.int32)
    table[1] = (partition == parts - 1).astype(jnp.int32)
    table[2] = place[0] % GROUP
    for j in range(total):
        order[flow[before, j]] = j
        order[total + flow[partition, j]] = j
        order[2 * total + flow[after, j]] = j
    for j in range(total):
        joined = sectors[partition, j]
        table[3 + j] = order[j]
        table[3 + total + j] = order[2 * total + joined]
        table[3 + 2 * total + j] = joined
        table[3 + 3 * total + j] = order[total + j]
        table[3 + 4 * total + j] = order[total + sectors[before, j]]
    begin = 0
    for c, count in enumerate(chunks):
        copies += pick(
            table, left_env, right_env, outs[2 * c], outs[2 * c + 1], sems, begin, count
        )
        begin += count
    small[...] = jnp.zeros_like(small)
    small[:, : bond.shape[1]] = bond[...]
    for side in range(2):
        copy = pltpu.make_async_copy(
            small, outs[side].at[pl.ds(base + own * size, terms)], more.at[side, own]
        )
        copy.start()
        copies.append(copy)
    for copy in copies:
        copy.wait()


def prepare_kernel(own, table, states, pieces, vec_out, middle_out, left_out, right_out, back_out):
    total, size = vec_out.shape[0], vec_out.shape[1]
    row = lax.broadcasted_iota(jnp.int32, (size, size), 0)
    col = lax.broadcasted_iota(jnp.int32, (size, size), 1)
    eye = (row == col).astype(jnp.float32)
    member = table[2]

    def block(sector, kind):
        return pieces[(sector // own) ^ member, sector % own, kind]

    def state_of(sector):
        return states[(sector // own) ^ member, sector % own]

    square = jnp.zeros((size, size), jnp.float32)
    for j in range(total):
        value = state_of(j)
        square = square + value * value
    norm = jnp.sqrt(jnp.sum(square))

    def body(j, carry):
        vec = state_of(j) / norm
        left = jnp.where(table[0] == 1, eye, block(table[3 + j], 0))
        right = jnp.where(table[1] == 1, eye, block(table[3 + total + j], 1))
        vec_out[j] = vec
        left_out[j] = split_left(left)
        right_out[j] = split_right(right)
        back_out[j, 0] = jnp.transpose(left)
        back_out[j, 1] = jnp.transpose(right)
        middle_out[j] = split_right(product(product(left, vec), right))
        return carry

    lax.fori_loop(0, total, body, 0)


def first_kernel(
    own, begin, table, bond, left_got, left_own, right_got, right_own, middle, vec, back, onsite,
    env_out, mixed_out, part_out,
):
    size = vec.shape[-1]
    terms = bond.shape[0]
    first, last, member = table[0] == 1, table[1] == 1, table[2]
    rows = lambda s, m: slice((s * terms + m) * size, (s * terms + m + 1) * size)

    for s in range(part_out.shape[0]):
        for m in range(terms):
            block = jnp.where(first, left_own[rows(s, m)], left_got[rows(s, m)])
            env_out[s, rows(0, m)] = split_left(block)
        blocks = [jnp.where(last, right_own[rows(s, m)], right_got[rows(s, m)]) for m in range(terms)]
        for m in range(terms):
            total = bond[m, 0] * blocks[0]
            for k in range(1, terms):
                total = total + bond[m, k] * blocks[k]
            mixed_out[s, rows(0, m)] = split_left(total)
        j = begin + s
        core = core_of(env_out[s], mixed_out[s], middle[j], terms)
        part = product(product(back[j, 0], core), back[j, 1])
        mine = (j // own == member).astype(jnp.float32)
        part_out[s] = part + (mine * onsite[j % own]) * vec[j]


def second_kernel(own, early, table, image, part0, part1, part2, part3, *refs):
    vec, left, right, onsite, *refs = refs
    count = len(CHUNKS)
    env_parts, mixed_parts, refs = refs[:count], refs[count : 2 * count], refs[2 * count :]
    second_out, share_out, work, middle = refs
    total, size = vec.shape[0], vec.shape[1]
    terms = mixed_parts[0].shape[1] // size
    member = table[2]
    home = [(c, s) for c, width in enumerate(CHUNKS) for s in range(width)]

    dot = jnp.zeros((size, size), jnp.float32)
    for j in range(total):
        if j < early:
            value = image[j]
        else:
            i = j - early
            value = (part0[i] + part1[i]) + (part2[i] + part3[i])
        work[j] = value
        dot = dot + vec[j] * value
    alpha1 = jnp.sum(dot)
    square = jnp.zeros((size, size), jnp.float32)
    for j in range(total):
        resid = work[j] - alpha1 * vec[j]
        work[j] = resid
        square = square + resid * resid
    beta = jnp.sqrt(jnp.full((8, 128), jnp.sum(square) + 1e-06, jnp.float32))
    scale = 1.0 / beta[0:1, :]

    for j in range(total):
        value = work[j] * scale
        work[j] = value
        temp = fold(jnp.dot(left[j], split_right(value), preferred_element_type=jnp.float32))
        middle[j] = fold(
            jnp.dot(split_left(temp), right[j], preferred_element_type=jnp.float32)
        )

    share = jnp.zeros((size, size), jnp.float32)
    for j, (c, s) in enumerate(home):
        value = middle[j]
        core = core_of(env_parts[c][s], mixed_parts[c][s], split_right(value), terms)
        share = share + value * core
    for i in range(own):
        mine = work[member * own + i]
        second_out[i] = mine
        share = share + (onsite[i] * mine) * mine
    share_out[0] = jnp.full((8, 128), jnp.sum(share), jnp.float32)
    share_out[1] = jnp.full((8, 128), alpha1, jnp.float32)
    share_out[2] = beta


def final_kernel(own, count, table, share0, share1, share2, share3, vec, second, out, energy_out):
    member = table[2]
    alpha2 = (share0[0] + share1[0]) + (share2[0] + share3[0])
    alpha1, beta = share0[1], share0[2]
    energy = (alpha1 + alpha2) / 2.0 - jnp.sqrt(((alpha1 - alpha2) / 2.0) ** 2 + beta * beta)
    height = jnp.sqrt(beta * beta + (energy - alpha1) ** 2)
    scale = math.sqrt(count)
    weight1 = (scale * (beta / height))[0:1]
    weight2 = (scale * ((energy - alpha1) / height))[0:1]
    for i in range(own):
        out[i] = weight1 * vec[member * own + i] + weight2 * second[i]
    energy_out[0] = energy[0, 0]


def on_device(
    state, left_tensor, right_tensor, onsite, left_env, right_env, mpo_bond, sectors, flow
):
    position = lax.axis_index("sites")
    parts = lax.axis_size("sites") // GROUP
    own, size = state.shape[0], state.shape[1]
    terms, total = left_env.shape[0], left_env.shape[1]
    f32, bf16 = jnp.float32, jnp.bfloat16
    begins = [sum(CHUNKS[:c]) for c in range(len(CHUNKS))]
    early = begins[-1]

    smem = pl.BlockSpec(memory_space=pltpu.SMEM)
    vmem = pl.BlockSpec(memory_space=pltpu.VMEM)
    hbm = pl.BlockSpec(memory_space=pltpu.HBM)
    shape = jax.ShapeDtypeStruct
    dma = pltpu.SemaphoreType.DMA
    params = lambda mib: pltpu.CompilerParams(vmem_limit_bytes=mib * MIB)

    small_cost = pl.CostEstimate(flops=1, bytes_accessed=1, transcendentals=0)

    rows = lambda width: width * terms * size
    chunk = lambda c: (rows(CHUNKS[c]) + (own * size + terms if c == 0 else 0), size)
    pair = lambda sent: (shift(sent[0], GROUP), shift(sent[1], -GROUP))
    table, *opened = pl.pallas_call(
        functools.partial(open_kernel, CHUNKS, parts),
        in_specs=[hbm] * 8,
        out_specs=[smem] + [vmem] * (2 * len(CHUNKS)),
        out_shape=[shape((3 + 5 * total,), jnp.int32)]
        + [pltpu.VMEM(chunk(c), f32) for c in range(len(CHUNKS)) for _ in range(2)],
        scratch_shapes=[
            pltpu.SMEM((1,), jnp.int32),
            pltpu.SMEM(sectors.shape, jnp.int32),
            pltpu.SMEM(flow.shape, jnp.int32),
            pltpu.SMEM((3 * total,), jnp.int32),
            pltpu.VMEM(mpo_bond.shape, f32),
            pltpu.VMEM((terms, size), f32),
            dma((2, total)),
            dma((2, own + 1)),
            dma((4,)),
        ],
        cost_estimate=small_cost,
        compiler_params=params(16),
        name="open",
    )(
        *(
            pltpu.with_memory_space_constraint(value, pltpu.HBM)
            for value in (
                jnp.reshape(position, (1,)).astype(jnp.int32), sectors, flow, mpo_bond,
                left_tensor, right_tensor, left_env, right_env,
            )
        )
    )
    sent, got = [], []
    for c in range(len(CHUNKS)):
        buffers = tuple(opened[2 * c : 2 * c + 2])
        sent.append(buffers)
        got.append(pair(buffers))
    states = gather(state)

    from_left, from_right = (block[rows(CHUNKS[0]) :] for block in got[0])
    small = jnp.eye(terms, dtype=f32)
    bond_left = jnp.where(table[0] == 1, small, from_left[own * size :, : mpo_bond.shape[1]])
    bond_right = jnp.where(table[1] == 1, small, from_right[own * size :, : mpo_bond.shape[1]])
    bond = jnp.sum(bond_left[:, None, :] * bond_right[None, :, :], axis=2)
    tensors = lambda block: block[: own * size].reshape(own, size, size)
    pieces = gather(jnp.stack([tensors(from_left), tensors(from_right)], 1))

    vec, middle, left, right, back = pl.pallas_call(
        functools.partial(prepare_kernel, own),
        in_specs=[smem, vmem, vmem],
        out_specs=[vmem] * 5,
        out_shape=[
            shape((total, size, size), f32),
            shape((total, 2 * size, 2 * size), bf16),
            shape((total, size, 2 * size), bf16),
            shape((total, 2 * size, 2 * size), bf16),
            shape((total, 2, size, size), f32),
        ],
        cost_estimate=small_cost,
        compiler_params=params(12),
        name="prepare",
    )(table, states, pieces)

    envs, mixeds, sums = [], [], []
    for c, (begin, width) in enumerate(zip(begins, CHUNKS)):
        if c > 0:
            got[c], _ = lax.optimization_barrier((got[c], sums[c - 1]))
        env, mixed, part = pl.pallas_call(
            functools.partial(first_kernel, own, begin),
            in_specs=[smem, smem] + [vmem] * 8,
            out_specs=[vmem] * 3,
            out_shape=[
                shape((width, rows(1), 2 * size), bf16),
                shape((width, rows(1), 2 * size), bf16),
                shape((width, size, size), f32),
            ],
            cost_estimate=small_cost,
        compiler_params=params(12),
            name=f"first_matvec{c}",
        )(table, bond, got[c][0], sent[c][1], got[c][1], sent[c][0], middle, vec, back, onsite)
        envs.append(env)
        mixeds.append(mixed)
        if c < len(CHUNKS) - 1:
            sums.append(total_of(part))

    image = jnp.concatenate(sums, 0)
    parts = [part] + [partner(part, mask) for mask in (1, 2, 3)]
    second, share = pl.pallas_call(
        functools.partial(second_kernel, own, early),
        in_specs=[smem] + [vmem] * (9 + 2 * len(CHUNKS)),
        out_specs=[vmem] * 2,
        out_shape=[shape((own, size, size), f32), shape((3, 8, 128), f32)],
        scratch_shapes=[
            pltpu.VMEM((total, size, size), f32),
            pltpu.VMEM((total, size, size), f32),
        ],
        cost_estimate=small_cost,
        compiler_params=params(20),
        name="second_matvec",
    )(table, image, *parts, vec, left, right, onsite, *envs, *mixeds)

    shares = [share] + [partner(share[:1], mask) for mask in (1, 2, 3)]
    new_state, energy = pl.pallas_call(
        functools.partial(final_kernel, own, total * size * size),
        in_specs=[smem] + [vmem] * 6,
        out_specs=[vmem, smem],
        out_shape=[shape((own, size, size), f32), shape((1,), f32)],
        cost_estimate=small_cost,
        compiler_params=params(4),
        name="ritz_update",
    )(table, *shares, vec, second)
    return (new_state, energy)


def solution(mesh):
    return jax.shard_map(
        on_device,
        mesh=mesh,
        in_specs=(
            P(("groups", "sites"), None, None),
            P(("groups", "sites"), None, None),
            P(("groups", "sites"), None, None),
            P(("groups", "sites"), None, None),
            P(("groups", "sites"), None, None, None),
            P(("groups", "sites"), None, None, None),
            P(("groups", "sites"), None),
            P("groups", None),
            P("groups", None),
        ),
        out_specs=(P(("groups", "sites"), None, None), P(("groups", "sites"))),
        check_vma=False,
    )
```

```python
import functools
import math

import jax
import jax.numpy as jnp
from jax import lax
from jax.experimental import pallas as pl
from jax.experimental.pallas import tpu as pltpu
from jax.sharding import PartitionSpec as P

GROUP = 4
CHUNKS = (3, 3, 1, 1)
MIB = 1024 * 1024


def hand_over(block, parity):
    count = lax.axis_size("sites")
    route = [(i, i + (GROUP if i % 2 == parity else -GROUP)) for i in range(count)]
    return lax.ppermute(block, "sites", [(i, j) for i, j in route if 0 <= j < count])


def partner(block, mask):
    route = [(i, i ^ mask) for i in range(lax.axis_size("sites"))]
    return lax.ppermute(block, "sites", route)


def gather(block):
    pieces = [block] + [partner(block, mask) for mask in (1, 2, 3)]
    return jnp.stack(pieces, 0)


def total_of(block):
    pair = block + partner(block, 1)
    return pair + partner(pair, 2)


def halves(value):
    high = value.astype(jnp.bfloat16)
    return high, (value - high.astype(jnp.float32)).astype(jnp.bfloat16)


def split_left(value):
    return jnp.concatenate(halves(value), axis=1)


def split_right(value):
    high, low = halves(value)
    return jnp.concatenate(
        [
            jnp.concatenate([high, low], axis=1),
            jnp.concatenate([high, jnp.zeros_like(low)], axis=1),
        ],
        axis=0,
    )


def fold(wide):
    half = wide.shape[1] // 2
    return wide[:, :half] + wide[:, half:]


def product(left, right):
    return fold(jnp.dot(split_left(left), split_right(right), preferred_element_type=jnp.float32))


def core_of(env_split, mixed_split, middle_split, terms):
    size = mixed_split.shape[0] // terms
    temp = fold(jnp.dot(env_split, middle_split, preferred_element_type=jnp.float32))
    high, low = halves(temp)
    wide = lambda part: jnp.concatenate(
        [part[m * size : (m + 1) * size] for m in range(terms)], axis=1
    )
    out = jnp.dot(
        jnp.concatenate([wide(high), wide(low)], axis=0),
        mixed_split,
        preferred_element_type=jnp.float32,
    )
    return fold(out[:size]) + out[size:, :size]


HEAD = 4


def sector_copy(env, index, out, row, sem):
    terms, _, size, _ = env.shape
    target = out.at[pl.ds(row, terms * size)].reshape(terms, size, size)
    return pltpu.make_async_copy(env.at[:, index], target, sem)


def pick(table, left_env, right_env, outs, sems, begin, chunks):
    terms, total, size = left_env.shape[:3]
    copies = []
    for c, width in enumerate(chunks):
        for side in range(2):
            base = HEAD + (3 + side) * total
            from_left = table[HEAD + 5 * total + side] == 0
            for s in range(width):
                place = (
                    table[base + begin + s], outs[2 * c + side], s * terms * size,
                    sems.at[side, begin + s],
                )
                left, right = sector_copy(left_env, *place), sector_copy(right_env, *place)
                pl.when(from_left)(left.start)
                pl.when(jnp.logical_not(from_left))(right.start)
                copies.append(left)
        begin += width
    return copies


def open_kernel(
    chunks, parts, place_hbm, sectors_hbm, flow_hbm, bond_hbm, left_tensor, right_tensor,
    left_env, right_env, table, *refs,
):
    outs, refs = refs[: 2 * len(chunks)], refs[2 * len(chunks) :]
    place, sectors, flow, order, bond, small, sems, more, some = refs
    own, size = left_tensor.shape[0], left_tensor.shape[1]
    terms, total = left_env.shape[0], left_env.shape[1]
    base = chunks[0] * terms * size
    inputs = ((place_hbm, place), (sectors_hbm, sectors), (flow_hbm, flow), (bond_hbm, bond))
    loads = [pltpu.make_async_copy(a, b, some.at[i]) for i, (a, b) in enumerate(inputs)]
    for copy in loads:
        copy.start()
    for copy in loads:
        copy.wait()
    partition = place[0] // GROUP
    before = jnp.maximum(partition - 1, 0)
    after = jnp.minimum(partition + 1, parts - 1)
    first, last = partition == 0, partition == parts - 1
    swap = place[0] % 2 == 1
    table[0] = first.astype(jnp.int32)
    table[1] = last.astype(jnp.int32)
    table[2] = place[0] % GROUP
    table[3] = swap.astype(jnp.int32)
    for j in range(total):
        order[flow[before, j]] = j
        order[total + flow[partition, j]] = j
        order[2 * total + flow[after, j]] = j
    for j in range(total):
        joined = sectors[partition, j]
        table[HEAD + j] = order[j]
        table[HEAD + total + j] = order[2 * total + joined]
        table[HEAD + 2 * total + j] = joined
        ahead = jnp.where(last, joined, order[total + j])
        behind = jnp.where(first, j, order[total + sectors[before, j]])
        table[HEAD + 3 * total + j] = jnp.where(swap, behind, ahead)
        table[HEAD + 4 * total + j] = jnp.where(swap, ahead, behind)
    ahead, behind = last.astype(jnp.int32), 1 - first.astype(jnp.int32)
    table[HEAD + 5 * total] = jnp.where(swap, behind, ahead)
    table[HEAD + 5 * total + 1] = jnp.where(swap, ahead, behind)
    copies = pick(table, left_env, right_env, outs, sems, 0, chunks)
    small[...] = jnp.zeros_like(small)
    small[:, : bond.shape[1]] = bond[...]
    for side in range(2):
        for i in range(own):
            target = outs[side].at[pl.ds(base + i * size, size)]
            straight = pltpu.make_async_copy(
                (left_tensor, right_tensor)[side].at[i], target, more.at[side, i]
            )
            crossed = pltpu.make_async_copy(
                (right_tensor, left_tensor)[side].at[i], target, more.at[side, i]
            )
            pl.when(jnp.logical_not(swap))(straight.start)
            pl.when(swap)(crossed.start)
            copies.append(straight)
        copy = pltpu.make_async_copy(
            small, outs[side].at[pl.ds(base + own * size, terms)], more.at[side, own]
        )
        copy.start()
        copies.append(copy)
    for copy in copies:
        copy.wait()


def prepare_kernel(
    own, table, states, pieces, vec_out, middle_out, plain_out, left_out, right_out, back_out,
):
    total, size = vec_out.shape[0], vec_out.shape[1]
    row = lax.broadcasted_iota(jnp.int32, (size, size), 0)
    col = lax.broadcasted_iota(jnp.int32, (size, size), 1)
    eye = (row == col).astype(jnp.float32)
    member = table[2]

    def block(sector, kind):
        return pieces[(sector // own) ^ member, sector % own, kind]

    def state_of(sector):
        return states[(sector // own) ^ member, sector % own]

    square = jnp.zeros((size, size), jnp.float32)
    for j in range(total):
        value = state_of(j)
        square = square + value * value
    norm = jnp.sqrt(jnp.sum(square))

    def body(j, carry):
        vec = state_of(j) / norm
        left = jnp.where(table[0] == 1, eye, block(table[HEAD + j], 0))
        right = jnp.where(table[1] == 1, eye, block(table[HEAD + total + j], 1))
        vec_out[j] = vec
        left_out[j] = split_left(left)
        right_out[j] = split_right(right)
        back_out[j, 0] = jnp.transpose(left)
        back_out[j, 1] = jnp.transpose(right)
        middle = product(product(left, vec), right)
        middle_out[j] = split_right(middle)
        plain_out[j] = middle
        return carry

    lax.fori_loop(0, total, body, 0)


def first_kernel(
    own, begin, table, bond, got0, got1, sent0, sent1, middle, vec, back, onsite,
    env_out, mixed_out, part_out,
):
    size = vec.shape[-1]
    terms = bond.shape[0]
    first, last, member, swap = table[0] == 1, table[1] == 1, table[2], table[3] == 1
    rows = lambda s, m: slice((s * terms + m) * size, (s * terms + m + 1) * size)

    def chosen(at, end, sent_a, sent_b, got_a, got_b):
        there = jnp.where(swap, got_b[at], got_a[at])
        return jnp.where(end, jnp.where(swap, sent_b[at], sent_a[at]), there)

    for s in range(part_out.shape[0]):
        for m in range(terms):
            block = chosen(rows(s, m), first, sent1, sent0, got0, got1)
            env_out[s, rows(0, m)] = split_left(block)
        blocks = [chosen(rows(s, m), last, sent0, sent1, got1, got0) for m in range(terms)]
        for m in range(terms):
            total = bond[m, 0] * blocks[0]
            for k in range(1, terms):
                total = total + bond[m, k] * blocks[k]
            mixed_out[s, rows(0, m)] = split_left(total)
        j = begin + s
        core = core_of(env_out[s], mixed_out[s], middle[j], terms)
        part = product(product(back[j, 0], core), back[j, 1])
        mine = (j // own == member).astype(jnp.float32)
        part_out[s] = part + (mine * onsite[j % own]) * vec[j]


def inward(block, left, right):
    temp = fold(jnp.dot(left, split_right(block), preferred_element_type=jnp.float32))
    return fold(jnp.dot(split_left(temp), right, preferred_element_type=jnp.float32))


def early_kernel(
    own, begin, table, image, part, vec, middle, left, right, onsite, env, mixed,
    resid_out, stat_out, moved, cores,
):
    width, size = image.shape[0], image.shape[1]
    terms = mixed.shape[1] // size
    member = table[2]
    zero = jnp.zeros((size, size), jnp.float32)
    tile = lambda value: jnp.full((8, 128), value, jnp.float32)

    along, norm = zero, zero
    for i in range(width):
        along = along + vec[begin + i] * image[i]
        norm = norm + vec[begin + i] * vec[begin + i]
    along, norm = jnp.sum(along), jnp.sum(norm)
    guess = jnp.where(norm > 0, along / jnp.where(norm > 0, norm, 1.0), 0.0)
    left_over, square = zero, zero
    for i in range(width):
        resid = image[i] - guess * vec[begin + i]
        resid_out[i] = resid
        left_over = left_over + resid * vec[begin + i]
        square = square + resid * resid
    square = tile(jnp.sum(square))
    length = jnp.sqrt(square + 1e-06)
    scale = (1.0 / length)[0:1]
    stat_out[0] = tile(guess)
    stat_out[1] = tile(norm)
    stat_out[2] = tile(jnp.sum(left_over))
    stat_out[3] = square
    stat_out[4] = length

    for i in range(width):
        resid = resid_out[i] * scale
        resid_out[i] = resid
        moved[i] = inward(resid, left[begin + i], right[begin + i])
    for i in range(width):
        cores[i] = core_of(env[i], mixed[i], split_right(moved[i]), terms)
    shares = lambda i: jnp.where((begin + i) // own == member, 1.0, 0.0) * onsite[(begin + i) % own]
    both = zero
    for i in range(width):
        resid = resid_out[i]
        both = both + moved[i] * cores[i] + (shares(i) * resid) * resid
    stat_out[5] = tile(jnp.sum(both))
    cross = zero
    for i in range(width):
        resid = resid_out[i]
        cross = cross + middle[begin + i] * cores[i]
        cross = cross + resid * (part[i] + shares(i) * vec[begin + i])
    stat_out[6] = tile(jnp.sum(cross))
    plain = zero
    for i in range(width):
        plain = plain + vec[begin + i] * part[i]
    stat_out[7] = tile(jnp.sum(plain))


def second_kernel(
    own, widths, table, part0, part1, part2, part3, vec, left, right, onsite, env, mixed, *refs
):
    count = len(widths)
    resids, stats = refs[:count], refs[count : 2 * count]
    second_out, share_out, work = refs[2 * count :]
    total, size, late = vec.shape[0], vec.shape[1], part0.shape[0]
    early = total - late
    terms = mixed.shape[1] // size
    member = table[2]
    zero = jnp.zeros((size, size), jnp.float32)
    tile = lambda value: jnp.full((8, 128), value, jnp.float32)

    images = [(part0[i] + part1[i]) + (part2[i] + part3[i]) for i in range(late)]
    along = zero
    for i in range(late):
        along = along + vec[early + i] * images[i]
    alpha1 = tile(jnp.sum(along))
    for stat in stats:
        alpha1 = alpha1 + (stat[0] * stat[1] + stat[2])
    rest = zero
    for i in range(late):
        images[i] = images[i] - alpha1[0:1] * vec[early + i]
        rest = rest + images[i] * images[i]
    square = tile(jnp.sum(rest)) + 1e-06
    for stat in stats:
        away = alpha1 - stat[0]
        square = square + jnp.maximum(
            stat[3] - 2.0 * away * stat[2] + away * (away * stat[1]), 0.0
        )
    beta = jnp.sqrt(square)
    scale = (1.0 / beta)[0:1]
    share = zero
    for i in range(late):
        j = early + i
        value = images[i] * scale
        work[j] = value
        moved = inward(value, left[j], right[j])
        core = core_of(env[i], mixed[i], split_right(moved), terms)
        mine = jnp.where(j // own == member, 1.0, 0.0) * onsite[j % own]
        share = share + moved * core + (mine * value) * value
    begin = 0
    sums = zero[:8]
    for resid, stat, width in zip(resids, stats, widths):
        long, off = stat[4] / beta, (alpha1 - stat[0]) / beta
        sums = sums + long * (long * stat[5]) - off * (long * stat[6]) + off * (off * stat[7])
        for i in range(width):
            work[begin + i] = long[0:1] * resid[i] - off[0:1] * vec[begin + i]
        begin += width
    share_out[0] = tile(jnp.sum(share)) + sums
    share_out[1] = alpha1
    share_out[2] = beta
    for i in range(own):
        second_out[i] = work[member * own + i]


def final_kernel(own, count, table, share0, share1, share2, share3, vec, second, out, energy_out):
    member = table[2]
    alpha2 = (share0[0] + share1[0]) + (share2[0] + share3[0])
    alpha1, beta = share0[1], share0[2]
    energy = (alpha1 + alpha2) / 2.0 - jnp.sqrt(((alpha1 - alpha2) / 2.0) ** 2 + beta * beta)
    height = jnp.sqrt(beta * beta + (energy - alpha1) ** 2)
    scale = math.sqrt(count)
    weight1 = (scale * (beta / height))[0:1]
    weight2 = (scale * ((energy - alpha1) / height))[0:1]
    for i in range(own):
        out[i] = weight1 * vec[member * own + i] + weight2 * second[i]
    energy_out[0] = energy[0, 0]


def on_device(
    state, left_tensor, right_tensor, onsite, left_env, right_env, mpo_bond, sectors, flow
):
    position = lax.axis_index("sites")
    parts = lax.axis_size("sites") // GROUP
    own, size = state.shape[0], state.shape[1]
    terms, total = left_env.shape[0], left_env.shape[1]
    f32, bf16 = jnp.float32, jnp.bfloat16
    begins = [sum(CHUNKS[:c]) for c in range(len(CHUNKS))]

    smem = pl.BlockSpec(memory_space=pltpu.SMEM)
    vmem = pl.BlockSpec(memory_space=pltpu.VMEM)
    hbm = pl.BlockSpec(memory_space=pltpu.HBM)
    shape = jax.ShapeDtypeStruct
    dma = pltpu.SemaphoreType.DMA
    params = lambda mib: pltpu.CompilerParams(vmem_limit_bytes=mib * MIB)

    small_cost = pl.CostEstimate(flops=1, bytes_accessed=1, transcendentals=0)

    rows = lambda width: width * terms * size
    chunk = lambda c: (rows(CHUNKS[c]) + (own * size + terms if c == 0 else 0), size)
    chunks = lambda some: [pltpu.VMEM(chunk(c), f32) for c in some for _ in range(2)]
    in_hbm = lambda *values: [
        pltpu.with_memory_space_constraint(value, pltpu.HBM) for value in values
    ]
    table, *opened = pl.pallas_call(
        functools.partial(open_kernel, CHUNKS, parts),
        in_specs=[hbm] * 8,
        out_specs=[smem] + [vmem] * (2 * len(CHUNKS)),
        out_shape=[shape((HEAD + 5 * total + 2,), jnp.int32)] + chunks(range(len(CHUNKS))),
        scratch_shapes=[
            pltpu.SMEM((1,), jnp.int32),
            pltpu.SMEM(sectors.shape, jnp.int32),
            pltpu.SMEM(flow.shape, jnp.int32),
            pltpu.SMEM((3 * total,), jnp.int32),
            pltpu.VMEM(mpo_bond.shape, f32),
            pltpu.VMEM((terms, size), f32),
            dma((2, total)),
            dma((2, own + 1)),
            dma((4,)),
        ],
        cost_estimate=small_cost,
        compiler_params=params(16),
        name="open",
    )(
        *in_hbm(
            jnp.reshape(position, (1,)).astype(jnp.int32), sectors, flow, mpo_bond,
            left_tensor, right_tensor, left_env, right_env,
        )
    )
    sent = [tuple(opened[2 * c : 2 * c + 2]) for c in range(len(CHUNKS))]
    states = gather(state)
    sent[1], _ = lax.optimization_barrier((sent[1], states))
    got = [tuple(hand_over(block, side) for side, block in enumerate(pair)) for pair in sent]

    tail = [block[rows(CHUNKS[0]) :] for block in got[0]]
    swap = table[3] == 1
    from_left, from_right = jnp.where(swap, tail[1], tail[0]), jnp.where(swap, tail[0], tail[1])
    small = jnp.eye(terms, dtype=f32)
    bond_left = jnp.where(table[0] == 1, small, from_left[own * size :, : mpo_bond.shape[1]])
    bond_right = jnp.where(table[1] == 1, small, from_right[own * size :, : mpo_bond.shape[1]])
    bond = jnp.sum(bond_left[:, None, :] * bond_right[None, :, :], axis=2)
    tensors = lambda block: block[: own * size].reshape(own, size, size)
    pieces = gather(jnp.stack([tensors(from_left), tensors(from_right)], 1))

    vec, middle, plain, left, right, back = pl.pallas_call(
        functools.partial(prepare_kernel, own),
        in_specs=[smem, vmem, vmem],
        out_specs=[vmem] * 6,
        out_shape=[
            shape((total, size, size), f32),
            shape((total, 2 * size, 2 * size), bf16),
            shape((total, size, size), f32),
            shape((total, size, 2 * size), bf16),
            shape((total, 2 * size, 2 * size), bf16),
            shape((total, 2, size, size), f32),
        ],
        cost_estimate=small_cost,
        compiler_params=params(12),
        name="prepare",
    )(table, states, pieces)

    def early(begin, width, image, part, env, mixed, after):
        image, _ = lax.optimization_barrier((image, after))
        return pl.pallas_call(
            functools.partial(early_kernel, own, begin),
            in_specs=[smem] + [vmem] * 9,
            out_specs=[vmem] * 2,
            out_shape=[shape((width, size, size), f32), shape((8, 8, 128), f32)],
            scratch_shapes=[pltpu.VMEM((width, size, size), f32)] * 2,
            cost_estimate=small_cost,
            compiler_params=params(12),
            name="early_second_matvec",
        )(table, image, part, vec, plain, left, right, onsite, env, mixed)

    resids, stats, waits, held = [], [], [], None
    for c, (begin, width) in enumerate(zip(begins, CHUNKS)):
        if c > 0:
            got[c], _ = lax.optimization_barrier((got[c], waits[c - 1]))
        env, mixed, part = pl.pallas_call(
            functools.partial(first_kernel, own, begin),
            in_specs=[smem, smem] + [vmem] * 8,
            out_specs=[vmem] * 3,
            out_shape=[
                shape((width, rows(1), 2 * size), bf16),
                shape((width, rows(1), 2 * size), bf16),
                shape((width, size, size), f32),
            ],
            cost_estimate=small_cost,
        compiler_params=params(12),
            name=f"first_matvec{c}",
        )(table, bond, *got[c], *sent[c], middle, vec, back, onsite)
        if held is not None:
            resid, stat = early(*held, after=part)
            resids.append(resid)
            stats.append(stat)
        if c < len(CHUNKS) - 1:
            image = total_of(part)
            held = (begin, width, image, part, env, mixed)
            waits.append([image] + stats[-1:])

    parts = [part] + [partner(part, mask) for mask in (1, 2, 3)]
    second, share = pl.pallas_call(
        functools.partial(second_kernel, own, CHUNKS[:-1]),
        in_specs=[smem] + [vmem] * (10 + 2 * (len(CHUNKS) - 1)),
        out_specs=[vmem] * 2,
        out_shape=[shape((own, size, size), f32), shape((3, 8, 128), f32)],
        scratch_shapes=[pltpu.VMEM((total, size, size), f32)],
        cost_estimate=small_cost,
        compiler_params=params(12),
        name="second_matvec",
    )(table, *parts, vec, left, right, onsite, env, mixed, *resids, *stats)

    shares = [share] + [partner(share[:1], mask) for mask in (1, 2, 3)]
    new_state, energy = pl.pallas_call(
        functools.partial(final_kernel, own, total * size * size),
        in_specs=[smem] + [vmem] * 6,
        out_specs=[vmem, smem],
        out_shape=[shape((own, size, size), f32), shape((1,), f32)],
        cost_estimate=small_cost,
        compiler_params=params(4),
        name="ritz_update",
    )(table, *shares, vec, second)
    return (new_state, energy)


def solution(mesh):
    return jax.shard_map(
        on_device,
        mesh=mesh,
        in_specs=(
            P(("groups", "sites"), None, None),
            P(("groups", "sites"), None, None),
            P(("groups", "sites"), None, None),
            P(("groups", "sites"), None, None),
            P(("groups", "sites"), None, None, None),
            P(("groups", "sites"), None, None, None),
            P(("groups", "sites"), None),
            P("groups", None),
            P("groups", None),
        ),
        out_specs=(P(("groups", "sites"), None, None), P(("groups", "sites"))),
        check_vma=False,
    )
```

```python
import functools
import math

import jax
import jax.numpy as jnp
from jax import lax
from jax.experimental import pallas as pl
from jax.experimental.pallas import tpu as pltpu
from jax.sharding import PartitionSpec as P

GROUP = 4
CHUNKS = (3, 3, 1, 1)
MIB = 1024 * 1024


def hand_over(block, parity):
    count = lax.axis_size("sites")
    route = [(i, i + (GROUP if i % 2 == parity else -GROUP)) for i in range(count)]
    return lax.ppermute(block, "sites", [(i, j) for i, j in route if 0 <= j < count])


def partner(block, mask):
    route = [(i, i ^ mask) for i in range(lax.axis_size("sites"))]
    return lax.ppermute(block, "sites", route)


def gather(block):
    pieces = [block] + [partner(block, mask) for mask in (1, 2, 3)]
    return jnp.stack(pieces, 0)


def total_of(block):
    pair = block + partner(block, 1)
    return pair + partner(pair, 2)


def halves(value):
    high = value.astype(jnp.bfloat16)
    return high, (value - high.astype(jnp.float32)).astype(jnp.bfloat16)


def split_left(value):
    return jnp.concatenate(halves(value), axis=1)


def split_right(value):
    high, low = halves(value)
    return jnp.concatenate(
        [
            jnp.concatenate([high, low], axis=1),
            jnp.concatenate([high, jnp.zeros_like(low)], axis=1),
        ],
        axis=0,
    )


def fold(wide):
    half = wide.shape[1] // 2
    return wide[:, :half] + wide[:, half:]


def product(left, right):
    return fold(jnp.dot(split_left(left), split_right(right), preferred_element_type=jnp.float32))


def core_of(env_split, mixed_split, middle_split, terms):
    size = mixed_split.shape[0] // terms
    temp = fold(jnp.dot(env_split, middle_split, preferred_element_type=jnp.float32))
    high, low = halves(temp)
    wide = lambda part: jnp.concatenate(
        [part[m * size : (m + 1) * size] for m in range(terms)], axis=1
    )
    out = jnp.dot(
        jnp.concatenate([wide(high), wide(low)], axis=0),
        mixed_split,
        preferred_element_type=jnp.float32,
    )
    return fold(out[:size]) + out[size:, :size]


HEAD = 4


def sector_copy(env, index, out, row, sem):
    terms, _, size, _ = env.shape
    target = out.at[pl.ds(row, terms * size)].reshape(terms, size, size)
    return pltpu.make_async_copy(env.at[:, index], target, sem)


def pick(table, left_env, right_env, outs, sems, begin, chunks):
    terms, total, size = left_env.shape[:3]
    copies = []
    for c, width in enumerate(chunks):
        for side in range(2):
            base = HEAD + (3 + side) * total
            from_left = table[HEAD + 5 * total + side] == 0
            for s in range(width):
                place = (
                    table[base + begin + s], outs[2 * c + side], s * terms * size,
                    sems.at[side, begin + s],
                )
                left, right = sector_copy(left_env, *place), sector_copy(right_env, *place)
                pl.when(from_left)(left.start)
                pl.when(jnp.logical_not(from_left))(right.start)
                copies.append(left)
        begin += width
    return copies


def open_kernel(
    chunks, parts, place_hbm, sectors_hbm, flow_hbm, bond_hbm, left_tensor, right_tensor,
    left_env, right_env, table, *refs,
):
    outs, refs = refs[: 2 * len(chunks)], refs[2 * len(chunks) :]
    place, sectors, flow, order, bond, small, sems, more, some = refs
    own, size = left_tensor.shape[0], left_tensor.shape[1]
    terms, total = left_env.shape[0], left_env.shape[1]
    base = chunks[0] * terms * size
    inputs = ((place_hbm, place), (sectors_hbm, sectors), (flow_hbm, flow), (bond_hbm, bond))
    loads = [pltpu.make_async_copy(a, b, some.at[i]) for i, (a, b) in enumerate(inputs)]
    for copy in loads:
        copy.start()
    for copy in loads:
        copy.wait()
    partition = place[0] // GROUP
    before = jnp.maximum(partition - 1, 0)
    after = jnp.minimum(partition + 1, parts - 1)
    first, last = partition == 0, partition == parts - 1
    swap = place[0] % 2 == 1
    table[0] = first.astype(jnp.int32)
    table[1] = last.astype(jnp.int32)
    table[2] = place[0] % GROUP
    table[3] = swap.astype(jnp.int32)
    for j in range(total):
        order[flow[before, j]] = j
        order[total + flow[partition, j]] = j
        order[2 * total + flow[after, j]] = j
    for j in range(total):
        joined = sectors[partition, j]
        table[HEAD + j] = order[j]
        table[HEAD + total + j] = order[2 * total + joined]
        table[HEAD + 2 * total + j] = joined
        ahead = jnp.where(last, joined, order[total + j])
        behind = jnp.where(first, j, order[total + sectors[before, j]])
        table[HEAD + 3 * total + j] = jnp.where(swap, behind, ahead)
        table[HEAD + 4 * total + j] = jnp.where(swap, ahead, behind)
    ahead, behind = last.astype(jnp.int32), 1 - first.astype(jnp.int32)
    table[HEAD + 5 * total] = jnp.where(swap, behind, ahead)
    table[HEAD + 5 * total + 1] = jnp.where(swap, ahead, behind)
    copies = pick(table, left_env, right_env, outs, sems, 0, chunks)
    small[...] = jnp.zeros_like(small)
    small[:, : bond.shape[1]] = bond[...]
    for side in range(2):
        for i in range(own):
            target = outs[side].at[pl.ds(base + i * size, size)]
            straight = pltpu.make_async_copy(
                (left_tensor, right_tensor)[side].at[i], target, more.at[side, i]
            )
            crossed = pltpu.make_async_copy(
                (right_tensor, left_tensor)[side].at[i], target, more.at[side, i]
            )
            pl.when(jnp.logical_not(swap))(straight.start)
            pl.when(swap)(crossed.start)
            copies.append(straight)
        copy = pltpu.make_async_copy(
            small, outs[side].at[pl.ds(base + own * size, terms)], more.at[side, own]
        )
        copy.start()
        copies.append(copy)
    for copy in copies:
        copy.wait()


def pick_kernel(begin, chunks, table, left_env, right_env, *refs):
    for copy in pick(table, left_env, right_env, refs[:-1], refs[-1], begin, chunks):
        copy.wait()


def prepare_kernel(
    own, table, states, pieces, vec_out, middle_out, plain_out, left_out, right_out, back_out,
):
    total, size = vec_out.shape[0], vec_out.shape[1]
    row = lax.broadcasted_iota(jnp.int32, (size, size), 0)
    col = lax.broadcasted_iota(jnp.int32, (size, size), 1)
    eye = (row == col).astype(jnp.float32)
    member = table[2]

    def block(sector, kind):
        return pieces[(sector // own) ^ member, sector % own, kind]

    def state_of(sector):
        return states[(sector // own) ^ member, sector % own]

    square = jnp.zeros((size, size), jnp.float32)
    for j in range(total):
        value = state_of(j)
        square = square + value * value
    norm = jnp.sqrt(jnp.sum(square))

    def body(j, carry):
        vec = state_of(j) / norm
        left = jnp.where(table[0] == 1, eye, block(table[HEAD + j], 0))
        right = jnp.where(table[1] == 1, eye, block(table[HEAD + total + j], 1))
        vec_out[j] = vec
        left_out[j] = split_left(left)
        right_out[j] = split_right(right)
        back_out[j, 0] = jnp.transpose(left)
        back_out[j, 1] = jnp.transpose(right)
        middle = product(product(left, vec), right)
        middle_out[j] = split_right(middle)
        plain_out[j] = middle
        return carry

    lax.fori_loop(0, total, body, 0)


def first_kernel(
    own, begin, table, bond, got0, got1, sent0, sent1, middle, vec, back, onsite,
    env_out, mixed_out, part_out,
):
    size = vec.shape[-1]
    terms = bond.shape[0]
    first, last, member, swap = table[0] == 1, table[1] == 1, table[2], table[3] == 1
    rows = lambda s, m: slice((s * terms + m) * size, (s * terms + m + 1) * size)

    def chosen(at, end, sent_a, sent_b, got_a, got_b):
        there = jnp.where(swap, got_b[at], got_a[at])
        return jnp.where(end, jnp.where(swap, sent_b[at], sent_a[at]), there)

    for s in range(part_out.shape[0]):
        for m in range(terms):
            block = chosen(rows(s, m), first, sent1, sent0, got0, got1)
            env_out[s, rows(0, m)] = split_left(block)
        blocks = [chosen(rows(s, m), last, sent0, sent1, got1, got0) for m in range(terms)]
        for m in range(terms):
            total = bond[m, 0] * blocks[0]
            for k in range(1, terms):
                total = total + bond[m, k] * blocks[k]
            mixed_out[s, rows(0, m)] = split_left(total)
        j = begin + s
        core = core_of(env_out[s], mixed_out[s], middle[j], terms)
        part = product(product(back[j, 0], core), back[j, 1])
        mine = (j // own == member).astype(jnp.float32)
        part_out[s] = part + (mine * onsite[j % own]) * vec[j]


def inward(block, left, right):
    temp = fold(jnp.dot(left, split_right(block), preferred_element_type=jnp.float32))
    return fold(jnp.dot(split_left(temp), right, preferred_element_type=jnp.float32))


def early_kernel(
    own, begin, table, image, part, vec, middle, left, right, onsite, env, mixed,
    resid_out, stat_out, moved, cores,
):
    width, size = image.shape[0], image.shape[1]
    terms = mixed.shape[1] // size
    member = table[2]
    zero = jnp.zeros((size, size), jnp.float32)
    tile = lambda value: jnp.full((8, 128), value, jnp.float32)

    along, norm = zero, zero
    for i in range(width):
        along = along + vec[begin + i] * image[i]
        norm = norm + vec[begin + i] * vec[begin + i]
    along, norm = jnp.sum(along), jnp.sum(norm)
    guess = jnp.where(norm > 0, along / jnp.where(norm > 0, norm, 1.0), 0.0)
    left_over, square = zero, zero
    for i in range(width):
        resid = image[i] - guess * vec[begin + i]
        resid_out[i] = resid
        left_over = left_over + resid * vec[begin + i]
        square = square + resid * resid
    square = tile(jnp.sum(square))
    length = jnp.sqrt(square + 1e-06)
    scale = (1.0 / length)[0:1]
    stat_out[0] = tile(guess)
    stat_out[1] = tile(norm)
    stat_out[2] = tile(jnp.sum(left_over))
    stat_out[3] = square
    stat_out[4] = length

    for i in range(width):
        resid = resid_out[i] * scale
        resid_out[i] = resid
        moved[i] = inward(resid, left[begin + i], right[begin + i])
    for i in range(width):
        cores[i] = core_of(env[i], mixed[i], split_right(moved[i]), terms)
    shares = lambda i: jnp.where((begin + i) // own == member, 1.0, 0.0) * onsite[(begin + i) % own]
    both = zero
    for i in range(width):
        resid = resid_out[i]
        both = both + moved[i] * cores[i] + (shares(i) * resid) * resid
    stat_out[5] = tile(jnp.sum(both))
    cross = zero
    for i in range(width):
        resid = resid_out[i]
        cross = cross + middle[begin + i] * cores[i]
        cross = cross + resid * (part[i] + shares(i) * vec[begin + i])
    stat_out[6] = tile(jnp.sum(cross))
    plain = zero
    for i in range(width):
        plain = plain + vec[begin + i] * part[i]
    stat_out[7] = tile(jnp.sum(plain))


def second_kernel(
    own, widths, table, part0, part1, part2, part3, vec, left, right, onsite, env, mixed, *refs
):
    count = len(widths)
    resids, stats = refs[:count], refs[count : 2 * count]
    second_out, share_out, work = refs[2 * count :]
    total, size, late = vec.shape[0], vec.shape[1], part0.shape[0]
    early = total - late
    terms = mixed.shape[1] // size
    member = table[2]
    zero = jnp.zeros((size, size), jnp.float32)
    tile = lambda value: jnp.full((8, 128), value, jnp.float32)

    images = [(part0[i] + part1[i]) + (part2[i] + part3[i]) for i in range(late)]
    along = zero
    for i in range(late):
        along = along + vec[early + i] * images[i]
    alpha1 = tile(jnp.sum(along))
    for stat in stats:
        alpha1 = alpha1 + (stat[0] * stat[1] + stat[2])
    rest = zero
    for i in range(late):
        images[i] = images[i] - alpha1[0:1] * vec[early + i]
        rest = rest + images[i] * images[i]
    square = tile(jnp.sum(rest)) + 1e-06
    for stat in stats:
        away = alpha1 - stat[0]
        square = square + jnp.maximum(
            stat[3] - 2.0 * away * stat[2] + away * (away * stat[1]), 0.0
        )
    beta = jnp.sqrt(square)
    scale = (1.0 / beta)[0:1]
    share = zero
    for i in range(late):
        j = early + i
        value = images[i] * scale
        work[j] = value
        moved = inward(value, left[j], right[j])
        core = core_of(env[i], mixed[i], split_right(moved), terms)
        mine = jnp.where(j // own == member, 1.0, 0.0) * onsite[j % own]
        share = share + moved * core + (mine * value) * value
    begin = 0
    sums = zero[:8]
    for resid, stat, width in zip(resids, stats, widths):
        long, off = stat[4] / beta, (alpha1 - stat[0]) / beta
        sums = sums + long * (long * stat[5]) - off * (long * stat[6]) + off * (off * stat[7])
        for i in range(width):
            work[begin + i] = long[0:1] * resid[i] - off[0:1] * vec[begin + i]
        begin += width
    share_out[0] = tile(jnp.sum(share)) + sums
    share_out[1] = alpha1
    share_out[2] = beta
    for i in range(own):
        second_out[i] = work[member * own + i]


def final_kernel(own, count, table, share0, share1, share2, share3, vec, second, out, energy_out):
    member = table[2]
    alpha2 = (share0[0] + share1[0]) + (share2[0] + share3[0])
    alpha1, beta = share0[1], share0[2]
    energy = (alpha1 + alpha2) / 2.0 - jnp.sqrt(((alpha1 - alpha2) / 2.0) ** 2 + beta * beta)
    height = jnp.sqrt(beta * beta + (energy - alpha1) ** 2)
    scale = math.sqrt(count)
    weight1 = (scale * (beta / height))[0:1]
    weight2 = (scale * ((energy - alpha1) / height))[0:1]
    for i in range(own):
        out[i] = weight1 * vec[member * own + i] + weight2 * second[i]
    energy_out[0] = energy[0, 0]


def on_device(
    state, left_tensor, right_tensor, onsite, left_env, right_env, mpo_bond, sectors, flow
):
    position = lax.axis_index("sites")
    parts = lax.axis_size("sites") // GROUP
    own, size = state.shape[0], state.shape[1]
    terms, total = left_env.shape[0], left_env.shape[1]
    f32, bf16 = jnp.float32, jnp.bfloat16
    begins = [sum(CHUNKS[:c]) for c in range(len(CHUNKS))]

    smem = pl.BlockSpec(memory_space=pltpu.SMEM)
    vmem = pl.BlockSpec(memory_space=pltpu.VMEM)
    hbm = pl.BlockSpec(memory_space=pltpu.HBM)
    shape = jax.ShapeDtypeStruct
    dma = pltpu.SemaphoreType.DMA
    params = lambda mib: pltpu.CompilerParams(vmem_limit_bytes=mib * MIB)

    small_cost = pl.CostEstimate(flops=1, bytes_accessed=1, transcendentals=0)

    rows = lambda width: width * terms * size
    chunk = lambda c: (rows(CHUNKS[c]) + (own * size + terms if c == 0 else 0), size)
    chunks = lambda some: [pltpu.VMEM(chunk(c), f32) for c in some for _ in range(2)]
    in_hbm = lambda *values: [
        pltpu.with_memory_space_constraint(value, pltpu.HBM) for value in values
    ]
    table, *opened = pl.pallas_call(
        functools.partial(open_kernel, CHUNKS[:1], parts),
        in_specs=[hbm] * 8,
        out_specs=[smem] + [vmem] * 2,
        out_shape=[shape((HEAD + 5 * total + 2,), jnp.int32)] + chunks([0]),
        scratch_shapes=[
            pltpu.SMEM((1,), jnp.int32),
            pltpu.SMEM(sectors.shape, jnp.int32),
            pltpu.SMEM(flow.shape, jnp.int32),
            pltpu.SMEM((3 * total,), jnp.int32),
            pltpu.VMEM(mpo_bond.shape, f32),
            pltpu.VMEM((terms, size), f32),
            dma((2, total)),
            dma((2, own + 1)),
            dma((4,)),
        ],
        cost_estimate=small_cost,
        compiler_params=params(16),
        name="open",
    )(
        *in_hbm(
            jnp.reshape(position, (1,)).astype(jnp.int32), sectors, flow, mpo_bond,
            left_tensor, right_tensor, left_env, right_env,
        )
    )
    later = range(1, len(CHUNKS))
    opened += pl.pallas_call(
        functools.partial(pick_kernel, CHUNKS[0], CHUNKS[1:]),
        in_specs=[smem] + [hbm] * 2,
        out_specs=[vmem] * (2 * len(later)),
        out_shape=chunks(later),
        scratch_shapes=[dma((2, total))],
        cost_estimate=small_cost,
        compiler_params=params(16),
        name="pick",
    )(table, *in_hbm(left_env, right_env))
    sent = [tuple(opened[2 * c : 2 * c + 2]) for c in range(len(CHUNKS))]
    states = gather(state)
    sent[1], _ = lax.optimization_barrier((sent[1], states))
    got = [tuple(hand_over(block, side) for side, block in enumerate(pair)) for pair in sent]

    tail = [block[rows(CHUNKS[0]) :] for block in got[0]]
    swap = table[3] == 1
    from_left, from_right = jnp.where(swap, tail[1], tail[0]), jnp.where(swap, tail[0], tail[1])
    small = jnp.eye(terms, dtype=f32)
    bond_left = jnp.where(table[0] == 1, small, from_left[own * size :, : mpo_bond.shape[1]])
    bond_right = jnp.where(table[1] == 1, small, from_right[own * size :, : mpo_bond.shape[1]])
    bond = jnp.sum(bond_left[:, None, :] * bond_right[None, :, :], axis=2)
    tensors = lambda block: block[: own * size].reshape(own, size, size)
    pieces = gather(jnp.stack([tensors(from_left), tensors(from_right)], 1))

    vec, middle, plain, left, right, back = pl.pallas_call(
        functools.partial(prepare_kernel, own),
        in_specs=[smem, vmem, vmem],
        out_specs=[vmem] * 6,
        out_shape=[
            shape((total, size, size), f32),
            shape((total, 2 * size, 2 * size), bf16),
            shape((total, size, size), f32),
            shape((total, size, 2 * size), bf16),
            shape((total, 2 * size, 2 * size), bf16),
            shape((total, 2, size, size), f32),
        ],
        cost_estimate=small_cost,
        compiler_params=params(12),
        name="prepare",
    )(table, states, pieces)

    def early(begin, width, image, part, env, mixed, after):
        image, _ = lax.optimization_barrier((image, after))
        return pl.pallas_call(
            functools.partial(early_kernel, own, begin),
            in_specs=[smem] + [vmem] * 9,
            out_specs=[vmem] * 2,
            out_shape=[shape((width, size, size), f32), shape((8, 8, 128), f32)],
            scratch_shapes=[pltpu.VMEM((width, size, size), f32)] * 2,
            cost_estimate=small_cost,
            compiler_params=params(12),
            name="early_second_matvec",
        )(table, image, part, vec, plain, left, right, onsite, env, mixed)

    resids, stats, waits, held = [], [], [], None
    for c, (begin, width) in enumerate(zip(begins, CHUNKS)):
        if c > 0:
            got[c], _ = lax.optimization_barrier((got[c], waits[c - 1]))
        env, mixed, part = pl.pallas_call(
            functools.partial(first_kernel, own, begin),
            in_specs=[smem, smem] + [vmem] * 8,
            out_specs=[vmem] * 3,
            out_shape=[
                shape((width, rows(1), 2 * size), bf16),
                shape((width, rows(1), 2 * size), bf16),
                shape((width, size, size), f32),
            ],
            cost_estimate=small_cost,
        compiler_params=params(12),
            name=f"first_matvec{c}",
        )(table, bond, *got[c], *sent[c], middle, vec, back, onsite)
        if held is not None:
            resid, stat = early(*held, after=part)
            resids.append(resid)
            stats.append(stat)
        if c < len(CHUNKS) - 1:
            image = total_of(part)
            held = (begin, width, image, part, env, mixed)
            waits.append([image] + stats[-1:])

    parts = [part] + [partner(part, mask) for mask in (1, 2, 3)]
    second, share = pl.pallas_call(
        functools.partial(second_kernel, own, CHUNKS[:-1]),
        in_specs=[smem] + [vmem] * (10 + 2 * (len(CHUNKS) - 1)),
        out_specs=[vmem] * 2,
        out_shape=[shape((own, size, size), f32), shape((3, 8, 128), f32)],
        scratch_shapes=[pltpu.VMEM((total, size, size), f32)],
        cost_estimate=small_cost,
        compiler_params=params(12),
        name="second_matvec",
    )(table, *parts, vec, left, right, onsite, env, mixed, *resids, *stats)

    shares = [share] + [partner(share[:1], mask) for mask in (1, 2, 3)]
    new_state, energy = pl.pallas_call(
        functools.partial(final_kernel, own, total * size * size),
        in_specs=[smem] + [vmem] * 6,
        out_specs=[vmem, smem],
        out_shape=[shape((own, size, size), f32), shape((1,), f32)],
        cost_estimate=small_cost,
        compiler_params=params(4),
        name="ritz_update",
    )(table, *shares, vec, second)
    return (new_state, energy)


def solution(mesh):
    return jax.shard_map(
        on_device,
        mesh=mesh,
        in_specs=(
            P(("groups", "sites"), None, None),
            P(("groups", "sites"), None, None),
            P(("groups", "sites"), None, None),
            P(("groups", "sites"), None, None),
            P(("groups", "sites"), None, None, None),
            P(("groups", "sites"), None, None, None),
            P(("groups", "sites"), None),
            P("groups", None),
            P("groups", None),
        ),
        out_specs=(P(("groups", "sites"), None, None), P(("groups", "sites"))),
        check_vma=False,
    )
```

```python
import functools
import math

import jax
import jax.numpy as jnp
from jax import lax
from jax.experimental import pallas as pl
from jax.experimental.pallas import tpu as pltpu
from jax.sharding import PartitionSpec as P

GROUP = 4
CHUNKS = (3, 3, 1, 1)
MIB = 1024 * 1024


def hand_over(block, parity):
    count = lax.axis_size("sites")
    route = [(i, i + (GROUP if i % 2 == parity else -GROUP)) for i in range(count)]
    return lax.ppermute(block, "sites", [(i, j) for i, j in route if 0 <= j < count])


def partner(block, mask):
    route = [(i, i ^ mask) for i in range(lax.axis_size("sites"))]
    return lax.ppermute(block, "sites", route)


def gather(block):
    pieces = [block] + [partner(block, mask) for mask in (1, 2, 3)]
    return jnp.stack(pieces, 0)


def total_of(block):
    pair = block + partner(block, 1)
    return pair + partner(pair, 2)


def halves(value):
    high = value.astype(jnp.bfloat16)
    return high, (value - high.astype(jnp.float32)).astype(jnp.bfloat16)


def split_left(value):
    return jnp.concatenate(halves(value), axis=1)


def split_right(value):
    high, low = halves(value)
    return jnp.concatenate(
        [
            jnp.concatenate([high, low], axis=1),
            jnp.concatenate([high, jnp.zeros_like(low)], axis=1),
        ],
        axis=0,
    )


def fold(wide):
    half = wide.shape[1] // 2
    return wide[:, :half] + wide[:, half:]


def product(left, right):
    return fold(jnp.dot(split_left(left), split_right(right), preferred_element_type=jnp.float32))


def inward(block, left, right):
    temp = fold(jnp.dot(left, split_right(block), preferred_element_type=jnp.float32))
    return fold(jnp.dot(split_left(temp), right, preferred_element_type=jnp.float32))


def core_of(env_split, mixed_split, middle_split, terms):
    size = mixed_split.shape[0] // terms
    temp = fold(jnp.dot(env_split, middle_split, preferred_element_type=jnp.float32))
    high, low = halves(temp)
    wide = lambda part: jnp.concatenate(
        [part[m * size : (m + 1) * size] for m in range(terms)], axis=1
    )
    out = jnp.dot(
        jnp.concatenate([wide(high), wide(low)], axis=0),
        mixed_split,
        preferred_element_type=jnp.float32,
    )
    return fold(out[:size]) + out[size:, :size]


HEAD = 4


def sector_copy(env, index, out, row, sem):
    terms, _, size, _ = env.shape
    target = out.at[pl.ds(row, terms * size)].reshape(terms, size, size)
    return pltpu.make_async_copy(env.at[:, index], target, sem)


def pick(table, left_env, right_env, outs, sems, begin, chunks):
    terms, total, size = left_env.shape[:3]
    copies = []
    for c, width in enumerate(chunks):
        for side in range(2):
            base = HEAD + (3 + side) * total
            from_left = table[HEAD + 5 * total + side] == 0
            for s in range(width):
                place = (
                    table[base + begin + s], outs[2 * c + side], s * terms * size,
                    sems.at[side, begin + s],
                )
                left, right = sector_copy(left_env, *place), sector_copy(right_env, *place)
                pl.when(from_left)(left.start)
                pl.when(jnp.logical_not(from_left))(right.start)
                copies.append(left)
        begin += width
    return copies


def open_kernel(
    chunks, parts, place_hbm, sectors_hbm, flow_hbm, bond_hbm, left_tensor, right_tensor,
    left_env, right_env, table, *refs,
):
    outs, refs = refs[: 2 * len(chunks)], refs[2 * len(chunks) :]
    place, sectors, flow, order, bond, small, sems, more, some = refs
    own, size = left_tensor.shape[0], left_tensor.shape[1]
    terms, total = left_env.shape[0], left_env.shape[1]
    base = chunks[0] * terms * size
    inputs = ((place_hbm, place), (sectors_hbm, sectors), (flow_hbm, flow), (bond_hbm, bond))
    loads = [pltpu.make_async_copy(a, b, some.at[i]) for i, (a, b) in enumerate(inputs)]
    for copy in loads:
        copy.start()
    for copy in loads:
        copy.wait()
    partition = place[0] // GROUP
    before = jnp.maximum(partition - 1, 0)
    after = jnp.minimum(partition + 1, parts - 1)
    first, last = partition == 0, partition == parts - 1
    swap = place[0] % 2 == 1
    table[0] = first.astype(jnp.int32)
    table[1] = last.astype(jnp.int32)
    table[2] = place[0] % GROUP
    table[3] = swap.astype(jnp.int32)
    for j in range(total):
        order[flow[before, j]] = j
        order[total + flow[partition, j]] = j
        order[2 * total + flow[after, j]] = j
    for j in range(total):
        joined = sectors[partition, j]
        table[HEAD + j] = order[j]
        table[HEAD + total + j] = order[2 * total + joined]
        table[HEAD + 2 * total + j] = joined
        ahead = jnp.where(last, joined, order[total + j])
        behind = jnp.where(first, j, order[total + sectors[before, j]])
        table[HEAD + 3 * total + j] = jnp.where(swap, behind, ahead)
        table[HEAD + 4 * total + j] = jnp.where(swap, ahead, behind)
    ahead, behind = last.astype(jnp.int32), 1 - first.astype(jnp.int32)
    table[HEAD + 5 * total] = jnp.where(swap, behind, ahead)
    table[HEAD + 5 * total + 1] = jnp.where(swap, ahead, behind)
    copies = pick(table, left_env, right_env, outs, sems, 0, chunks)
    small[...] = jnp.zeros_like(small)
    small[:, : bond.shape[1]] = bond[...]
    for side in range(2):
        for i in range(own):
            target = outs[side].at[pl.ds(base + i * size, size)]
            straight = pltpu.make_async_copy(
                (left_tensor, right_tensor)[side].at[i], target, more.at[side, i]
            )
            crossed = pltpu.make_async_copy(
                (right_tensor, left_tensor)[side].at[i], target, more.at[side, i]
            )
            pl.when(jnp.logical_not(swap))(straight.start)
            pl.when(swap)(crossed.start)
            copies.append(straight)
        copy = pltpu.make_async_copy(
            small, outs[side].at[pl.ds(base + own * size, terms)], more.at[side, own]
        )
        copy.start()
        copies.append(copy)
    for copy in copies:
        copy.wait()


def pick_kernel(begin, chunks, table, left_env, right_env, *refs):
    for copy in pick(table, left_env, right_env, refs[:-1], refs[-1], begin, chunks):
        copy.wait()


def prepare_kernel(
    own, table, states, pieces, onsite, vec_out, middle_out, plain_out, left_out, right_out,
    back_out, diagonal_out, mine_out,
):
    total, size = vec_out.shape[0], vec_out.shape[1]
    row = lax.broadcasted_iota(jnp.int32, (size, size), 0)
    col = lax.broadcasted_iota(jnp.int32, (size, size), 1)
    eye = (row == col).astype(jnp.float32)
    member = table[2]

    def block(sector, kind):
        return pieces[(sector // own) ^ member, sector % own, kind]

    square = jnp.zeros((size, size), jnp.float32)
    for j in range(total):
        value = states[(j // own) ^ member, j % own]
        square = square + value * value
    norm = jnp.sqrt(jnp.full((8, size), jnp.sum(square), jnp.float32))[0:1]

    for j in range(total):
        vec = states[(j // own) ^ member, j % own] / norm
        vec_out[j] = vec
        diagonal_out[j] = jnp.where(j // own == member, onsite[j % own], 0.0)
        left = jnp.where(table[0] == 1, eye, block(table[HEAD + j], 0))
        right = jnp.where(table[1] == 1, eye, block(table[HEAD + total + j], 1))
        left_out[j] = split_left(left)
        right_out[j] = split_right(right)
        back_out[j, 0] = jnp.transpose(left)
        back_out[j, 1] = jnp.transpose(right)
    for i in range(own):
        mine_out[i] = states[0, i] / norm
    for j in range(total):
        middle = inward(vec_out[j], left_out[j], right_out[j])
        middle_out[j] = split_right(middle)
        plain_out[j] = middle


def first_kernel(
    begin, flags, bond, got0, got1, sent0, sent1, middle, vec, back, diagonal,
    env_out, mixed_out, part_out,
):
    size = vec.shape[-1]
    terms = bond.shape[0]
    flag = lambda k: jnp.broadcast_to(flags[k, 0:1] != 0, (size, size))
    first, last, swap = flag(0), flag(1), flag(2)
    rows = lambda s, m: slice((s * terms + m) * size, (s * terms + m + 1) * size)

    def chosen(at, end, sent_a, sent_b, got_a, got_b):
        there = jnp.where(swap, got_b[at], got_a[at])
        return jnp.where(end, jnp.where(swap, sent_b[at], sent_a[at]), there)

    def weighted(m, k, block):
        tiles = block.reshape(size // 8, 8, size)
        return (tiles * bond[m, k][None]).reshape(size, size)

    for s in range(part_out.shape[0]):
        for m in range(terms):
            block = chosen(rows(s, m), first, sent1, sent0, got0, got1)
            env_out[s, rows(0, m)] = split_left(block)
        blocks = [chosen(rows(s, m), last, sent0, sent1, got1, got0) for m in range(terms)]
        for m in range(terms):
            total = weighted(m, 0, blocks[0])
            for k in range(1, terms):
                total = total + weighted(m, k, blocks[k])
            mixed_out[s, rows(0, m)] = split_left(total)
        j = begin + s
        core = core_of(env_out[s], mixed_out[s], middle[j], terms)
        part = product(product(back[j, 0], core), back[j, 1])
        part_out[s] = part + diagonal[j] * vec[j]


def early_kernel(
    begin, image, part, vec, middle, left, right, diagonal, env, mixed,
    resid_out, stat_out, moved, cores,
):
    width, size = image.shape[0], image.shape[1]
    terms = mixed.shape[1] // size
    zero = jnp.zeros((size, size), jnp.float32)
    tile = lambda value: jnp.full((8, 128), value, jnp.float32)

    along, norm = zero, zero
    for i in range(width):
        along = along + vec[begin + i] * image[i]
        norm = norm + vec[begin + i] * vec[begin + i]
    along, norm = jnp.sum(along), jnp.sum(norm)
    guess = jnp.where(norm > 0, along / jnp.where(norm > 0, norm, 1.0), 0.0)
    left_over, square = zero, zero
    for i in range(width):
        resid = image[i] - guess * vec[begin + i]
        resid_out[i] = resid
        left_over = left_over + resid * vec[begin + i]
        square = square + resid * resid
    square = tile(jnp.sum(square))
    length = jnp.sqrt(square + 1e-06)
    scale = (1.0 / length)[0:1]
    stat_out[0] = tile(guess)
    stat_out[1] = tile(norm)
    stat_out[2] = tile(jnp.sum(left_over))
    stat_out[3] = square
    stat_out[4] = length

    for i in range(width):
        resid = resid_out[i] * scale
        resid_out[i] = resid
        moved[i] = inward(resid, left[begin + i], right[begin + i])
    for i in range(width):
        cores[i] = core_of(env[i], mixed[i], split_right(moved[i]), terms)
    shares = lambda i: diagonal[begin + i]
    both = zero
    for i in range(width):
        resid = resid_out[i]
        both = both + moved[i] * cores[i] + (shares(i) * resid) * resid
    stat_out[5] = tile(jnp.sum(both))
    cross = zero
    for i in range(width):
        resid = resid_out[i]
        cross = cross + middle[begin + i] * cores[i]
        cross = cross + resid * (part[i] + shares(i) * vec[begin + i])
    stat_out[6] = tile(jnp.sum(cross))
    plain = zero
    for i in range(width):
        plain = plain + vec[begin + i] * part[i]
    stat_out[7] = tile(jnp.sum(plain))


def second_kernel(
    own, widths, flags, part0, part1, part2, part3, vec, left, right, diagonal, env, mixed, *refs
):
    count = len(widths)
    resids, stats = refs[:count], refs[count : 2 * count]
    second_out, share_out, work = refs[2 * count :]
    total, size, late = vec.shape[0], vec.shape[1], part0.shape[0]
    early = total - late
    terms = mixed.shape[1] // size
    zero = jnp.zeros((size, size), jnp.float32)
    tile = lambda value: jnp.full((8, 128), value, jnp.float32)

    images = [(part0[i] + part1[i]) + (part2[i] + part3[i]) for i in range(late)]
    along = zero
    for i in range(late):
        along = along + vec[early + i] * images[i]
    alpha1 = tile(jnp.sum(along))
    for stat in stats:
        alpha1 = alpha1 + (stat[0] * stat[1] + stat[2])
    rest = zero
    for i in range(late):
        images[i] = images[i] - alpha1[0:1] * vec[early + i]
        rest = rest + images[i] * images[i]
    square = tile(jnp.sum(rest)) + 1e-06
    for stat in stats:
        away = alpha1 - stat[0]
        square = square + jnp.maximum(
            stat[3] - 2.0 * away * stat[2] + away * (away * stat[1]), 0.0
        )
    beta = jnp.sqrt(square)
    scale = (1.0 / beta)[0:1]
    share = zero
    for i in range(late):
        j = early + i
        value = images[i] * scale
        work[j] = value
        moved = inward(value, left[j], right[j])
        core = core_of(env[i], mixed[i], split_right(moved), terms)
        share = share + moved * core + (diagonal[j] * value) * value
    begin = 0
    sums = zero[:8]
    for resid, stat, width in zip(resids, stats, widths):
        long, off = stat[4] / beta, (alpha1 - stat[0]) / beta
        sums = sums + long * (long * stat[5]) - off * (long * stat[6]) + off * (off * stat[7])
        for i in range(width):
            work[begin + i] = long[0:1] * resid[i] - off[0:1] * vec[begin + i]
        begin += width
    share_out[0] = tile(jnp.sum(share)) + sums
    share_out[1] = alpha1
    share_out[2] = beta
    for i in range(own):
        mine = work[i]
        for g in range(1, total // own):
            mine = jnp.where(flags[3 + g, 0:1] != 0, work[g * own + i], mine)
        second_out[i] = mine


def final_kernel(count, share0, share1, share2, share3, mine, second, out, energy_out):
    alpha2 = (share0[0] + share1[0]) + (share2[0] + share3[0])
    alpha1, beta = share0[1], share0[2]
    energy = (alpha1 + alpha2) / 2.0 - jnp.sqrt(((alpha1 - alpha2) / 2.0) ** 2 + beta * beta)
    height = jnp.sqrt(beta * beta + (energy - alpha1) ** 2)
    scale = math.sqrt(count)
    weight1 = (scale * (beta / height))[0:1]
    weight2 = (scale * ((energy - alpha1) / height))[0:1]
    for i in range(out.shape[0]):
        out[i] = weight1 * mine[i] + weight2 * second[i]
    energy_out[0] = energy[0, 0]


def on_device(
    state, left_tensor, right_tensor, onsite, left_env, right_env, mpo_bond, sectors, flow
):
    position = lax.axis_index("sites")
    parts = lax.axis_size("sites") // GROUP
    own, size = state.shape[0], state.shape[1]
    terms, total = left_env.shape[0], left_env.shape[1]
    f32, bf16 = jnp.float32, jnp.bfloat16
    begins = [sum(CHUNKS[:c]) for c in range(len(CHUNKS))]

    smem = pl.BlockSpec(memory_space=pltpu.SMEM)
    vmem = pl.BlockSpec(memory_space=pltpu.VMEM)
    hbm = pl.BlockSpec(memory_space=pltpu.HBM)
    shape = jax.ShapeDtypeStruct
    dma = pltpu.SemaphoreType.DMA
    params = lambda mib: pltpu.CompilerParams(vmem_limit_bytes=mib * MIB)

    small_cost = pl.CostEstimate(flops=1, bytes_accessed=1, transcendentals=0)

    rows = lambda width: width * terms * size
    chunk = lambda c: (rows(CHUNKS[c]) + (own * size + terms if c == 0 else 0), size)
    chunks = lambda some: [pltpu.VMEM(chunk(c), f32) for c in some for _ in range(2)]
    in_hbm = lambda *values: [
        pltpu.with_memory_space_constraint(value, pltpu.HBM) for value in values
    ]
    table, *opened = pl.pallas_call(
        functools.partial(open_kernel, CHUNKS[:1], parts),
        in_specs=[hbm] * 8,
        out_specs=[smem] + [vmem] * 2,
        out_shape=[shape((HEAD + 5 * total + 2,), jnp.int32)] + chunks([0]),
        scratch_shapes=[
            pltpu.SMEM((1,), jnp.int32),
            pltpu.SMEM(sectors.shape, jnp.int32),
            pltpu.SMEM(flow.shape, jnp.int32),
            pltpu.SMEM((3 * total,), jnp.int32),
            pltpu.VMEM(mpo_bond.shape, f32),
            pltpu.VMEM((terms, size), f32),
            dma((2, total)),
            dma((2, own + 1)),
            dma((4,)),
        ],
        cost_estimate=small_cost,
        compiler_params=params(16),
        name="open",
    )(
        *in_hbm(
            jnp.reshape(position, (1,)).astype(jnp.int32), sectors, flow, mpo_bond,
            left_tensor, right_tensor, left_env, right_env,
        )
    )
    later = range(1, len(CHUNKS))
    opened += pl.pallas_call(
        functools.partial(pick_kernel, CHUNKS[0], CHUNKS[1:]),
        in_specs=[smem] + [hbm] * 2,
        out_specs=[vmem] * (2 * len(later)),
        out_shape=chunks(later),
        scratch_shapes=[dma((2, total))],
        cost_estimate=small_cost,
        compiler_params=params(16),
        name="pick",
    )(table, *in_hbm(left_env, right_env))
    sent = [tuple(opened[2 * c : 2 * c + 2]) for c in range(len(CHUNKS))]
    states = gather(state)
    sent[1], _ = lax.optimization_barrier((sent[1], states))
    got = [tuple(hand_over(block, side) for side, block in enumerate(pair)) for pair in sent]

    tail = [block[rows(CHUNKS[0]) :] for block in got[0]]
    swap = table[3] == 1
    from_left, from_right = jnp.where(swap, tail[1], tail[0]), jnp.where(swap, tail[0], tail[1])
    small = jnp.eye(terms, dtype=f32)
    bond_left = jnp.where(table[0] == 1, small, from_left[own * size :, : mpo_bond.shape[1]])
    bond_right = jnp.where(table[1] == 1, small, from_right[own * size :, : mpo_bond.shape[1]])
    bond = jnp.sum(bond_left[:, None, :] * bond_right[None, :, :], axis=2)
    bond = jnp.broadcast_to(bond[:, :, None, None], (terms, terms, 8, size))
    flags = jnp.concatenate(
        [table[0:2], table[3:4], (table[2] == jnp.arange(GROUP)).astype(jnp.int32)]
    )
    flags = jnp.broadcast_to(flags[:, None, None], (3 + GROUP, 8, size))
    tensors = lambda block: block[: own * size].reshape(own, size, size)
    pieces = gather(jnp.stack([tensors(from_left), tensors(from_right)], 1))

    vec, middle, plain, left, right, back, diagonal, mine = pl.pallas_call(
        functools.partial(prepare_kernel, own),
        in_specs=[smem] + [vmem] * 3,
        out_specs=[vmem] * 8,
        out_shape=[
            shape((total, size, size), f32),
            shape((total, 2 * size, 2 * size), bf16),
            shape((total, size, size), f32),
            shape((total, size, 2 * size), bf16),
            shape((total, 2 * size, 2 * size), bf16),
            shape((total, 2, size, size), f32),
            shape((total, size, size), f32),
            shape((own, size, size), f32),
        ],
        cost_estimate=small_cost,
        compiler_params=params(12),
        name="prepare",
    )(table, states, pieces, onsite)

    def early(begin, width, image, part, env, mixed, after):
        image, _ = lax.optimization_barrier((image, after))
        return pl.pallas_call(
            functools.partial(early_kernel, begin),
            in_specs=[vmem] * 9,
            out_specs=[vmem] * 2,
            out_shape=[shape((width, size, size), f32), shape((8, 8, 128), f32)],
            scratch_shapes=[pltpu.VMEM((width, size, size), f32)] * 2,
            cost_estimate=small_cost,
            compiler_params=params(12),
            name="early_second_matvec",
        )(image, part, vec, plain, left, right, diagonal, env, mixed)

    resids, stats, waits, held = [], [], [], None
    for c, (begin, width) in enumerate(zip(begins, CHUNKS)):
        if c > 0:
            got[c], _ = lax.optimization_barrier((got[c], waits[c - 1]))
        env, mixed, part = pl.pallas_call(
            functools.partial(first_kernel, begin),
            in_specs=[vmem] * 10,
            out_specs=[vmem] * 3,
            out_shape=[
                shape((width, rows(1), 2 * size), bf16),
                shape((width, rows(1), 2 * size), bf16),
                shape((width, size, size), f32),
            ],
            cost_estimate=small_cost,
        compiler_params=params(12),
            name=f"first_matvec{c}",
        )(flags, bond, *got[c], *sent[c], middle, vec, back, diagonal)
        if held is not None:
            resid, stat = early(*held, after=part)
            resids.append(resid)
            stats.append(stat)
        if c < len(CHUNKS) - 1:
            image = total_of(part)
            held = (begin, width, image, part, env, mixed)
            waits.append([image] + stats[-1:])

    parts = [part] + [partner(part, mask) for mask in (1, 2, 3)]
    second, share = pl.pallas_call(
        functools.partial(second_kernel, own, CHUNKS[:-1]),
        in_specs=[vmem] * (11 + 2 * (len(CHUNKS) - 1)),
        out_specs=[vmem] * 2,
        out_shape=[shape((own, size, size), f32), shape((3, 8, 128), f32)],
        scratch_shapes=[pltpu.VMEM((total, size, size), f32)],
        cost_estimate=small_cost,
        compiler_params=params(12),
        name="second_matvec",
    )(flags, *parts, vec, left, right, diagonal, env, mixed, *resids, *stats)

    shares = [share] + [partner(share[:1], mask) for mask in (1, 2, 3)]
    new_state, energy = pl.pallas_call(
        functools.partial(final_kernel, total * size * size),
        in_specs=[vmem] * 6,
        out_specs=[vmem, smem],
        out_shape=[shape((own, size, size), f32), shape((1,), f32)],
        cost_estimate=small_cost,
        compiler_params=params(4),
        name="ritz_update",
    )(*shares, mine, second)
    return (new_state, energy)


def solution(mesh):
    return jax.shard_map(
        on_device,
        mesh=mesh,
        in_specs=(
            P(("groups", "sites"), None, None),
            P(("groups", "sites"), None, None),
            P(("groups", "sites"), None, None),
            P(("groups", "sites"), None, None),
            P(("groups", "sites"), None, None, None),
            P(("groups", "sites"), None, None, None),
            P(("groups", "sites"), None),
            P("groups", None),
            P("groups", None),
        ),
        out_specs=(P(("groups", "sites"), None, None), P(("groups", "sites"))),
        check_vma=False,
    )
```

```python
import functools
import math

import jax
import jax.numpy as jnp
from jax import lax
from jax.experimental import pallas as pl
from jax.experimental.pallas import tpu as pltpu
from jax.sharding import PartitionSpec as P

GROUP = 4
CHUNKS = (3, 3, 1, 1)
MIB = 1024 * 1024


def hand_over(block, parity):
    count = lax.axis_size("sites")
    route = [(i, i + (GROUP if i % 2 == parity else -GROUP)) for i in range(count)]
    return lax.ppermute(block, "sites", [(i, j) for i, j in route if 0 <= j < count])


def partner(block, mask):
    route = [(i, i ^ mask) for i in range(lax.axis_size("sites"))]
    return lax.ppermute(block, "sites", route)


def gather(block):
    pieces = [block] + [partner(block, mask) for mask in (1, 2, 3)]
    return jnp.stack(pieces, 0)


def total_of(block):
    pair = block + partner(block, 1)
    return pair + partner(pair, 2)


def halves(value):
    high = value.astype(jnp.bfloat16)
    return high, (value - high.astype(jnp.float32)).astype(jnp.bfloat16)


def split_left(value):
    return jnp.concatenate(halves(value), axis=1)


def split_right(value):
    high, low = halves(value)
    return jnp.concatenate(
        [
            jnp.concatenate([high, low], axis=1),
            jnp.concatenate([high, jnp.zeros_like(low)], axis=1),
        ],
        axis=0,
    )


def fold(wide):
    half = wide.shape[1] // 2
    return wide[:, :half] + wide[:, half:]


def product(left, right):
    return fold(jnp.dot(split_left(left), split_right(right), preferred_element_type=jnp.float32))


def inward(block, left, right):
    temp = fold(jnp.dot(left, split_right(block), preferred_element_type=jnp.float32))
    return fold(jnp.dot(split_left(temp), right, preferred_element_type=jnp.float32))


def core_of(env_split, mixed_split, middle_split, terms):
    size = mixed_split.shape[0] // terms
    temp = fold(jnp.dot(env_split, middle_split, preferred_element_type=jnp.float32))
    high, low = halves(temp)
    wide = lambda part: jnp.concatenate(
        [part[m * size : (m + 1) * size] for m in range(terms)], axis=1
    )
    out = jnp.dot(
        jnp.concatenate([wide(high), wide(low)], axis=0),
        mixed_split,
        preferred_element_type=jnp.float32,
    )
    return fold(out[:size]) + out[size:, :size]


HEAD = 4


def sector_copy(env, index, out, row, sem):
    terms, _, size, _ = env.shape
    target = out.at[pl.ds(row, terms * size)].reshape(terms, size, size)
    return pltpu.make_async_copy(env.at[:, index], target, sem)


def pick(table, left_env, right_env, outs, sems, begin, chunks):
    terms, total, size = left_env.shape[:3]
    copies = []
    for c, width in enumerate(chunks):
        for side in range(2):
            base = HEAD + (3 + side) * total
            from_left = table[HEAD + 5 * total + side] == 0
            for s in range(width):
                place = (
                    table[base + begin + s], outs[2 * c + side], s * terms * size,
                    sems.at[side, begin + s],
                )
                left, right = sector_copy(left_env, *place), sector_copy(right_env, *place)
                pl.when(from_left)(left.start)
                pl.when(jnp.logical_not(from_left))(right.start)
                copies.append(left)
        begin += width
    return copies


def open_kernel(
    chunks, parts, place_hbm, sectors_hbm, flow_hbm, bond_hbm, left_tensor, right_tensor,
    left_env, right_env, table, *refs,
):
    outs, refs = refs[: 2 * len(chunks)], refs[2 * len(chunks) :]
    place, sectors, flow, order, bond, small, sems, more, some = refs
    own, size = left_tensor.shape[0], left_tensor.shape[1]
    terms, total = left_env.shape[0], left_env.shape[1]
    base = chunks[0] * terms * size
    inputs = ((place_hbm, place), (sectors_hbm, sectors), (flow_hbm, flow), (bond_hbm, bond))
    loads = [pltpu.make_async_copy(a, b, some.at[i]) for i, (a, b) in enumerate(inputs)]
    for copy in loads:
        copy.start()
    for copy in loads:
        copy.wait()
    partition = place[0] // GROUP
    before = jnp.maximum(partition - 1, 0)
    after = jnp.minimum(partition + 1, parts - 1)
    first, last = partition == 0, partition == parts - 1
    swap = place[0] % 2 == 1
    table[0] = first.astype(jnp.int32)
    table[1] = last.astype(jnp.int32)
    table[2] = place[0] % GROUP
    table[3] = swap.astype(jnp.int32)
    for j in range(total):
        order[flow[before, j]] = j
        order[total + flow[partition, j]] = j
        order[2 * total + flow[after, j]] = j
    for j in range(total):
        joined = sectors[partition, j]
        table[HEAD + j] = order[j]
        table[HEAD + total + j] = order[2 * total + joined]
        table[HEAD + 2 * total + j] = joined
        ahead = jnp.where(last, joined, order[total + j])
        behind = jnp.where(first, j, order[total + sectors[before, j]])
        table[HEAD + 3 * total + j] = jnp.where(swap, behind, ahead)
        table[HEAD + 4 * total + j] = jnp.where(swap, ahead, behind)
    ahead, behind = last.astype(jnp.int32), 1 - first.astype(jnp.int32)
    table[HEAD + 5 * total] = jnp.where(swap, behind, ahead)
    table[HEAD + 5 * total + 1] = jnp.where(swap, ahead, behind)
    copies = pick(table, left_env, right_env, outs, sems, 0, chunks)
    small[...] = jnp.zeros_like(small)
    small[:, : bond.shape[1]] = bond[...]
    for side in range(2):
        for i in range(own):
            target = outs[side].at[pl.ds(base + i * size, size)]
            straight = pltpu.make_async_copy(
                (left_tensor, right_tensor)[side].at[i], target, more.at[side, i]
            )
            crossed = pltpu.make_async_copy(
                (right_tensor, left_tensor)[side].at[i], target, more.at[side, i]
            )
            pl.when(jnp.logical_not(swap))(straight.start)
            pl.when(swap)(crossed.start)
            copies.append(straight)
        copy = pltpu.make_async_copy(
            small, outs[side].at[pl.ds(base + own * size, terms)], more.at[side, own]
        )
        copy.start()
        copies.append(copy)
    for copy in copies:
        copy.wait()


def pick_kernel(begin, chunks, table, left_env, right_env, *refs):
    for copy in pick(table, left_env, right_env, refs[:-1], refs[-1], begin, chunks):
        copy.wait()


def prepare_kernel(
    own, table, states, pieces, onsite, vec_out, middle_out, plain_out, left_out, right_out,
    back_out, diagonal_out, mine_out,
):
    total, size = vec_out.shape[0], vec_out.shape[1]
    row = lax.broadcasted_iota(jnp.int32, (size, size), 0)
    col = lax.broadcasted_iota(jnp.int32, (size, size), 1)
    eye = (row == col).astype(jnp.float32)
    member = table[2]

    def block(sector, kind):
        return pieces[(sector // own) ^ member, sector % own, kind]

    square = jnp.zeros((size, size), jnp.float32)
    for j in range(total):
        value = states[(j // own) ^ member, j % own]
        square = square + value * value
    norm = jnp.sqrt(jnp.full((8, size), jnp.sum(square), jnp.float32))[0:1]

    for j in range(total):
        vec = states[(j // own) ^ member, j % own] / norm
        vec_out[j] = vec
        diagonal_out[j] = jnp.where(j // own == member, onsite[j % own], 0.0)
        left = jnp.where(table[0] == 1, eye, block(table[HEAD + j], 0))
        right = jnp.where(table[1] == 1, eye, block(table[HEAD + total + j], 1))
        left_out[j] = split_left(left)
        right_out[j] = split_right(right)
        back_out[j, 0] = jnp.transpose(left)
        back_out[j, 1] = jnp.transpose(right)
    for i in range(own):
        mine_out[i] = states[0, i] / norm
    for j in range(total):
        middle = inward(vec_out[j], left_out[j], right_out[j])
        middle_out[j] = split_right(middle)
        plain_out[j] = middle


def first_kernel(
    begin, flags, bond, got0, got1, sent0, sent1, middle, vec, back, diagonal,
    env_out, mixed_out, part_out,
):
    size = vec.shape[-1]
    terms = bond.shape[0]
    flag = lambda k: jnp.broadcast_to(flags[k, 0:1] != 0, (size, size))
    first, last, swap = flag(0), flag(1), flag(2)
    rows = lambda s, m: slice((s * terms + m) * size, (s * terms + m + 1) * size)

    def chosen(at, end, sent_a, sent_b, got_a, got_b):
        there = jnp.where(swap, got_b[at], got_a[at])
        return jnp.where(end, jnp.where(swap, sent_b[at], sent_a[at]), there)

    def weighted(m, k, block):
        tiles = block.reshape(size // 8, 8, size)
        return (tiles * bond[m, k][None]).reshape(size, size)

    for s in range(part_out.shape[0]):
        for m in range(terms):
            block = chosen(rows(s, m), first, sent1, sent0, got0, got1)
            env_out[s, rows(0, m)] = split_left(block)
        blocks = [chosen(rows(s, m), last, sent0, sent1, got1, got0) for m in range(terms)]
        for m in range(terms):
            total = weighted(m, 0, blocks[0])
            for k in range(1, terms):
                total = total + weighted(m, k, blocks[k])
            mixed_out[s, rows(0, m)] = split_left(total)
        j = begin + s
        core = core_of(env_out[s], mixed_out[s], middle[j], terms)
        part = product(product(back[j, 0], core), back[j, 1])
        part_out[s] = part + diagonal[j] * vec[j]


def early_kernel(
    begin, image, part, vec, middle, left, right, diagonal, env, mixed,
    resid_out, stat_out, moved, cores,
):
    width, size = image.shape[0], image.shape[1]
    terms = mixed.shape[1] // size
    zero = jnp.zeros((size, size), jnp.float32)
    tile = lambda value: jnp.full((8, 128), value, jnp.float32)

    along, norm = zero, zero
    for i in range(width):
        along = along + vec[begin + i] * image[i]
        norm = norm + vec[begin + i] * vec[begin + i]
    along, norm = jnp.sum(along), jnp.sum(norm)
    guess = jnp.where(norm > 0, along / jnp.where(norm > 0, norm, 1.0), 0.0)
    left_over, square = zero, zero
    for i in range(width):
        resid = image[i] - guess * vec[begin + i]
        resid_out[i] = resid
        left_over = left_over + resid * vec[begin + i]
        square = square + resid * resid
    square = tile(jnp.sum(square))
    length = jnp.sqrt(square + 1e-06)
    scale = (1.0 / length)[0:1]
    stat_out[0] = tile(guess)
    stat_out[1] = tile(norm)
    stat_out[2] = tile(jnp.sum(left_over))
    stat_out[3] = square
    stat_out[4] = length

    for i in range(width):
        resid = resid_out[i] * scale
        resid_out[i] = resid
        moved[i] = inward(resid, left[begin + i], right[begin + i])
    for i in range(width):
        cores[i] = core_of(env[i], mixed[i], split_right(moved[i]), terms)
    shares = lambda i: diagonal[begin + i]
    both = zero
    for i in range(width):
        resid = resid_out[i]
        both = both + moved[i] * cores[i] + (shares(i) * resid) * resid
    stat_out[5] = tile(jnp.sum(both))
    cross = zero
    for i in range(width):
        resid = resid_out[i]
        cross = cross + middle[begin + i] * cores[i]
        cross = cross + resid * (part[i] + shares(i) * vec[begin + i])
    stat_out[6] = tile(jnp.sum(cross))
    plain = zero
    for i in range(width):
        plain = plain + vec[begin + i] * part[i]
    stat_out[7] = tile(jnp.sum(plain))


def second_kernel(
    own, widths, flags, part0, part1, part2, part3, vec, left, right, diagonal, env, mixed, *refs
):
    count = len(widths)
    resids, stats = refs[:count], refs[count : 2 * count]
    second_out, share_out, work = refs[2 * count :]
    total, size, late = vec.shape[0], vec.shape[1], part0.shape[0]
    early = total - late
    terms = mixed.shape[1] // size
    zero = jnp.zeros((size, size), jnp.float32)
    tile = lambda value: jnp.full((8, 128), value, jnp.float32)

    images = [(part0[i] + part1[i]) + (part2[i] + part3[i]) for i in range(late)]
    along = zero
    for i in range(late):
        along = along + vec[early + i] * images[i]
    alpha1 = tile(jnp.sum(along))
    for stat in stats:
        alpha1 = alpha1 + (stat[0] * stat[1] + stat[2])
    rest = zero
    for i in range(late):
        images[i] = images[i] - alpha1[0:1] * vec[early + i]
        rest = rest + images[i] * images[i]
    square = tile(jnp.sum(rest)) + 1e-06
    for stat in stats:
        away = alpha1 - stat[0]
        square = square + jnp.maximum(
            stat[3] - 2.0 * away * stat[2] + away * (away * stat[1]), 0.0
        )
    beta = jnp.sqrt(square)
    scale = (1.0 / beta)[0:1]
    share = zero
    for i in range(late):
        j = early + i
        value = images[i] * scale
        work[j] = value
        moved = inward(value, left[j], right[j])
        core = core_of(env[i], mixed[i], split_right(moved), terms)
        share = share + moved * core + (diagonal[j] * value) * value
    begin = 0
    sums = zero[:8]
    for resid, stat, width in zip(resids, stats, widths):
        long, off = stat[4] / beta, (alpha1 - stat[0]) / beta
        sums = sums + long * (long * stat[5]) - off * (long * stat[6]) + off * (off * stat[7])
        for i in range(width):
            work[begin + i] = long[0:1] * resid[i] - off[0:1] * vec[begin + i]
        begin += width
    share_out[0] = tile(jnp.sum(share)) + sums
    share_out[1] = alpha1
    share_out[2] = beta
    for i in range(own):
        mine = work[i]
        for g in range(1, total // own):
            mine = jnp.where(flags[3 + g, 0:1] != 0, work[g * own + i], mine)
        second_out[i] = mine


def final_kernel(count, share0, share1, share2, share3, mine, second, out, energy_out):
    alpha2 = (share0[0] + share1[0]) + (share2[0] + share3[0])
    alpha1, beta = share0[1], share0[2]
    energy = (alpha1 + alpha2) / 2.0 - jnp.sqrt(((alpha1 - alpha2) / 2.0) ** 2 + beta * beta)
    height = jnp.sqrt(beta * beta + (energy - alpha1) ** 2)
    scale = math.sqrt(count)
    weight1 = (scale * (beta / height))[0:1]
    weight2 = (scale * ((energy - alpha1) / height))[0:1]
    for i in range(out.shape[0]):
        out[i] = weight1 * mine[i] + weight2 * second[i]
    energy_out[0] = energy[0, 0]


def on_device(
    state, left_tensor, right_tensor, onsite, left_env, right_env, mpo_bond, sectors, flow
):
    position = lax.axis_index("sites")
    parts = lax.axis_size("sites") // GROUP
    own, size = state.shape[0], state.shape[1]
    terms, total = left_env.shape[0], left_env.shape[1]
    f32, bf16 = jnp.float32, jnp.bfloat16
    begins = [sum(CHUNKS[:c]) for c in range(len(CHUNKS))]

    smem = pl.BlockSpec(memory_space=pltpu.SMEM)
    vmem = pl.BlockSpec(memory_space=pltpu.VMEM)
    hbm = pl.BlockSpec(memory_space=pltpu.HBM)
    shape = jax.ShapeDtypeStruct
    dma = pltpu.SemaphoreType.DMA
    params = lambda mib: pltpu.CompilerParams(vmem_limit_bytes=mib * MIB)

    small_cost = pl.CostEstimate(flops=1, bytes_accessed=1, transcendentals=0)

    rows = lambda width: width * terms * size
    chunk = lambda c: (rows(CHUNKS[c]) + (own * size + terms if c == 0 else 0), size)
    chunks = lambda some: [pltpu.VMEM(chunk(c), f32) for c in some for _ in range(2)]
    in_hbm = lambda *values: [
        pltpu.with_memory_space_constraint(value, pltpu.HBM) for value in values
    ]
    table, *opened = pl.pallas_call(
        functools.partial(open_kernel, CHUNKS[:1], parts),
        in_specs=[hbm] * 8,
        out_specs=[smem] + [vmem] * 2,
        out_shape=[shape((HEAD + 5 * total + 2,), jnp.int32)] + chunks([0]),
        scratch_shapes=[
            pltpu.SMEM((1,), jnp.int32),
            pltpu.SMEM(sectors.shape, jnp.int32),
            pltpu.SMEM(flow.shape, jnp.int32),
            pltpu.SMEM((3 * total,), jnp.int32),
            pltpu.VMEM(mpo_bond.shape, f32),
            pltpu.VMEM((terms, size), f32),
            dma((2, total)),
            dma((2, own + 1)),
            dma((4,)),
        ],
        cost_estimate=small_cost,
        compiler_params=params(16),
        name="open",
    )(
        *in_hbm(
            jnp.reshape(position, (1,)).astype(jnp.int32), sectors, flow, mpo_bond,
            left_tensor, right_tensor, left_env, right_env,
        )
    )
    later = range(1, len(CHUNKS))
    opened += pl.pallas_call(
        functools.partial(pick_kernel, CHUNKS[0], CHUNKS[1:]),
        in_specs=[smem] + [hbm] * 2,
        out_specs=[vmem] * (2 * len(later)),
        out_shape=chunks(later),
        scratch_shapes=[dma((2, total))],
        cost_estimate=small_cost,
        compiler_params=params(16),
        name="pick",
    )(table, *in_hbm(left_env, right_env))
    sent = [tuple(opened[2 * c : 2 * c + 2]) for c in range(len(CHUNKS))]
    states = gather(state)
    sent[1], _ = lax.optimization_barrier((sent[1], states))
    got = [tuple(hand_over(block, side) for side, block in enumerate(pair)) for pair in sent]

    tail = [block[rows(CHUNKS[0]) :] for block in got[0]]
    swap = table[3] == 1
    from_left, from_right = jnp.where(swap, tail[1], tail[0]), jnp.where(swap, tail[0], tail[1])
    small = jnp.eye(terms, dtype=f32)
    bond_left = jnp.where(table[0] == 1, small, from_left[own * size :, : mpo_bond.shape[1]])
    bond_right = jnp.where(table[1] == 1, small, from_right[own * size :, : mpo_bond.shape[1]])
    bond = jnp.sum(bond_left[:, None, :] * bond_right[None, :, :], axis=2)
    bond = jnp.broadcast_to(bond[:, :, None, None], (terms, terms, 8, size))
    flags = jnp.concatenate(
        [table[0:2], table[3:4], (table[2] == jnp.arange(GROUP)).astype(jnp.int32)]
    )
    flags = jnp.broadcast_to(flags[:, None, None], (3 + GROUP, 8, size))
    tensors = lambda block: block[: own * size].reshape(own, size, size)
    pieces = gather(jnp.stack([tensors(from_left), tensors(from_right)], 1))

    vec, middle, plain, left, right, back, diagonal, mine = pl.pallas_call(
        functools.partial(prepare_kernel, own),
        in_specs=[smem] + [vmem] * 3,
        out_specs=[vmem] * 8,
        out_shape=[
            shape((total, size, size), f32),
            shape((total, 2 * size, 2 * size), bf16),
            shape((total, size, size), f32),
            shape((total, size, 2 * size), bf16),
            shape((total, 2 * size, 2 * size), bf16),
            shape((total, 2, size, size), f32),
            shape((total, size, size), f32),
            shape((own, size, size), f32),
        ],
        cost_estimate=small_cost,
        compiler_params=params(12),
        name="prepare",
    )(table, states, pieces, onsite)

    def early(begin, width, image, part, env, mixed, after):
        image, _ = lax.optimization_barrier((image, after))
        return pl.pallas_call(
            functools.partial(early_kernel, begin),
            in_specs=[vmem] * 9,
            out_specs=[vmem] * 2,
            out_shape=[shape((width, size, size), f32), shape((8, 8, 128), f32)],
            scratch_shapes=[pltpu.VMEM((width, size, size), f32)] * 2,
            cost_estimate=small_cost,
            compiler_params=params(12),
            name="early_second_matvec",
        )(image, part, vec, plain, left, right, diagonal, env, mixed)

    resids, stats, waits, held = [], [], [], None
    for c, (begin, width) in enumerate(zip(begins, CHUNKS)):
        if c > 0:
            got[c], _ = lax.optimization_barrier((got[c], waits[c - 1]))
        env, mixed, part = pl.pallas_call(
            functools.partial(first_kernel, begin),
            in_specs=[vmem] * 10,
            out_specs=[vmem] * 3,
            out_shape=[
                shape((width, rows(1), 2 * size), bf16),
                shape((width, rows(1), 2 * size), bf16),
                shape((width, size, size), f32),
            ],
            cost_estimate=small_cost,
        compiler_params=params(12),
            name=f"first_matvec{c}",
        )(flags, bond, *got[c], *sent[c], middle, vec, back, diagonal)
        if held is not None:
            resid, stat = early(*held, after=part)
            resids.append(resid)
            stats.append(stat)
        if c < len(CHUNKS) - 1:
            beside = part + partner(part, 1)
            image = beside + partner(beside, 2)
            held = (begin, width, image, part, env, mixed)
            waits.append([beside if c == len(CHUNKS) - 2 else image] + stats[-1:])

    parts = [part] + [partner(part, mask) for mask in (1, 2, 3)]
    second, share = pl.pallas_call(
        functools.partial(second_kernel, own, CHUNKS[:-1]),
        in_specs=[vmem] * (11 + 2 * (len(CHUNKS) - 1)),
        out_specs=[vmem] * 2,
        out_shape=[shape((own, size, size), f32), shape((3, 8, 128), f32)],
        scratch_shapes=[pltpu.VMEM((total, size, size), f32)],
        cost_estimate=small_cost,
        compiler_params=params(12),
        name="second_matvec",
    )(flags, *parts, vec, left, right, diagonal, env, mixed, *resids, *stats)

    shares = [share] + [partner(share[:1], mask) for mask in (1, 2, 3)]
    new_state, energy = pl.pallas_call(
        functools.partial(final_kernel, total * size * size),
        in_specs=[vmem] * 6,
        out_specs=[vmem, smem],
        out_shape=[shape((own, size, size), f32), shape((1,), f32)],
        cost_estimate=small_cost,
        compiler_params=params(4),
        name="ritz_update",
    )(*shares, mine, second)
    return (new_state, energy)


def solution(mesh):
    return jax.shard_map(
        on_device,
        mesh=mesh,
        in_specs=(
            P(("groups", "sites"), None, None),
            P(("groups", "sites"), None, None),
            P(("groups", "sites"), None, None),
            P(("groups", "sites"), None, None),
            P(("groups", "sites"), None, None, None),
            P(("groups", "sites"), None, None, None),
            P(("groups", "sites"), None),
            P("groups", None),
            P("groups", None),
        ),
        out_specs=(P(("groups", "sites"), None, None), P(("groups", "sites"))),
        check_vma=False,
    )
```

```python
import functools
import math

import jax
import jax.numpy as jnp
from jax import lax
from jax.experimental import pallas as pl
from jax.experimental.pallas import tpu as pltpu
from jax.sharding import PartitionSpec as P

GROUP = 4
CHUNKS = (2, 3, 2, 1)
MIB = 1024 * 1024


def hand_over(block, parity):
    count = lax.axis_size("sites")
    route = [(i, i + (GROUP if i % 2 == parity else -GROUP)) for i in range(count)]
    return lax.ppermute(block, "sites", [(i, j) for i, j in route if 0 <= j < count])


def partner(block, mask):
    route = [(i, i ^ mask) for i in range(lax.axis_size("sites"))]
    return lax.ppermute(block, "sites", route)


def gather(block):
    pieces = [block] + [partner(block, mask) for mask in (1, 2, 3)]
    return jnp.stack(pieces, 0)


def total_of(block):
    pair = block + partner(block, 1)
    return pair + partner(pair, 2)


def halves(value):
    high = value.astype(jnp.bfloat16)
    return high, (value - high.astype(jnp.float32)).astype(jnp.bfloat16)


def split_left(value):
    return jnp.concatenate(halves(value), axis=1)


def split_right(value):
    high, low = halves(value)
    return jnp.concatenate(
        [
            jnp.concatenate([high, low], axis=1),
            jnp.concatenate([high, jnp.zeros_like(low)], axis=1),
        ],
        axis=0,
    )


def fold(wide):
    half = wide.shape[1] // 2
    return wide[:, :half] + wide[:, half:]


def product(left, right):
    return fold(jnp.dot(split_left(left), split_right(right), preferred_element_type=jnp.float32))


def inward(block, left, right):
    temp = fold(jnp.dot(left, split_right(block), preferred_element_type=jnp.float32))
    return fold(jnp.dot(split_left(temp), right, preferred_element_type=jnp.float32))


def core_of(env_split, mixed_split, middle_split, terms):
    size = mixed_split.shape[0] // terms
    temp = fold(jnp.dot(env_split, middle_split, preferred_element_type=jnp.float32))
    high, low = halves(temp)
    wide = lambda part: jnp.concatenate(
        [part[m * size : (m + 1) * size] for m in range(terms)], axis=1
    )
    out = jnp.dot(
        jnp.concatenate([wide(high), wide(low)], axis=0),
        mixed_split,
        preferred_element_type=jnp.float32,
    )
    return fold(out[:size]) + out[size:, :size]


HEAD = 4


def sector_copy(env, index, out, row, sem):
    terms, _, size, _ = env.shape
    target = out.at[pl.ds(row, terms * size)].reshape(terms, size, size)
    return pltpu.make_async_copy(env.at[:, index], target, sem)


def pick(table, left_env, right_env, outs, sems, begin, chunks):
    terms, total, size = left_env.shape[:3]
    copies = []
    for c, width in enumerate(chunks):
        for side in range(2):
            base = HEAD + (3 + side) * total
            from_left = table[HEAD + 5 * total + side] == 0
            for s in range(width):
                place = (
                    table[base + begin + s], outs[2 * c + side], s * terms * size,
                    sems.at[side, begin + s],
                )
                left, right = sector_copy(left_env, *place), sector_copy(right_env, *place)
                pl.when(from_left)(left.start)
                pl.when(jnp.logical_not(from_left))(right.start)
                copies.append(left)
        begin += width
    return copies


def open_kernel(
    chunks, parts, place_hbm, sectors_hbm, flow_hbm, bond_hbm, left_tensor, right_tensor,
    left_env, right_env, table, *refs,
):
    outs, refs = refs[: 2 * len(chunks)], refs[2 * len(chunks) :]
    place, sectors, flow, order, bond, small, sems, more, some = refs
    own, size = left_tensor.shape[0], left_tensor.shape[1]
    terms, total = left_env.shape[0], left_env.shape[1]
    base = chunks[0] * terms * size
    inputs = ((place_hbm, place), (sectors_hbm, sectors), (flow_hbm, flow), (bond_hbm, bond))
    loads = [pltpu.make_async_copy(a, b, some.at[i]) for i, (a, b) in enumerate(inputs)]
    for copy in loads:
        copy.start()
    for copy in loads:
        copy.wait()
    partition = place[0] // GROUP
    before = jnp.maximum(partition - 1, 0)
    after = jnp.minimum(partition + 1, parts - 1)
    first, last = partition == 0, partition == parts - 1
    swap = place[0] % 2 == 1
    table[0] = first.astype(jnp.int32)
    table[1] = last.astype(jnp.int32)
    table[2] = place[0] % GROUP
    table[3] = swap.astype(jnp.int32)
    for j in range(total):
        order[flow[before, j]] = j
        order[total + flow[partition, j]] = j
        order[2 * total + flow[after, j]] = j
    for j in range(total):
        joined = sectors[partition, j]
        table[HEAD + j] = order[j]
        table[HEAD + total + j] = order[2 * total + joined]
        table[HEAD + 2 * total + j] = joined
        ahead = jnp.where(last, joined, order[total + j])
        behind = jnp.where(first, j, order[total + sectors[before, j]])
        table[HEAD + 3 * total + j] = jnp.where(swap, behind, ahead)
        table[HEAD + 4 * total + j] = jnp.where(swap, ahead, behind)
    ahead, behind = last.astype(jnp.int32), 1 - first.astype(jnp.int32)
    table[HEAD + 5 * total] = jnp.where(swap, behind, ahead)
    table[HEAD + 5 * total + 1] = jnp.where(swap, ahead, behind)
    copies = pick(table, left_env, right_env, outs, sems, 0, chunks)
    small[...] = jnp.zeros_like(small)
    small[:, : bond.shape[1]] = bond[...]
    for side in range(2):
        for i in range(own):
            target = outs[side].at[pl.ds(base + i * size, size)]
            straight = pltpu.make_async_copy(
                (left_tensor, right_tensor)[side].at[i], target, more.at[side, i]
            )
            crossed = pltpu.make_async_copy(
                (right_tensor, left_tensor)[side].at[i], target, more.at[side, i]
            )
            pl.when(jnp.logical_not(swap))(straight.start)
            pl.when(swap)(crossed.start)
            copies.append(straight)
        copy = pltpu.make_async_copy(
            small, outs[side].at[pl.ds(base + own * size, terms)], more.at[side, own]
        )
        copy.start()
        copies.append(copy)
    for copy in copies:
        copy.wait()


def pick_kernel(begin, chunks, table, left_env, right_env, *refs):
    for copy in pick(table, left_env, right_env, refs[:-1], refs[-1], begin, chunks):
        copy.wait()


def prepare_kernel(
    own, table, states, pieces, onsite, vec_out, middle_out, plain_out, left_out, right_out,
    back_out, diagonal_out, mine_out,
):
    total, size = vec_out.shape[0], vec_out.shape[1]
    row = lax.broadcasted_iota(jnp.int32, (size, size), 0)
    col = lax.broadcasted_iota(jnp.int32, (size, size), 1)
    eye = (row == col).astype(jnp.float32)
    member = table[2]

    def block(sector, kind):
        return pieces[(sector // own) ^ member, sector % own, kind]

    square = jnp.zeros((size, size), jnp.float32)
    for j in range(total):
        value = states[(j // own) ^ member, j % own]
        square = square + value * value
    norm = jnp.sqrt(jnp.full((8, size), jnp.sum(square), jnp.float32))[0:1]

    for j in range(total):
        vec = states[(j // own) ^ member, j % own] / norm
        vec_out[j] = vec
        diagonal_out[j] = jnp.where(j // own == member, onsite[j % own], 0.0)
        left = jnp.where(table[0] == 1, eye, block(table[HEAD + j], 0))
        right = jnp.where(table[1] == 1, eye, block(table[HEAD + total + j], 1))
        left_out[j] = split_left(left)
        right_out[j] = split_right(right)
        back_out[j, 0] = jnp.transpose(left)
        back_out[j, 1] = jnp.transpose(right)
    for i in range(own):
        mine_out[i] = states[0, i] / norm
    for j in range(total):
        middle = inward(vec_out[j], left_out[j], right_out[j])
        middle_out[j] = split_right(middle)
        plain_out[j] = middle


def first_kernel(
    begin, flags, bond, got0, got1, sent0, sent1, middle, vec, back, diagonal,
    env_out, mixed_out, part_out,
):
    size = vec.shape[-1]
    terms = bond.shape[0]
    flag = lambda k: jnp.broadcast_to(flags[k, 0:1] != 0, (size, size))
    first, last, swap = flag(0), flag(1), flag(2)
    rows = lambda s, m: slice((s * terms + m) * size, (s * terms + m + 1) * size)

    def chosen(at, end, sent_a, sent_b, got_a, got_b):
        there = jnp.where(swap, got_b[at], got_a[at])
        return jnp.where(end, jnp.where(swap, sent_b[at], sent_a[at]), there)

    def weighted(m, k, block):
        tiles = block.reshape(size // 8, 8, size)
        return (tiles * bond[m, k][None]).reshape(size, size)

    for s in range(part_out.shape[0]):
        for m in range(terms):
            block = chosen(rows(s, m), first, sent1, sent0, got0, got1)
            env_out[s, rows(0, m)] = split_left(block)
        blocks = [chosen(rows(s, m), last, sent0, sent1, got1, got0) for m in range(terms)]
        for m in range(terms):
            total = weighted(m, 0, blocks[0])
            for k in range(1, terms):
                total = total + weighted(m, k, blocks[k])
            mixed_out[s, rows(0, m)] = split_left(total)
        j = begin + s
        core = core_of(env_out[s], mixed_out[s], middle[j], terms)
        part = product(product(back[j, 0], core), back[j, 1])
        part_out[s] = part + diagonal[j] * vec[j]


def early_kernel(
    begin, image, part, vec, middle, left, right, diagonal, env, mixed,
    resid_out, stat_out, moved, cores,
):
    width, size = image.shape[0], image.shape[1]
    terms = mixed.shape[1] // size
    zero = jnp.zeros((size, size), jnp.float32)
    tile = lambda value: jnp.full((8, 128), value, jnp.float32)

    along, norm = zero, zero
    for i in range(width):
        along = along + vec[begin + i] * image[i]
        norm = norm + vec[begin + i] * vec[begin + i]
    along, norm = jnp.sum(along), jnp.sum(norm)
    guess = jnp.where(norm > 0, along / jnp.where(norm > 0, norm, 1.0), 0.0)
    left_over, square = zero, zero
    for i in range(width):
        resid = image[i] - guess * vec[begin + i]
        resid_out[i] = resid
        left_over = left_over + resid * vec[begin + i]
        square = square + resid * resid
    square = tile(jnp.sum(square))
    length = jnp.sqrt(square + 1e-06)
    scale = (1.0 / length)[0:1]
    stat_out[0] = tile(guess)
    stat_out[1] = tile(norm)
    stat_out[2] = tile(jnp.sum(left_over))
    stat_out[3] = square
    stat_out[4] = length

    for i in range(width):
        resid = resid_out[i] * scale
        resid_out[i] = resid
        moved[i] = inward(resid, left[begin + i], right[begin + i])
    for i in range(width):
        cores[i] = core_of(env[i], mixed[i], split_right(moved[i]), terms)
    shares = lambda i: diagonal[begin + i]
    both = zero
    for i in range(width):
        resid = resid_out[i]
        both = both + moved[i] * cores[i] + (shares(i) * resid) * resid
    stat_out[5] = tile(jnp.sum(both))
    cross = zero
    for i in range(width):
        resid = resid_out[i]
        cross = cross + middle[begin + i] * cores[i]
        cross = cross + resid * (part[i] + shares(i) * vec[begin + i])
    stat_out[6] = tile(jnp.sum(cross))
    plain = zero
    for i in range(width):
        plain = plain + vec[begin + i] * part[i]
    stat_out[7] = tile(jnp.sum(plain))


def second_kernel(
    own, widths, flags, part0, part1, vec, left, right, diagonal, env, mixed, *refs
):
    count = len(widths)
    resids, stats = refs[:count], refs[count : 2 * count]
    second_out, share_out, work = refs[2 * count :]
    total, size, late = vec.shape[0], vec.shape[1], part0.shape[0]
    early = total - late
    terms = mixed.shape[1] // size
    zero = jnp.zeros((size, size), jnp.float32)
    tile = lambda value: jnp.full((8, 128), value, jnp.float32)

    images = [part0[i] + part1[i] for i in range(late)]
    along = zero
    for i in range(late):
        along = along + vec[early + i] * images[i]
    alpha1 = tile(jnp.sum(along))
    for stat in stats:
        alpha1 = alpha1 + (stat[0] * stat[1] + stat[2])
    rest = zero
    for i in range(late):
        images[i] = images[i] - alpha1[0:1] * vec[early + i]
        rest = rest + images[i] * images[i]
    square = tile(jnp.sum(rest)) + 1e-06
    for stat in stats:
        away = alpha1 - stat[0]
        square = square + jnp.maximum(
            stat[3] - 2.0 * away * stat[2] + away * (away * stat[1]), 0.0
        )
    beta = jnp.sqrt(square)
    scale = (1.0 / beta)[0:1]
    share = zero
    for i in range(late):
        j = early + i
        value = images[i] * scale
        work[j] = value
        moved = inward(value, left[j], right[j])
        core = core_of(env[i], mixed[i], split_right(moved), terms)
        share = share + moved * core + (diagonal[j] * value) * value
    begin = 0
    sums = zero[:8]
    for resid, stat, width in zip(resids, stats, widths):
        long, off = stat[4] / beta, (alpha1 - stat[0]) / beta
        sums = sums + long * (long * stat[5]) - off * (long * stat[6]) + off * (off * stat[7])
        for i in range(width):
            work[begin + i] = long[0:1] * resid[i] - off[0:1] * vec[begin + i]
        begin += width
    share_out[0] = tile(jnp.sum(share)) + sums
    share_out[1] = alpha1
    share_out[2] = beta
    for i in range(own):
        mine = work[i]
        for g in range(1, total // own):
            mine = jnp.where(flags[3 + g, 0:1] != 0, work[g * own + i], mine)
        second_out[i] = mine


def final_kernel(count, share0, share1, share2, share3, mine, second, out, energy_out):
    alpha2 = (share0[0] + share1[0]) + (share2[0] + share3[0])
    alpha1, beta = share0[1], share0[2]
    energy = (alpha1 + alpha2) / 2.0 - jnp.sqrt(((alpha1 - alpha2) / 2.0) ** 2 + beta * beta)
    height = jnp.sqrt(beta * beta + (energy - alpha1) ** 2)
    scale = math.sqrt(count)
    weight1 = (scale * (beta / height))[0:1]
    weight2 = (scale * ((energy - alpha1) / height))[0:1]
    for i in range(out.shape[0]):
        out[i] = weight1 * mine[i] + weight2 * second[i]
    energy_out[0] = energy[0, 0]


def on_device(
    state, left_tensor, right_tensor, onsite, left_env, right_env, mpo_bond, sectors, flow
):
    position = lax.axis_index("sites")
    parts = lax.axis_size("sites") // GROUP
    own, size = state.shape[0], state.shape[1]
    terms, total = left_env.shape[0], left_env.shape[1]
    f32, bf16 = jnp.float32, jnp.bfloat16
    begins = [sum(CHUNKS[:c]) for c in range(len(CHUNKS))]

    smem = pl.BlockSpec(memory_space=pltpu.SMEM)
    vmem = pl.BlockSpec(memory_space=pltpu.VMEM)
    hbm = pl.BlockSpec(memory_space=pltpu.HBM)
    shape = jax.ShapeDtypeStruct
    dma = pltpu.SemaphoreType.DMA
    params = lambda mib: pltpu.CompilerParams(vmem_limit_bytes=mib * MIB)

    small_cost = pl.CostEstimate(flops=1, bytes_accessed=1, transcendentals=0)

    rows = lambda width: width * terms * size
    chunk = lambda c: (rows(CHUNKS[c]) + (own * size + terms if c == 0 else 0), size)
    chunks = lambda some: [pltpu.VMEM(chunk(c), f32) for c in some for _ in range(2)]
    in_hbm = lambda *values: [
        pltpu.with_memory_space_constraint(value, pltpu.HBM) for value in values
    ]
    table, *opened = pl.pallas_call(
        functools.partial(open_kernel, CHUNKS[:1], parts),
        in_specs=[hbm] * 8,
        out_specs=[smem] + [vmem] * 2,
        out_shape=[shape((HEAD + 5 * total + 2,), jnp.int32)] + chunks([0]),
        scratch_shapes=[
            pltpu.SMEM((1,), jnp.int32),
            pltpu.SMEM(sectors.shape, jnp.int32),
            pltpu.SMEM(flow.shape, jnp.int32),
            pltpu.SMEM((3 * total,), jnp.int32),
            pltpu.VMEM(mpo_bond.shape, f32),
            pltpu.VMEM((terms, size), f32),
            dma((2, total)),
            dma((2, own + 1)),
            dma((4,)),
        ],
        cost_estimate=small_cost,
        compiler_params=params(16),
        name="open",
    )(
        *in_hbm(
            jnp.reshape(position, (1,)).astype(jnp.int32), sectors, flow, mpo_bond,
            left_tensor, right_tensor, left_env, right_env,
        )
    )
    later = range(1, len(CHUNKS))
    opened += pl.pallas_call(
        functools.partial(pick_kernel, CHUNKS[0], CHUNKS[1:]),
        in_specs=[smem] + [hbm] * 2,
        out_specs=[vmem] * (2 * len(later)),
        out_shape=chunks(later),
        scratch_shapes=[dma((2, total))],
        cost_estimate=small_cost,
        compiler_params=params(16),
        name="pick",
    )(table, *in_hbm(left_env, right_env))
    sent = [tuple(opened[2 * c : 2 * c + 2]) for c in range(len(CHUNKS))]
    states = gather(state)
    sent[1], _ = lax.optimization_barrier((sent[1], states))
    got = [tuple(hand_over(block, side) for side, block in enumerate(pair)) for pair in sent]

    tail = [block[rows(CHUNKS[0]) :] for block in got[0]]
    swap = table[3] == 1
    from_left, from_right = jnp.where(swap, tail[1], tail[0]), jnp.where(swap, tail[0], tail[1])
    small = jnp.eye(terms, dtype=f32)
    bond_left = jnp.where(table[0] == 1, small, from_left[own * size :, : mpo_bond.shape[1]])
    bond_right = jnp.where(table[1] == 1, small, from_right[own * size :, : mpo_bond.shape[1]])
    bond = jnp.sum(bond_left[:, None, :] * bond_right[None, :, :], axis=2)
    bond = jnp.broadcast_to(bond[:, :, None, None], (terms, terms, 8, size))
    flags = jnp.concatenate(
        [table[0:2], table[3:4], (table[2] == jnp.arange(GROUP)).astype(jnp.int32)]
    )
    flags = jnp.broadcast_to(flags[:, None, None], (3 + GROUP, 8, size))
    tensors = lambda block: block[: own * size].reshape(own, size, size)
    pieces = gather(jnp.stack([tensors(from_left), tensors(from_right)], 1))

    vec, middle, plain, left, right, back, diagonal, mine = pl.pallas_call(
        functools.partial(prepare_kernel, own),
        in_specs=[smem] + [vmem] * 3,
        out_specs=[vmem] * 8,
        out_shape=[
            shape((total, size, size), f32),
            shape((total, 2 * size, 2 * size), bf16),
            shape((total, size, size), f32),
            shape((total, size, 2 * size), bf16),
            shape((total, 2 * size, 2 * size), bf16),
            shape((total, 2, size, size), f32),
            shape((total, size, size), f32),
            shape((own, size, size), f32),
        ],
        cost_estimate=small_cost,
        compiler_params=params(12),
        name="prepare",
    )(table, states, pieces, onsite)

    def early(begin, width, image, part, env, mixed, after):
        image, _ = lax.optimization_barrier((image, after))
        return pl.pallas_call(
            functools.partial(early_kernel, begin),
            in_specs=[vmem] * 9,
            out_specs=[vmem] * 2,
            out_shape=[shape((width, size, size), f32), shape((8, 8, 128), f32)],
            scratch_shapes=[pltpu.VMEM((width, size, size), f32)] * 2,
            cost_estimate=small_cost,
            compiler_params=params(12),
            name="early_second_matvec",
        )(image, part, vec, plain, left, right, diagonal, env, mixed)

    resids, stats, waits, held = [], [], [], None
    for c, (begin, width) in enumerate(zip(begins, CHUNKS)):
        if c > 0:
            got[c], _ = lax.optimization_barrier((got[c], waits[c - 1]))
        env, mixed, part = pl.pallas_call(
            functools.partial(first_kernel, begin),
            in_specs=[vmem] * 10,
            out_specs=[vmem] * 3,
            out_shape=[
                shape((width, rows(1), 2 * size), bf16),
                shape((width, rows(1), 2 * size), bf16),
                shape((width, size, size), f32),
            ],
            cost_estimate=small_cost,
        compiler_params=params(12),
            name=f"first_matvec{c}",
        )(flags, bond, *got[c], *sent[c], middle, vec, back, diagonal)
        if held is not None:
            resid, stat = early(*held, after=part)
            resids.append(resid)
            stats.append(stat)
        if c < len(CHUNKS) - 1:
            beside = part + partner(part, 1)
            image = beside + partner(beside, 2)
            held = (begin, width, image, part, env, mixed)
            waits.append([beside if c == len(CHUNKS) - 2 else image] + stats[-1:])

    beside = part + partner(part, 1)
    parts = [beside, partner(beside, 2)]
    second, share = pl.pallas_call(
        functools.partial(second_kernel, own, CHUNKS[:-1]),
        in_specs=[vmem] * (9 + 2 * (len(CHUNKS) - 1)),
        out_specs=[vmem] * 2,
        out_shape=[shape((own, size, size), f32), shape((3, 8, 128), f32)],
        scratch_shapes=[pltpu.VMEM((total, size, size), f32)],
        cost_estimate=small_cost,
        compiler_params=params(12),
        name="second_matvec",
    )(flags, *parts, vec, left, right, diagonal, env, mixed, *resids, *stats)

    shares = [share] + [partner(share[:1], mask) for mask in (1, 2, 3)]
    new_state, energy = pl.pallas_call(
        functools.partial(final_kernel, total * size * size),
        in_specs=[vmem] * 6,
        out_specs=[vmem, smem],
        out_shape=[shape((own, size, size), f32), shape((1,), f32)],
        cost_estimate=small_cost,
        compiler_params=params(4),
        name="ritz_update",
    )(*shares, mine, second)
    return (new_state, energy)


def solution(mesh):
    return jax.shard_map(
        on_device,
        mesh=mesh,
        in_specs=(
            P(("groups", "sites"), None, None),
            P(("groups", "sites"), None, None),
            P(("groups", "sites"), None, None),
            P(("groups", "sites"), None, None),
            P(("groups", "sites"), None, None, None),
            P(("groups", "sites"), None, None, None),
            P(("groups", "sites"), None),
            P("groups", None),
            P("groups", None),
        ),
        out_specs=(P(("groups", "sites"), None, None), P(("groups", "sites"))),
        check_vma=False,
    )
```

```python
import functools
import math

import jax
import jax.numpy as jnp
from jax import lax
from jax.experimental import pallas as pl
from jax.experimental.pallas import tpu as pltpu
from jax.sharding import PartitionSpec as P

GROUP = 4
CHUNKS = (2, 3, 2, 1)
MIB = 1024 * 1024


def hand_over(block, parity):
    count = lax.axis_size("sites")
    route = [(i, i + (GROUP if i % 2 == parity else -GROUP)) for i in range(count)]
    return lax.ppermute(block, "sites", [(i, j) for i, j in route if 0 <= j < count])


def partner(block, mask):
    route = [(i, i ^ mask) for i in range(lax.axis_size("sites"))]
    return lax.ppermute(block, "sites", route)


def gather(block):
    pieces = [block] + [partner(block, mask) for mask in (1, 2, 3)]
    return jnp.stack(pieces, 0)


def total_of(block):
    pair = block + partner(block, 1)
    return pair + partner(pair, 2)


def halves(value):
    high = value.astype(jnp.bfloat16)
    return high, (value - high.astype(jnp.float32)).astype(jnp.bfloat16)


def split_left(value):
    return jnp.concatenate(halves(value), axis=1)


def split_right(value):
    high, low = halves(value)
    return jnp.concatenate(
        [
            jnp.concatenate([high, low], axis=1),
            jnp.concatenate([high, jnp.zeros_like(low)], axis=1),
        ],
        axis=0,
    )


def fold(wide):
    half = wide.shape[1] // 2
    return wide[:, :half] + wide[:, half:]


def product(left, right):
    return fold(jnp.dot(split_left(left), split_right(right), preferred_element_type=jnp.float32))


def inward(block, left, right):
    temp = fold(jnp.dot(left, split_right(block), preferred_element_type=jnp.float32))
    return fold(jnp.dot(split_left(temp), right, preferred_element_type=jnp.float32))


def core_of(env_split, mixed_split, middle_split, terms):
    size = mixed_split.shape[0] // terms
    temp = fold(jnp.dot(env_split, middle_split, preferred_element_type=jnp.float32))
    high, low = halves(temp)
    wide = lambda part: jnp.concatenate(
        [part[m * size : (m + 1) * size] for m in range(terms)], axis=1
    )
    out = jnp.dot(
        jnp.concatenate([wide(high), wide(low)], axis=0),
        mixed_split,
        preferred_element_type=jnp.float32,
    )
    return fold(out[:size]) + out[size:, :size]


HEAD = 4


def sector_copy(env, index, out, row, sem):
    terms, _, size, _ = env.shape
    target = out.at[pl.ds(row, terms * size)].reshape(terms, size, size)
    return pltpu.make_async_copy(env.at[:, index], target, sem)


def ends(parts):
    position = lax.axis_index("sites")
    partition = position // GROUP
    return partition, partition == 0, partition == parts - 1, position % 2 == 1


def open_kernel(
    width, parts, bond_hbm, left_tensor, right_tensor, left_env, right_env, out0, out1,
    bond, sems, more, some,
):
    own, size = left_tensor.shape[0], left_tensor.shape[1]
    terms = left_env.shape[0]
    base = width * terms * size
    _, first, last, swap = ends(parts)
    load = pltpu.make_async_copy(bond_hbm, bond, some.at[0])
    ahead, behind = jnp.logical_not(last), first
    copies = []

    def start(flag, one, other):
        pl.when(flag)(one.start)
        pl.when(jnp.logical_not(flag))(other.start)
        copies.append(one)

    for side, out in enumerate((out0, out1)):
        crossed = swap if side == 0 else jnp.logical_not(swap)
        from_left = jnp.logical_or(
            jnp.logical_and(jnp.logical_not(crossed), ahead), jnp.logical_and(crossed, behind)
        )
        for i in range(width):
            place = (i, out, i * terms * size, sems.at[side, i])
            start(from_left, sector_copy(left_env, *place), sector_copy(right_env, *place))
        for i in range(own):
            target = out.at[pl.ds(base + i * size, size)]
            start(
                jnp.logical_not(crossed),
                pltpu.make_async_copy(left_tensor.at[i], target, more.at[side, i]),
                pltpu.make_async_copy(right_tensor.at[i], target, more.at[side, i]),
            )
    load.start()
    load.wait()
    for out in (out0, out1):
        rows = slice(base + own * size, base + own * size + terms)
        out[rows] = jnp.zeros((terms, size), jnp.float32)
        out[rows, : bond.shape[1]] = bond[...]
    for copy in copies:
        copy.wait()


def pick_kernel(
    chunks, parts, sectors_hbm, flow_hbm, left_env, right_env, table, *refs
):
    outs, (sectors, flow, turned, lists, sems, some) = refs[:-6], refs[-6:]
    terms, total, size = left_env.shape[:3]
    width = chunks[0]
    paired = width + chunks[1]
    partition, first, last, swap = ends(parts)
    loads = [
        pltpu.make_async_copy(sectors_hbm, sectors, some.at[0]),
        pltpu.make_async_copy(flow_hbm, flow, some.at[1]),
    ]
    for copy in loads:
        copy.start()
    for copy in loads:
        copy.wait()
    as_int = lambda flag: flag.astype(jnp.int32)
    table[0] = as_int(first)
    table[1] = as_int(last)
    table[2] = lax.axis_index("sites") % GROUP
    table[3] = as_int(swap)
    step = total + 1

    def orders(which, index):
        index = jnp.clip(index, 0, parts - 1)
        base = which * 7 * step
        before, after = jnp.maximum(index - 1, 0), jnp.minimum(index + 1, parts - 1)
        for j in range(total):
            turned[flow[before, j]] = j
            turned[total + flow[after, j]] = j
        lefts, rights = [], []
        for t in range(total):
            joined = sectors[index, t]
            lefts.append(jnp.where(index == 0, t, turned[t]))
            rights.append(jnp.where(index == parts - 1, joined, turned[total + joined]))
        count = jnp.int32(0)
        known = [jnp.logical_or(a < width, b < width) for a, b in zip(lefts, rights)]
        for wanted in (True, False):
            for t in range(total):
                lists[base + count] = lefts[t]
                lists[base + step + count] = rights[t]
                lists[base + 2 * step + count] = t
                count = count + as_int(known[t] if wanted else jnp.logical_not(known[t]))
        for side in range(2):
            count = jnp.int32(width)
            for i in range(width):
                lists[base + (3 + side) * step + i] = i
            for i in range(paired):
                source = lists[base + side * step + i]
                lists[base + (3 + side) * step + count] = source
                late = source >= width
                lists[base + (5 + side) * step + i] = jnp.where(late, count, source)
                count = count + as_int(late)
            for i in range(paired, total):
                lists[base + (3 + side) * step + i] = lists[base + side * step + i]
        return base

    behind_base = orders(0, partition - 1)
    here = orders(1, partition)
    ahead_base = orders(2, partition + 1)
    for i in range(total):
        for row, source in ((0, 0), (1, 1), (2, 2), (5, 5), (6, 6)):
            table[HEAD + row * total + i] = lists[here + source * step + i]
        ahead = jnp.where(last, lists[here + 4 * step + i], lists[ahead_base + 3 * step + i])
        behind = jnp.where(first, lists[here + 3 * step + i], lists[behind_base + 4 * step + i])
        table[HEAD + 3 * total + i] = jnp.where(swap, behind, ahead)
        table[HEAD + 4 * total + i] = jnp.where(swap, ahead, behind)
    ahead, behind = last.astype(jnp.int32), 1 - first.astype(jnp.int32)
    copies = []
    begin = width
    for c, count in enumerate(chunks[1:]):
        for side in range(2):
            kinds = (ahead, behind) if side == 0 else (behind, ahead)
            from_left = jnp.where(swap, kinds[1], kinds[0]) == 0
            for i in range(count):
                place = (
                    table[HEAD + (3 + side) * total + begin + i], outs[2 * c + side],
                    i * terms * size, sems.at[side, begin + i],
                )
                left, right = sector_copy(left_env, *place), sector_copy(right_env, *place)
                pl.when(from_left)(left.start)
                pl.when(jnp.logical_not(from_left))(right.start)
                copies.append(left)
        begin += count
    for copy in copies:
        copy.wait()


def prepare_kernel(
    own, table, states, pieces, onsite, vec_out, plain_out, left_out, right_out,
    back_out, diagonal_out, mine_out,
):
    total, size = vec_out.shape[0], vec_out.shape[1]
    row = lax.broadcasted_iota(jnp.int32, (size, size), 0)
    col = lax.broadcasted_iota(jnp.int32, (size, size), 1)
    eye = (row == col).astype(jnp.float32)
    member = table[2]

    def block(sector, kind):
        return pieces[(sector // own) ^ member, sector % own, kind]

    square = jnp.zeros((size, size), jnp.float32)
    for j in range(total):
        value = states[(j // own) ^ member, j % own]
        square = square + value * value
    norm = jnp.sqrt(jnp.full((8, size), jnp.sum(square), jnp.float32))[0:1]

    for j in range(total):
        target = table[HEAD + 2 * total + j]
        vec_out[j] = states[(target // own) ^ member, target % own] / norm
        diagonal_out[j] = jnp.where(target // own == member, onsite[target % own], 0.0)
        left = jnp.where(table[0] == 1, eye, block(table[HEAD + j], 0))
        right = jnp.where(table[1] == 1, eye, block(table[HEAD + total + j], 1))
        left_out[j] = split_left(left)
        right_out[j] = split_right(right)
        back_out[j, 0] = jnp.transpose(left)
        back_out[j, 1] = jnp.transpose(right)
    for i in range(own):
        mine_out[i] = states[0, i] / norm
    for j in range(total):
        plain_out[j] = inward(vec_out[j], left_out[j], right_out[j])


def chooser(flags, got0, got1, sent0, sent1, terms, size):
    flag = lambda k: jnp.broadcast_to(flags[k, 0:1] != 0, (size, size))
    first, last, swap = flag(0), flag(1), flag(2)

    def chosen(s, m, end, sent_a, sent_b, got_a, got_b):
        at = slice((s * terms + m) * size, (s * terms + m + 1) * size)
        there = jnp.where(swap, got_b[at], got_a[at])
        return jnp.where(end, jnp.where(swap, sent_b[at], sent_a[at]), there)

    left_of = lambda s, m: chosen(s, m, first, sent1, sent0, got0, got1)
    right_of = lambda s, m: chosen(s, m, last, sent0, sent1, got1, got0)
    return left_of, right_of


def spread(s, slot, bond, env_out, mixed_out, left_of, right_of):
    terms, size = bond.shape[0], bond.shape[-1]

    def weighted(m, k, block):
        tiles = block.reshape(size // 8, 8, size)
        return (tiles * bond[m, k][None]).reshape(size, size)

    rows = lambda m: slice(m * size, (m + 1) * size)
    for m in range(terms):
        env_out[slot, rows(m)] = split_left(left_of(s, m))
    blocks = [right_of(s, m) for m in range(terms)]
    for m in range(terms):
        total = weighted(m, 0, blocks[0])
        for k in range(1, terms):
            total = total + weighted(m, k, blocks[k])
        mixed_out[slot, rows(m)] = split_left(total)


def image_of(j, env, mixed, terms, plain, vec, back, diagonal):
    core = core_of(env, mixed, split_right(plain[j]), terms)
    return product(product(back[j, 0], core), back[j, 1]) + diagonal[j] * vec[j]


def either(before, after, slot):
    count = before.shape[0]
    late = slot >= count
    return jnp.where(
        late, after[jnp.maximum(slot - count, 0)], before[jnp.minimum(slot, count - 1)]
    )


def split_kernel(flags, bond, got0, got1, sent0, sent1, env_out, mixed_out):
    terms, size = bond.shape[0], bond.shape[-1]
    left_of, right_of = chooser(flags, got0, got1, sent0, sent1, terms, size)
    for s in range(env_out.shape[0]):
        spread(s, s, bond, env_out, mixed_out, left_of, right_of)


def first_kernel(
    begin, flags, bond, got0, got1, sent0, sent1, plain, vec, back, diagonal,
    env_out, mixed_out, part_out,
):
    terms, size = bond.shape[0], bond.shape[-1]
    left_of, right_of = chooser(flags, got0, got1, sent0, sent1, terms, size)
    for s in range(part_out.shape[0]):
        spread(s, s, bond, env_out, mixed_out, left_of, right_of)
        part_out[s] = image_of(
            begin + s, env_out[s], mixed_out[s], terms, plain, vec, back, diagonal
        )


def paired_kernel(
    slots, flags, bond, got0, got1, sent0, sent1, env_before, mixed_before,
    plain, vec, back, diagonal, env_out, mixed_out, part_out,
):
    terms, size = bond.shape[0], bond.shape[-1]
    total = vec.shape[0]
    left_of, right_of = chooser(flags, got0, got1, sent0, sent1, terms, size)
    for s in range(env_out.shape[0]):
        spread(s, s, bond, env_out, mixed_out, left_of, right_of)
    for j in range(part_out.shape[0]):
        env = either(env_before, env_out, slots[j])
        mixed = either(mixed_before, mixed_out, slots[total + j])
        part_out[j] = image_of(j, env, mixed, terms, plain, vec, back, diagonal)


def early_kernel(
    begin, slots, image, part, vec, middle, left, right, diagonal, env, mixed, *refs
):
    before, (resid_out, stat_out, moved, cores) = refs[:-4], refs[-4:]
    width, size = image.shape[0], image.shape[1]
    terms = mixed.shape[1] // size
    zero = jnp.zeros((size, size), jnp.float32)
    tile = lambda value: jnp.full((8, 128), value, jnp.float32)

    along, norm = zero, zero
    for i in range(width):
        along = along + vec[begin + i] * image[i]
        norm = norm + vec[begin + i] * vec[begin + i]
    along, norm = jnp.sum(along), jnp.sum(norm)
    guess = jnp.where(norm > 0, along / jnp.where(norm > 0, norm, 1.0), 0.0)
    left_over, square = zero, zero
    for i in range(width):
        resid = image[i] - guess * vec[begin + i]
        resid_out[i] = resid
        left_over = left_over + resid * vec[begin + i]
        square = square + resid * resid
    square = tile(jnp.sum(square))
    length = jnp.sqrt(square + 1e-06)
    scale = (1.0 / length)[0:1]
    stat_out[0] = tile(guess)
    stat_out[1] = tile(norm)
    stat_out[2] = tile(jnp.sum(left_over))
    stat_out[3] = square
    stat_out[4] = length

    for i in range(width):
        resid = resid_out[i] * scale
        resid_out[i] = resid
        moved[i] = inward(resid, left[begin + i], right[begin + i])
    for i in range(width):
        if slots is None:
            sides = env[i], mixed[i]
        else:
            sides = (
                either(before[0], env, slots[i]),
                either(before[1], mixed, slots[vec.shape[0] + i]),
            )
        cores[i] = core_of(*sides, split_right(moved[i]), terms)
    shares = lambda i: diagonal[begin + i]
    both = zero
    for i in range(width):
        resid = resid_out[i]
        both = both + moved[i] * cores[i] + (shares(i) * resid) * resid
    stat_out[5] = tile(jnp.sum(both))
    cross = zero
    for i in range(width):
        resid = resid_out[i]
        cross = cross + middle[begin + i] * cores[i]
        cross = cross + resid * (part[i] + shares(i) * vec[begin + i])
    stat_out[6] = tile(jnp.sum(cross))
    plain = zero
    for i in range(width):
        plain = plain + vec[begin + i] * part[i]
    stat_out[7] = tile(jnp.sum(plain))


def second_kernel(
    own, widths, flags, part0, part1, vec, left, right, diagonal, env, mixed, *refs
):
    count = len(widths)
    resids, stats = refs[:count], refs[count : 2 * count]
    second_out, share_out, work = refs[2 * count :]
    total, size, late = vec.shape[0], vec.shape[1], part0.shape[0]
    early = total - late
    terms = mixed.shape[1] // size
    zero = jnp.zeros((size, size), jnp.float32)
    tile = lambda value: jnp.full((8, 128), value, jnp.float32)

    images = [part0[i] + part1[i] for i in range(late)]
    along = zero
    for i in range(late):
        along = along + vec[early + i] * images[i]
    alpha1 = tile(jnp.sum(along))
    for stat in stats:
        alpha1 = alpha1 + (stat[0] * stat[1] + stat[2])
    rest = zero
    for i in range(late):
        images[i] = images[i] - alpha1[0:1] * vec[early + i]
        rest = rest + images[i] * images[i]
    square = tile(jnp.sum(rest)) + 1e-06
    for stat in stats:
        away = alpha1 - stat[0]
        square = square + jnp.maximum(
            stat[3] - 2.0 * away * stat[2] + away * (away * stat[1]), 0.0
        )
    beta = jnp.sqrt(square)
    scale = (1.0 / beta)[0:1]
    share = zero
    for i in range(late):
        j = early + i
        value = images[i] * scale
        work[j] = value
        moved = inward(value, left[j], right[j])
        core = core_of(env[i], mixed[i], split_right(moved), terms)
        share = share + moved * core + (diagonal[j] * value) * value
    begin = 0
    sums = zero[:8]
    for resid, stat, width in zip(resids, stats, widths):
        long, off = stat[4] / beta, (alpha1 - stat[0]) / beta
        sums = sums + long * (long * stat[5]) - off * (long * stat[6]) + off * (off * stat[7])
        for i in range(width):
            work[begin + i] = long[0:1] * resid[i] - off[0:1] * vec[begin + i]
        begin += width
    share_out[0] = tile(jnp.sum(share)) + sums
    share_out[1] = alpha1
    share_out[2] = beta
    for i in range(own):
        mine = work[0]
        for j in range(1, total):
            mine = jnp.where(flags[3 + i * total + j, 0:1] != 0, work[j], mine)
        second_out[i] = mine


def final_kernel(count, share0, share1, share2, share3, mine, second, out, energy_out):
    alpha2 = (share0[0] + share1[0]) + (share2[0] + share3[0])
    alpha1, beta = share0[1], share0[2]
    energy = (alpha1 + alpha2) / 2.0 - jnp.sqrt(((alpha1 - alpha2) / 2.0) ** 2 + beta * beta)
    height = jnp.sqrt(beta * beta + (energy - alpha1) ** 2)
    scale = math.sqrt(count)
    weight1 = (scale * (beta / height))[0:1]
    weight2 = (scale * ((energy - alpha1) / height))[0:1]
    for i in range(out.shape[0]):
        out[i] = weight1 * mine[i] + weight2 * second[i]
    energy_out[0] = energy[0, 0]


def on_device(
    state, left_tensor, right_tensor, onsite, left_env, right_env, mpo_bond, sectors, flow
):
    parts = lax.axis_size("sites") // GROUP
    own, size = state.shape[0], state.shape[1]
    terms, total = left_env.shape[0], left_env.shape[1]
    f32, bf16 = jnp.float32, jnp.bfloat16
    begins = [sum(CHUNKS[:c]) for c in range(len(CHUNKS))]

    smem = pl.BlockSpec(memory_space=pltpu.SMEM)
    vmem = pl.BlockSpec(memory_space=pltpu.VMEM)
    hbm = pl.BlockSpec(memory_space=pltpu.HBM)
    shape = jax.ShapeDtypeStruct
    dma = pltpu.SemaphoreType.DMA
    params = lambda mib: pltpu.CompilerParams(vmem_limit_bytes=mib * MIB)

    small_cost = pl.CostEstimate(flops=1, bytes_accessed=1, transcendentals=0)

    rows = lambda width: width * terms * size
    chunk = lambda c: (rows(CHUNKS[c]) + (own * size + terms if c == 0 else 0), size)
    chunks = lambda some: [pltpu.VMEM(chunk(c), f32) for c in some for _ in range(2)]
    in_hbm = lambda *values: [
        pltpu.with_memory_space_constraint(value, pltpu.HBM) for value in values
    ]
    opened = pl.pallas_call(
        functools.partial(open_kernel, CHUNKS[0], parts),
        in_specs=[hbm] * 5,
        out_specs=[vmem] * 2,
        out_shape=chunks([0]),
        scratch_shapes=[
            pltpu.VMEM(mpo_bond.shape, f32),
            dma((2, CHUNKS[0])),
            dma((2, own)),
            dma((1,)),
        ],
        cost_estimate=small_cost,
        compiler_params=params(4),
        name="open",
    )(*in_hbm(mpo_bond, left_tensor, right_tensor, left_env, right_env))
    later = range(1, len(CHUNKS))
    table, *picked = pl.pallas_call(
        functools.partial(pick_kernel, CHUNKS, parts),
        in_specs=[hbm] * 4,
        out_specs=[smem] + [vmem] * (2 * len(later)),
        out_shape=[shape((HEAD + 7 * total,), jnp.int32)] + chunks(later),
        scratch_shapes=[
            pltpu.SMEM(sectors.shape, jnp.int32),
            pltpu.SMEM(flow.shape, jnp.int32),
            pltpu.SMEM((2 * total,), jnp.int32),
            pltpu.SMEM((3 * 7 * (total + 1),), jnp.int32),
            dma((2, total)),
            dma((2,)),
        ],
        cost_estimate=small_cost,
        compiler_params=params(4),
        name="pick",
    )(*in_hbm(sectors, flow, left_env, right_env))
    opened = list(opened) + picked
    sent = [tuple(opened[2 * c : 2 * c + 2]) for c in range(len(CHUNKS))]
    states = gather(state)
    sent[1], _ = lax.optimization_barrier((sent[1], states))
    got = [tuple(hand_over(block, side) for side, block in enumerate(pair)) for pair in sent]

    tail = [block[rows(CHUNKS[0]) :] for block in got[0]]
    swap = table[3] == 1
    from_left, from_right = jnp.where(swap, tail[1], tail[0]), jnp.where(swap, tail[0], tail[1])
    small = jnp.eye(terms, dtype=f32)
    bond_left = jnp.where(table[0] == 1, small, from_left[own * size :, : mpo_bond.shape[1]])
    bond_right = jnp.where(table[1] == 1, small, from_right[own * size :, : mpo_bond.shape[1]])
    bond = jnp.sum(bond_left[:, None, :] * bond_right[None, :, :], axis=2)
    bond = jnp.broadcast_to(bond[:, :, None, None], (terms, terms, 8, size))
    flags = jnp.concatenate(
        [
            table[0:2],
            table[3:4],
            (
                table[HEAD + 2 * total : HEAD + 3 * total][None, :]
                == table[2] * own + jnp.arange(own, dtype=jnp.int32)[:, None]
            ).astype(jnp.int32).reshape(-1),
        ]
    )
    flags = jnp.broadcast_to(flags[:, None, None], (3 + own * total, 8, size))
    tensors = lambda block: block[: own * size].reshape(own, size, size)
    pieces = gather(jnp.stack([tensors(from_left), tensors(from_right)], 1))

    vec, plain, left, right, back, diagonal, mine = pl.pallas_call(
        functools.partial(prepare_kernel, own),
        in_specs=[smem] + [vmem] * 3,
        out_specs=[vmem] * 7,
        out_shape=[
            shape((total, size, size), f32),
            shape((total, size, size), f32),
            shape((total, size, 2 * size), bf16),
            shape((total, 2 * size, 2 * size), bf16),
            shape((total, 2, size, size), f32),
            shape((total, size, size), f32),
            shape((own, size, size), f32),
        ],
        cost_estimate=small_cost,
        compiler_params=params(12),
        name="prepare",
    )(table, states, pieces, onsite)

    def early(begin, width, image, part, env, mixed, after):
        image, _ = lax.optimization_barrier((image, after))
        return pl.pallas_call(
            functools.partial(early_kernel, begin) if begin == 0 else functools.partial(
                early_kernel, begin, None
            ),
            in_specs=([smem] + [vmem] * 2 if begin == 0 else []) + [vmem] * 9,
            out_specs=[vmem] * 2,
            out_shape=[shape((width, size, size), f32), shape((8, 8, 128), f32)],
            scratch_shapes=[pltpu.VMEM((width, size, size), f32)] * 2,
            cost_estimate=small_cost,
            compiler_params=params(12),
            name="early_second_matvec",
        )(*([slots] if begin == 0 else []), image, part, vec, plain, left, right, diagonal, env, mixed, *(before if begin == 0 else []))

    resids, stats, waits, held = [], [], [], None
    slots = table[HEAD + 5 * total : HEAD + 7 * total]
    groups = (CHUNKS[0] + CHUNKS[1],) + CHUNKS[2:]
    for c, (begin, width) in enumerate(zip([0] + begins[2:], groups)):
        if c > 0:
            got[c + 1], _ = lax.optimization_barrier((got[c + 1], waits[c - 1]))
            kernel, ahead = functools.partial(first_kernel, begin), [vmem] * 6
            operands = (flags, bond, *got[c + 1], *sent[c + 1])
        else:
            split = shape((CHUNKS[0], rows(1), 2 * size), bf16)
            kernel, ahead = paired_kernel, [smem] + [vmem] * 8
            before = pl.pallas_call(
                split_kernel,
                in_specs=[vmem] * 6,
                out_specs=[vmem] * 2,
                out_shape=[split, split],
                cost_estimate=small_cost,
                compiler_params=params(12),
                name="split",
            )(flags, bond, *got[0], *sent[0])
            operands = (slots, flags, bond, *got[1], *sent[1], *before)
        env, mixed, part = pl.pallas_call(
            kernel,
            in_specs=ahead + [vmem] * 4,
            out_specs=[vmem] * 3,
            out_shape=[
                shape((CHUNKS[c + 1], rows(1), 2 * size), bf16),
                shape((CHUNKS[c + 1], rows(1), 2 * size), bf16),
                shape((width, size, size), f32),
            ],
            cost_estimate=small_cost,
            compiler_params=params(12),
            name=f"first_matvec{c}",
        )(*operands, plain, vec, back, diagonal)
        if held is not None:
            resid, stat = early(*held, after=part)
            resids.append(resid)
            stats.append(stat)
        if c < len(groups) - 1:
            beside = part + partner(part, 1)
            image = beside + partner(beside, 2)
            held = (begin, width, image, part, env, mixed)
            waits.append([beside if c == len(groups) - 2 else image] + stats[-1:])

    beside = part + partner(part, 1)
    parts = [beside, partner(beside, 2)]
    second, share = pl.pallas_call(
        functools.partial(second_kernel, own, groups[:-1]),
        in_specs=[vmem] * (9 + 2 * (len(groups) - 1)),
        out_specs=[vmem] * 2,
        out_shape=[shape((own, size, size), f32), shape((3, 8, 128), f32)],
        scratch_shapes=[pltpu.VMEM((total, size, size), f32)],
        cost_estimate=small_cost,
        compiler_params=params(12),
        name="second_matvec",
    )(flags, *parts, vec, left, right, diagonal, env, mixed, *resids, *stats)

    shares = [share] + [partner(share[:1], mask) for mask in (1, 2, 3)]
    new_state, energy = pl.pallas_call(
        functools.partial(final_kernel, total * size * size),
        in_specs=[vmem] * 6,
        out_specs=[vmem, smem],
        out_shape=[shape((own, size, size), f32), shape((1,), f32)],
        cost_estimate=small_cost,
        compiler_params=params(4),
        name="ritz_update",
    )(*shares, mine, second)
    return (new_state, energy)


def solution(mesh):
    return jax.shard_map(
        on_device,
        mesh=mesh,
        in_specs=(
            P(("groups", "sites"), None, None),
            P(("groups", "sites"), None, None),
            P(("groups", "sites"), None, None),
            P(("groups", "sites"), None, None),
            P(("groups", "sites"), None, None, None),
            P(("groups", "sites"), None, None, None),
            P(("groups", "sites"), None),
            P("groups", None),
            P("groups", None),
        ),
        out_specs=(P(("groups", "sites"), None, None), P(("groups", "sites"))),
        check_vma=False,
    )
```

```python
import functools
import math

import jax
import jax.numpy as jnp
from jax import lax
from jax.experimental import pallas as pl
from jax.experimental.pallas import tpu as pltpu
from jax.sharding import PartitionSpec as P

GROUP = 4
CHUNKS = (2, 3, 2, 1)
MIB = 1024 * 1024


def hand_over(block, parity):
    count = lax.axis_size("sites")
    route = [(i, i + (GROUP if i % 2 == parity else -GROUP)) for i in range(count)]
    return lax.ppermute(block, "sites", [(i, j) for i, j in route if 0 <= j < count])


def partner(block, mask):
    route = [(i, i ^ mask) for i in range(lax.axis_size("sites"))]
    return lax.ppermute(block, "sites", route)


def gather(block):
    pieces = [block] + [partner(block, mask) for mask in (1, 2, 3)]
    return jnp.stack(pieces, 0)


def total_of(block):
    pair = block + partner(block, 1)
    return pair + partner(pair, 2)


def halves(value):
    high = value.astype(jnp.bfloat16)
    return high, (value - high.astype(jnp.float32)).astype(jnp.bfloat16)


def split_left(value):
    return jnp.concatenate(halves(value), axis=1)


def split_right(value):
    high, low = halves(value)
    return jnp.concatenate(
        [
            jnp.concatenate([high, low], axis=1),
            jnp.concatenate([high, jnp.zeros_like(low)], axis=1),
        ],
        axis=0,
    )


def fold(wide):
    half = wide.shape[1] // 2
    return wide[:, :half] + wide[:, half:]


def product(left, right):
    return fold(jnp.dot(split_left(left), split_right(right), preferred_element_type=jnp.float32))


def inward(block, left, right):
    temp = fold(jnp.dot(left, split_right(block), preferred_element_type=jnp.float32))
    return fold(jnp.dot(split_left(temp), right, preferred_element_type=jnp.float32))


def core_of(env_split, mixed_split, middle_split, terms):
    size = mixed_split.shape[0] // terms
    temp = fold(jnp.dot(env_split, middle_split, preferred_element_type=jnp.float32))
    high, low = halves(temp)
    wide = lambda part: jnp.concatenate(
        [part[m * size : (m + 1) * size] for m in range(terms)], axis=1
    )
    out = jnp.dot(
        jnp.concatenate([wide(high), wide(low)], axis=0),
        mixed_split,
        preferred_element_type=jnp.float32,
    )
    return fold(out[:size]) + out[size:, :size]


HEAD = 4


def sector_copy(env, index, out, row, sem):
    terms, _, size, _ = env.shape
    target = out.at[pl.ds(row, terms * size)].reshape(terms, size, size)
    return pltpu.make_async_copy(env.at[:, index], target, sem)


def ends(parts):
    position = lax.axis_index("sites")
    partition = position // GROUP
    return partition, partition == 0, partition == parts - 1, position % 2 == 1


def open_kernel(
    width, parts, bond_hbm, left_tensor, right_tensor, left_env, right_env, out0, out1,
    bond, sems, more, some,
):
    own, size = left_tensor.shape[0], left_tensor.shape[1]
    terms = left_env.shape[0]
    base = width * terms * size
    _, first, last, swap = ends(parts)
    load = pltpu.make_async_copy(bond_hbm, bond, some.at[0])
    ahead, behind = jnp.logical_not(last), first
    copies = []

    def start(flag, one, other):
        pl.when(flag)(one.start)
        pl.when(jnp.logical_not(flag))(other.start)
        copies.append(one)

    for side, out in enumerate((out0, out1)):
        crossed = swap if side == 0 else jnp.logical_not(swap)
        from_left = jnp.logical_or(
            jnp.logical_and(jnp.logical_not(crossed), ahead), jnp.logical_and(crossed, behind)
        )
        for i in range(width):
            place = (i, out, i * terms * size, sems.at[side, i])
            start(from_left, sector_copy(left_env, *place), sector_copy(right_env, *place))
        for i in range(own):
            target = out.at[pl.ds(base + i * size, size)]
            start(
                jnp.logical_not(crossed),
                pltpu.make_async_copy(left_tensor.at[i], target, more.at[side, i]),
                pltpu.make_async_copy(right_tensor.at[i], target, more.at[side, i]),
            )
    load.start()
    load.wait()
    for out in (out0, out1):
        rows = slice(base + own * size, base + own * size + terms)
        out[rows] = jnp.zeros((terms, size), jnp.float32)
        out[rows, : bond.shape[1]] = bond[...]
    for copy in copies:
        copy.wait()


def pick_kernel(
    chunks, parts, sectors_hbm, flow_hbm, left_env, right_env, table, *refs
):
    outs, (sectors, flow, turned, lists, sems, some) = refs[:-6], refs[-6:]
    terms, total, size = left_env.shape[:3]
    width = chunks[0]
    paired = width + chunks[1]
    partition, first, last, swap = ends(parts)
    loads = [
        pltpu.make_async_copy(sectors_hbm, sectors, some.at[0]),
        pltpu.make_async_copy(flow_hbm, flow, some.at[1]),
    ]
    for copy in loads:
        copy.start()
    for copy in loads:
        copy.wait()
    as_int = lambda flag: flag.astype(jnp.int32)
    table[0] = as_int(first)
    table[1] = as_int(last)
    table[2] = lax.axis_index("sites") % GROUP
    table[3] = as_int(swap)
    step = total + 1

    def orders(which, index):
        index = jnp.clip(index, 0, parts - 1)
        base = which * 7 * step
        before, after = jnp.maximum(index - 1, 0), jnp.minimum(index + 1, parts - 1)
        for j in range(total):
            turned[flow[before, j]] = j
            turned[total + flow[after, j]] = j
        lefts, rights = [], []
        for t in range(total):
            joined = sectors[index, t]
            lefts.append(jnp.where(index == 0, t, turned[t]))
            rights.append(jnp.where(index == parts - 1, joined, turned[total + joined]))
        count = jnp.int32(0)
        known = [jnp.logical_or(a < width, b < width) for a, b in zip(lefts, rights)]
        for wanted in (True, False):
            for t in range(total):
                lists[base + count] = lefts[t]
                lists[base + step + count] = rights[t]
                lists[base + 2 * step + count] = t
                count = count + as_int(known[t] if wanted else jnp.logical_not(known[t]))
        for side in range(2):
            count = jnp.int32(width)
            for i in range(width):
                lists[base + (3 + side) * step + i] = i
            for i in range(paired):
                source = lists[base + side * step + i]
                lists[base + (3 + side) * step + count] = source
                late = source >= width
                lists[base + (5 + side) * step + i] = jnp.where(late, count, source)
                count = count + as_int(late)
            for i in range(paired, total):
                lists[base + (3 + side) * step + i] = lists[base + side * step + i]
        return base

    behind_base = orders(0, partition - 1)
    here = orders(1, partition)
    ahead_base = orders(2, partition + 1)
    for i in range(total):
        for row, source in ((0, 0), (1, 1), (2, 2), (5, 5), (6, 6)):
            table[HEAD + row * total + i] = lists[here + source * step + i]
        ahead = jnp.where(last, lists[here + 4 * step + i], lists[ahead_base + 3 * step + i])
        behind = jnp.where(first, lists[here + 3 * step + i], lists[behind_base + 4 * step + i])
        table[HEAD + 3 * total + i] = jnp.where(swap, behind, ahead)
        table[HEAD + 4 * total + i] = jnp.where(swap, ahead, behind)
    ahead, behind = last.astype(jnp.int32), 1 - first.astype(jnp.int32)
    copies = []
    begin = width
    for c, count in enumerate(chunks[1:]):
        for side in range(2):
            kinds = (ahead, behind) if side == 0 else (behind, ahead)
            from_left = jnp.where(swap, kinds[1], kinds[0]) == 0
            for i in range(count):
                place = (
                    table[HEAD + (3 + side) * total + begin + i], outs[2 * c + side],
                    i * terms * size, sems.at[side, begin + i],
                )
                left, right = sector_copy(left_env, *place), sector_copy(right_env, *place)
                pl.when(from_left)(left.start)
                pl.when(jnp.logical_not(from_left))(right.start)
                copies.append(left)
        begin += count
    for copy in copies:
        copy.wait()


def prepare_kernel(
    own, table, states, pieces, onsite, vec_out, plain_out, left_out, right_out,
    back_out, diagonal_out, mine_out,
):
    total, size = vec_out.shape[0], vec_out.shape[1]
    row = lax.broadcasted_iota(jnp.int32, (size, size), 0)
    col = lax.broadcasted_iota(jnp.int32, (size, size), 1)
    eye = (row == col).astype(jnp.float32)
    member = table[2]

    def block(sector, kind):
        return pieces[(sector // own) ^ member, sector % own, kind]

    square = jnp.zeros((size, size), jnp.float32)
    for j in range(total):
        value = states[(j // own) ^ member, j % own]
        square = square + value * value
    norm = jnp.sqrt(jnp.full((8, size), jnp.sum(square), jnp.float32))[0:1]

    for j in range(total):
        target = table[HEAD + 2 * total + j]
        vec_out[j] = states[(target // own) ^ member, target % own] / norm
        diagonal_out[j] = jnp.where(target // own == member, onsite[target % own], 0.0)
        left = jnp.where(table[0] == 1, eye, block(table[HEAD + j], 0))
        right = jnp.where(table[1] == 1, eye, block(table[HEAD + total + j], 1))
        left_out[j] = split_left(left)
        right_out[j] = split_right(right)
        back_out[j, 0] = jnp.transpose(left)
        back_out[j, 1] = jnp.transpose(right)
    for i in range(own):
        mine_out[i] = states[0, i] / norm
    for j in range(total):
        plain_out[j] = inward(vec_out[j], left_out[j], right_out[j])


def chooser(flags, got0, got1, sent0, sent1, terms, size):
    flag = lambda k: jnp.broadcast_to(flags[k, 0:1] != 0, (size, size))
    first, last, swap = flag(0), flag(1), flag(2)

    def chosen(s, m, end, sent_a, sent_b, got_a, got_b):
        at = slice((s * terms + m) * size, (s * terms + m + 1) * size)
        there = jnp.where(swap, got_b[at], got_a[at])
        return jnp.where(end, jnp.where(swap, sent_b[at], sent_a[at]), there)

    left_of = lambda s, m: chosen(s, m, first, sent1, sent0, got0, got1)
    right_of = lambda s, m: chosen(s, m, last, sent0, sent1, got1, got0)
    return left_of, right_of


def spread(s, slot, bond, env_out, mixed_out, left_of, right_of):
    terms, size = bond.shape[0], bond.shape[-1]

    def weighted(m, k, block):
        tiles = block.reshape(size // 8, 8, size)
        return (tiles * bond[m, k][None]).reshape(size, size)

    rows = lambda m: slice(m * size, (m + 1) * size)
    for m in range(terms):
        env_out[slot, rows(m)] = split_left(left_of(s, m))
    blocks = [right_of(s, m) for m in range(terms)]
    for m in range(terms):
        total = weighted(m, 0, blocks[0])
        for k in range(1, terms):
            total = total + weighted(m, k, blocks[k])
        mixed_out[slot, rows(m)] = split_left(total)


def image_of(j, env, mixed, terms, plain, vec, back, diagonal):
    core = core_of(env, mixed, split_right(plain[j]), terms)
    return product(product(back[j, 0], core), back[j, 1]) + diagonal[j] * vec[j]


def either(before, after, slot):
    count = before.shape[0]
    late = slot >= count
    return jnp.where(
        late, after[jnp.maximum(slot - count, 0)], before[jnp.minimum(slot, count - 1)]
    )


def split_kernel(flags, bond, got0, got1, sent0, sent1, env_out, mixed_out):
    terms, size = bond.shape[0], bond.shape[-1]
    left_of, right_of = chooser(flags, got0, got1, sent0, sent1, terms, size)
    for s in range(env_out.shape[0]):
        spread(s, s, bond, env_out, mixed_out, left_of, right_of)


def first_kernel(
    begin, flags, bond, got0, got1, sent0, sent1, plain, vec, back, diagonal,
    env_out, mixed_out, part_out,
):
    terms, size = bond.shape[0], bond.shape[-1]
    left_of, right_of = chooser(flags, got0, got1, sent0, sent1, terms, size)
    for s in range(part_out.shape[0]):
        spread(s, s, bond, env_out, mixed_out, left_of, right_of)
        part_out[s] = image_of(
            begin + s, env_out[s], mixed_out[s], terms, plain, vec, back, diagonal
        )


def paired_kernel(
    slots, flags, bond, got0, got1, sent0, sent1, env_before, mixed_before,
    plain, vec, back, diagonal, env_out, mixed_out, part_out,
):
    terms, size = bond.shape[0], bond.shape[-1]
    total = vec.shape[0]
    left_of, right_of = chooser(flags, got0, got1, sent0, sent1, terms, size)
    for s in range(env_out.shape[0]):
        spread(s, s, bond, env_out, mixed_out, left_of, right_of)
    for j in range(part_out.shape[0]):
        env = either(env_before, env_out, slots[j])
        mixed = either(mixed_before, mixed_out, slots[total + j])
        part_out[j] = image_of(j, env, mixed, terms, plain, vec, back, diagonal)


def early_kernel(
    begin, slots, image, part, vec, middle, left, right, diagonal, env, mixed, *refs
):
    before, (resid_out, stat_out, moved, cores) = refs[:-4], refs[-4:]
    width, size = image.shape[0], image.shape[1]
    terms = mixed.shape[1] // size
    zero = jnp.zeros((size, size), jnp.float32)
    tile = lambda value: jnp.full((8, 128), value, jnp.float32)

    along, norm = zero, zero
    for i in range(width):
        along = along + vec[begin + i] * image[i]
        norm = norm + vec[begin + i] * vec[begin + i]
    along, norm = jnp.sum(along), jnp.sum(norm)
    guess = jnp.where(norm > 0, along / jnp.where(norm > 0, norm, 1.0), 0.0)
    left_over, square = zero, zero
    for i in range(width):
        resid = image[i] - guess * vec[begin + i]
        resid_out[i] = resid
        left_over = left_over + resid * vec[begin + i]
        square = square + resid * resid
    square = tile(jnp.sum(square))
    length = jnp.sqrt(square + 1e-06)
    scale = (1.0 / length)[0:1]
    stat_out[0] = tile(guess)
    stat_out[1] = tile(norm)
    stat_out[2] = tile(jnp.sum(left_over))
    stat_out[3] = square
    stat_out[4] = length

    for i in range(width):
        resid = resid_out[i] * scale
        resid_out[i] = resid
        moved[i] = inward(resid, left[begin + i], right[begin + i])
    for i in range(width):
        if slots is None:
            sides = env[i], mixed[i]
        else:
            sides = (
                either(before[0], env, slots[i]),
                either(before[1], mixed, slots[vec.shape[0] + i]),
            )
        cores[i] = core_of(*sides, split_right(moved[i]), terms)
    shares = lambda i: diagonal[begin + i]
    both = zero
    for i in range(width):
        resid = resid_out[i]
        both = both + moved[i] * cores[i] + (shares(i) * resid) * resid
    stat_out[5] = tile(jnp.sum(both))
    cross = zero
    for i in range(width):
        resid = resid_out[i]
        cross = cross + middle[begin + i] * cores[i]
        cross = cross + resid * (part[i] + shares(i) * vec[begin + i])
    stat_out[6] = tile(jnp.sum(cross))
    plain = zero
    for i in range(width):
        plain = plain + vec[begin + i] * part[i]
    stat_out[7] = tile(jnp.sum(plain))


def second_kernel(
    own, widths, flags, part0, part1, vec, left, right, diagonal, env, mixed, *refs
):
    count = len(widths)
    resids, stats = refs[:count], refs[count : 2 * count]
    second_out, share_out, work = refs[2 * count :]
    total, size, late = vec.shape[0], vec.shape[1], part0.shape[0]
    early = total - late
    terms = mixed.shape[1] // size
    zero = jnp.zeros((size, size), jnp.float32)
    tile = lambda value: jnp.full((8, 128), value, jnp.float32)

    images = [part0[i] + part1[i] for i in range(late)]
    along = zero
    for i in range(late):
        along = along + vec[early + i] * images[i]
    alpha1 = tile(jnp.sum(along))
    for stat in stats:
        alpha1 = alpha1 + (stat[0] * stat[1] + stat[2])
    rest = zero
    for i in range(late):
        images[i] = images[i] - alpha1[0:1] * vec[early + i]
        rest = rest + images[i] * images[i]
    square = tile(jnp.sum(rest)) + 1e-06
    for stat in stats:
        away = alpha1 - stat[0]
        square = square + jnp.maximum(
            stat[3] - 2.0 * away * stat[2] + away * (away * stat[1]), 0.0
        )
    beta = jnp.sqrt(square)
    scale = (1.0 / beta)[0:1]
    share = zero
    for i in range(late):
        j = early + i
        value = images[i] * scale
        work[j] = value
        moved = inward(value, left[j], right[j])
        core = core_of(env[i], mixed[i], split_right(moved), terms)
        share = share + moved * core + (diagonal[j] * value) * value
    begin = 0
    sums = zero[:8]
    for resid, stat, width in zip(resids, stats, widths):
        long, off = stat[4] / beta, (alpha1 - stat[0]) / beta
        sums = sums + long * (long * stat[5]) - off * (long * stat[6]) + off * (off * stat[7])
        for i in range(width):
            work[begin + i] = long[0:1] * resid[i] - off[0:1] * vec[begin + i]
        begin += width
    share_out[0] = tile(jnp.sum(share)) + sums
    share_out[1] = alpha1
    share_out[2] = beta
    for i in range(own):
        mine = work[0]
        for j in range(1, total):
            mine = jnp.where(flags[3 + i * total + j, 0:1] != 0, work[j], mine)
        second_out[i] = mine


def final_kernel(count, share0, share1, share2, share3, mine, second, out, energy_out):
    alpha2 = (share0[0] + share1[0]) + (share2[0] + share3[0])
    alpha1, beta = share0[1], share0[2]
    energy = (alpha1 + alpha2) / 2.0 - jnp.sqrt(((alpha1 - alpha2) / 2.0) ** 2 + beta * beta)
    height = jnp.sqrt(beta * beta + (energy - alpha1) ** 2)
    scale = math.sqrt(count)
    weight1 = (scale * (beta / height))[0:1]
    weight2 = (scale * ((energy - alpha1) / height))[0:1]
    for i in range(out.shape[0]):
        out[i] = weight1 * mine[i] + weight2 * second[i]
    energy_out[0] = energy[0, 0]


def on_device(
    state, left_tensor, right_tensor, onsite, left_env, right_env, mpo_bond, sectors, flow
):
    parts = lax.axis_size("sites") // GROUP
    own, size = state.shape[0], state.shape[1]
    terms, total = left_env.shape[0], left_env.shape[1]
    f32, bf16 = jnp.float32, jnp.bfloat16
    begins = [sum(CHUNKS[:c]) for c in range(len(CHUNKS))]

    smem = pl.BlockSpec(memory_space=pltpu.SMEM)
    vmem = pl.BlockSpec(memory_space=pltpu.VMEM)
    hbm = pl.BlockSpec(memory_space=pltpu.HBM)
    shape = jax.ShapeDtypeStruct
    dma = pltpu.SemaphoreType.DMA
    params = lambda mib: pltpu.CompilerParams(vmem_limit_bytes=mib * MIB)

    small_cost = pl.CostEstimate(flops=1, bytes_accessed=1, transcendentals=0)

    rows = lambda width: width * terms * size
    chunk = lambda c: (rows(CHUNKS[c]) + (own * size + terms if c == 0 else 0), size)
    chunks = lambda some: [pltpu.VMEM(chunk(c), f32) for c in some for _ in range(2)]
    in_hbm = lambda *values: [
        pltpu.with_memory_space_constraint(value, pltpu.HBM) for value in values
    ]
    opened = pl.pallas_call(
        functools.partial(open_kernel, CHUNKS[0], parts),
        in_specs=[hbm] * 5,
        out_specs=[vmem] * 2,
        out_shape=chunks([0]),
        scratch_shapes=[
            pltpu.VMEM(mpo_bond.shape, f32),
            dma((2, CHUNKS[0])),
            dma((2, own)),
            dma((1,)),
        ],
        cost_estimate=small_cost,
        compiler_params=params(4),
        name="open",
    )(*in_hbm(mpo_bond, left_tensor, right_tensor, left_env, right_env))
    later = range(1, len(CHUNKS))
    table, *picked = pl.pallas_call(
        functools.partial(pick_kernel, CHUNKS, parts),
        in_specs=[hbm] * 4,
        out_specs=[smem] + [vmem] * (2 * len(later)),
        out_shape=[shape((HEAD + 7 * total,), jnp.int32)] + chunks(later),
        scratch_shapes=[
            pltpu.SMEM(sectors.shape, jnp.int32),
            pltpu.SMEM(flow.shape, jnp.int32),
            pltpu.SMEM((2 * total,), jnp.int32),
            pltpu.SMEM((3 * 7 * (total + 1),), jnp.int32),
            dma((2, total)),
            dma((2,)),
        ],
        cost_estimate=small_cost,
        compiler_params=params(4),
        name="pick",
    )(*in_hbm(sectors, flow, left_env, right_env))
    opened = list(opened) + picked
    sent = [tuple(opened[2 * c : 2 * c + 2]) for c in range(len(CHUNKS))]
    states = gather(state)
    got = [tuple(hand_over(block, side) for side, block in enumerate(pair)) for pair in sent]

    tail = [block[rows(CHUNKS[0]) :] for block in got[0]]
    swap = table[3] == 1
    from_left, from_right = jnp.where(swap, tail[1], tail[0]), jnp.where(swap, tail[0], tail[1])
    small = jnp.eye(terms, dtype=f32)
    bond_left = jnp.where(table[0] == 1, small, from_left[own * size :, : mpo_bond.shape[1]])
    bond_right = jnp.where(table[1] == 1, small, from_right[own * size :, : mpo_bond.shape[1]])
    bond = jnp.sum(bond_left[:, None, :] * bond_right[None, :, :], axis=2)
    bond = jnp.broadcast_to(bond[:, :, None, None], (terms, terms, 8, size))
    flags = jnp.concatenate(
        [
            table[0:2],
            table[3:4],
            (
                table[HEAD + 2 * total : HEAD + 3 * total][None, :]
                == table[2] * own + jnp.arange(own, dtype=jnp.int32)[:, None]
            ).astype(jnp.int32).reshape(-1),
        ]
    )
    flags = jnp.broadcast_to(flags[:, None, None], (3 + own * total, 8, size))
    tensors = lambda block: block[: own * size].reshape(own, size, size)
    pieces = gather(jnp.stack([tensors(from_left), tensors(from_right)], 1))

    vec, plain, left, right, back, diagonal, mine = pl.pallas_call(
        functools.partial(prepare_kernel, own),
        in_specs=[smem] + [vmem] * 3,
        out_specs=[vmem] * 7,
        out_shape=[
            shape((total, size, size), f32),
            shape((total, size, size), f32),
            shape((total, size, 2 * size), bf16),
            shape((total, 2 * size, 2 * size), bf16),
            shape((total, 2, size, size), f32),
            shape((total, size, size), f32),
            shape((own, size, size), f32),
        ],
        cost_estimate=small_cost,
        compiler_params=params(12),
        name="prepare",
    )(table, states, pieces, onsite)

    def early(begin, width, image, part, env, mixed, after):
        image, _ = lax.optimization_barrier((image, after))
        return pl.pallas_call(
            functools.partial(early_kernel, begin) if begin == 0 else functools.partial(
                early_kernel, begin, None
            ),
            in_specs=([smem] + [vmem] * 2 if begin == 0 else []) + [vmem] * 9,
            out_specs=[vmem] * 2,
            out_shape=[shape((width, size, size), f32), shape((8, 8, 128), f32)],
            scratch_shapes=[pltpu.VMEM((width, size, size), f32)] * 2,
            cost_estimate=small_cost,
            compiler_params=params(12),
            name="early_second_matvec",
        )(*([slots] if begin == 0 else []), image, part, vec, plain, left, right, diagonal, env, mixed, *(before if begin == 0 else []))

    resids, stats, waits, held = [], [], [], None
    slots = table[HEAD + 5 * total : HEAD + 7 * total]
    groups = (CHUNKS[0] + CHUNKS[1],) + CHUNKS[2:]
    for c, (begin, width) in enumerate(zip([0] + begins[2:], groups)):
        if c > 0:
            got[c + 1], _ = lax.optimization_barrier((got[c + 1], waits[c - 1]))
            kernel, ahead = functools.partial(first_kernel, begin), [vmem] * 6
            operands = (flags, bond, *got[c + 1], *sent[c + 1])
        else:
            split = shape((CHUNKS[0], rows(1), 2 * size), bf16)
            kernel, ahead = paired_kernel, [smem] + [vmem] * 8
            before = pl.pallas_call(
                split_kernel,
                in_specs=[vmem] * 6,
                out_specs=[vmem] * 2,
                out_shape=[split, split],
                cost_estimate=small_cost,
                compiler_params=params(12),
                name="split",
            )(flags, bond, *got[0], *sent[0])
            operands = (slots, flags, bond, *got[1], *sent[1], *before)
        env, mixed, part = pl.pallas_call(
            kernel,
            in_specs=ahead + [vmem] * 4,
            out_specs=[vmem] * 3,
            out_shape=[
                shape((CHUNKS[c + 1], rows(1), 2 * size), bf16),
                shape((CHUNKS[c + 1], rows(1), 2 * size), bf16),
                shape((width, size, size), f32),
            ],
            cost_estimate=small_cost,
            compiler_params=params(12),
            name=f"first_matvec{c}",
        )(*operands, plain, vec, back, diagonal)
        if held is not None:
            resid, stat = early(*held, after=part)
            resids.append(resid)
            stats.append(stat)
        if c < len(groups) - 1:
            beside = part + partner(part, 1)
            image = beside + partner(beside, 2)
            held = (begin, width, image, part, env, mixed)
            waits.append([beside if c == len(groups) - 2 else image] + stats[-1:])

    beside = part + partner(part, 1)
    parts = [beside, partner(beside, 2)]
    second, share = pl.pallas_call(
        functools.partial(second_kernel, own, groups[:-1]),
        in_specs=[vmem] * (9 + 2 * (len(groups) - 1)),
        out_specs=[vmem] * 2,
        out_shape=[shape((own, size, size), f32), shape((3, 8, 128), f32)],
        scratch_shapes=[pltpu.VMEM((total, size, size), f32)],
        cost_estimate=small_cost,
        compiler_params=params(12),
        name="second_matvec",
    )(flags, *parts, vec, left, right, diagonal, env, mixed, *resids, *stats)

    shares = [share] + [partner(share[:1], mask) for mask in (1, 2, 3)]
    new_state, energy = pl.pallas_call(
        functools.partial(final_kernel, total * size * size),
        in_specs=[vmem] * 6,
        out_specs=[vmem, smem],
        out_shape=[shape((own, size, size), f32), shape((1,), f32)],
        cost_estimate=small_cost,
        compiler_params=params(4),
        name="ritz_update",
    )(*shares, mine, second)
    return (new_state, energy)


def solution(mesh):
    return jax.shard_map(
        on_device,
        mesh=mesh,
        in_specs=(
            P(("groups", "sites"), None, None),
            P(("groups", "sites"), None, None),
            P(("groups", "sites"), None, None),
            P(("groups", "sites"), None, None),
            P(("groups", "sites"), None, None, None),
            P(("groups", "sites"), None, None, None),
            P(("groups", "sites"), None),
            P("groups", None),
            P("groups", None),
        ),
        out_specs=(P(("groups", "sites"), None, None), P(("groups", "sites"))),
        check_vma=False,
    )
```

```python
import functools
import math

import jax
import jax.numpy as jnp
from jax import lax
from jax.experimental import pallas as pl
from jax.experimental.pallas import tpu as pltpu
from jax.sharding import PartitionSpec as P

GROUP = 4
CHUNKS = (2, 3, 2, 1)
MIB = 1024 * 1024


def hand_over(block, parity):
    count = lax.axis_size("sites")
    route = [(i, i + (GROUP if i % 2 == parity else -GROUP)) for i in range(count)]
    return lax.ppermute(block, "sites", [(i, j) for i, j in route if 0 <= j < count])


def partner(block, mask):
    route = [(i, i ^ mask) for i in range(lax.axis_size("sites"))]
    return lax.ppermute(block, "sites", route)


def gather(block):
    pieces = [block] + [partner(block, mask) for mask in (1, 2, 3)]
    return jnp.stack(pieces, 0)


def total_of(block):
    pair = block + partner(block, 1)
    return pair + partner(pair, 2)


def halves(value):
    high = value.astype(jnp.bfloat16)
    return high, (value - high.astype(jnp.float32)).astype(jnp.bfloat16)


def split_left(value):
    return jnp.concatenate(halves(value), axis=1)


def split_right(value):
    high, low = halves(value)
    return jnp.concatenate(
        [
            jnp.concatenate([high, low], axis=1),
            jnp.concatenate([high, jnp.zeros_like(low)], axis=1),
        ],
        axis=0,
    )


def fold(wide):
    half = wide.shape[1] // 2
    return wide[:, :half] + wide[:, half:]


def product(left, right):
    return fold(jnp.dot(split_left(left), split_right(right), preferred_element_type=jnp.float32))


def inward(block, left, right):
    temp = fold(jnp.dot(left, split_right(block), preferred_element_type=jnp.float32))
    return fold(jnp.dot(split_left(temp), right, preferred_element_type=jnp.float32))


def core_of(env_split, mixed_split, middle_split, terms):
    size = mixed_split.shape[0] // terms
    temp = fold(jnp.dot(env_split, middle_split, preferred_element_type=jnp.float32))
    high, low = halves(temp)
    wide = lambda part: jnp.concatenate(
        [part[m * size : (m + 1) * size] for m in range(terms)], axis=1
    )
    out = jnp.dot(
        jnp.concatenate([wide(high), wide(low)], axis=0),
        mixed_split,
        preferred_element_type=jnp.float32,
    )
    return fold(out[:size]) + out[size:, :size]


HEAD = 4


def sector_copy(env, index, out, row, sem):
    terms, _, size, _ = env.shape
    target = out.at[pl.ds(row, terms * size)].reshape(terms, size, size)
    return pltpu.make_async_copy(env.at[:, index], target, sem)


def ends(parts):
    position = lax.axis_index("sites")
    partition = position // GROUP
    return partition, partition == 0, partition == parts - 1, position % 2 == 1


def open_kernel(
    width, parts, bond_hbm, left_tensor, right_tensor, left_env, right_env, out0, out1,
    bond, sems, more, some,
):
    own, size = left_tensor.shape[0], left_tensor.shape[1]
    terms = left_env.shape[0]
    base = width * terms * size
    _, first, last, swap = ends(parts)
    load = pltpu.make_async_copy(bond_hbm, bond, some.at[0])
    ahead, behind = jnp.logical_not(last), first
    copies = []

    def start(flag, one, other):
        pl.when(flag)(one.start)
        pl.when(jnp.logical_not(flag))(other.start)
        copies.append(one)

    for side, out in enumerate((out0, out1)):
        crossed = swap if side == 0 else jnp.logical_not(swap)
        from_left = jnp.logical_or(
            jnp.logical_and(jnp.logical_not(crossed), ahead), jnp.logical_and(crossed, behind)
        )
        for i in range(width):
            place = (i, out, i * terms * size, sems.at[side, i])
            start(from_left, sector_copy(left_env, *place), sector_copy(right_env, *place))
        for i in range(own):
            target = out.at[pl.ds(base + i * size, size)]
            start(
                jnp.logical_not(crossed),
                pltpu.make_async_copy(left_tensor.at[i], target, more.at[side, i]),
                pltpu.make_async_copy(right_tensor.at[i], target, more.at[side, i]),
            )
    load.start()
    load.wait()
    for out in (out0, out1):
        rows = slice(base + own * size, base + own * size + terms)
        out[rows] = jnp.zeros((terms, size), jnp.float32)
        out[rows, : bond.shape[1]] = bond[...]
    for copy in copies:
        copy.wait()


def pick_kernel(
    chunks, parts, sectors_hbm, flow_hbm, left_env, right_env, table, *refs
):
    outs, (sectors, flow, turned, lists, sems, some) = refs[:-6], refs[-6:]
    terms, total, size = left_env.shape[:3]
    width = chunks[0]
    paired = width + chunks[1]
    partition, first, last, swap = ends(parts)
    loads = [
        pltpu.make_async_copy(sectors_hbm, sectors, some.at[0]),
        pltpu.make_async_copy(flow_hbm, flow, some.at[1]),
    ]
    for copy in loads:
        copy.start()
    for copy in loads:
        copy.wait()
    as_int = lambda flag: flag.astype(jnp.int32)
    table[0] = as_int(first)
    table[1] = as_int(last)
    table[2] = lax.axis_index("sites") % GROUP
    table[3] = as_int(swap)
    step = total + 1

    def orders(which, index):
        index = jnp.clip(index, 0, parts - 1)
        base = which * 7 * step
        before, after = jnp.maximum(index - 1, 0), jnp.minimum(index + 1, parts - 1)
        for j in range(total):
            turned[flow[before, j]] = j
            turned[total + flow[after, j]] = j
        lefts, rights = [], []
        for t in range(total):
            joined = sectors[index, t]
            lefts.append(jnp.where(index == 0, t, turned[t]))
            rights.append(jnp.where(index == parts - 1, joined, turned[total + joined]))
        count = jnp.int32(0)
        known = [jnp.logical_or(a < width, b < width) for a, b in zip(lefts, rights)]
        for wanted in (True, False):
            for t in range(total):
                lists[base + count] = lefts[t]
                lists[base + step + count] = rights[t]
                lists[base + 2 * step + count] = t
                count = count + as_int(known[t] if wanted else jnp.logical_not(known[t]))
        for side in range(2):
            count = jnp.int32(width)
            for i in range(width):
                lists[base + (3 + side) * step + i] = i
            for i in range(paired):
                source = lists[base + side * step + i]
                lists[base + (3 + side) * step + count] = source
                late = source >= width
                lists[base + (5 + side) * step + i] = jnp.where(late, count, source)
                count = count + as_int(late)
            for i in range(paired, total):
                lists[base + (3 + side) * step + i] = lists[base + side * step + i]
        return base

    behind_base = orders(0, partition - 1)
    here = orders(1, partition)
    ahead_base = orders(2, partition + 1)
    for i in range(total):
        for row, source in ((0, 0), (1, 1), (2, 2), (5, 5), (6, 6)):
            table[HEAD + row * total + i] = lists[here + source * step + i]
        ahead = jnp.where(last, lists[here + 4 * step + i], lists[ahead_base + 3 * step + i])
        behind = jnp.where(first, lists[here + 3 * step + i], lists[behind_base + 4 * step + i])
        table[HEAD + 3 * total + i] = jnp.where(swap, behind, ahead)
        table[HEAD + 4 * total + i] = jnp.where(swap, ahead, behind)
    ahead, behind = last.astype(jnp.int32), 1 - first.astype(jnp.int32)
    copies = []
    begin = width
    for c, count in enumerate(chunks[1:]):
        for side in range(2):
            kinds = (ahead, behind) if side == 0 else (behind, ahead)
            from_left = jnp.where(swap, kinds[1], kinds[0]) == 0
            for i in range(count):
                place = (
                    table[HEAD + (3 + side) * total + begin + i], outs[2 * c + side],
                    i * terms * size, sems.at[side, begin + i],
                )
                left, right = sector_copy(left_env, *place), sector_copy(right_env, *place)
                pl.when(from_left)(left.start)
                pl.when(jnp.logical_not(from_left))(right.start)
                copies.append(left)
        begin += count
    for copy in copies:
        copy.wait()


def prepare_kernel(
    own, table, states, pieces, onsite, vec_out, plain_out, left_out, right_out,
    back_out, diagonal_out, mine_out,
):
    total, size = vec_out.shape[0], vec_out.shape[1]
    row = lax.broadcasted_iota(jnp.int32, (size, size), 0)
    col = lax.broadcasted_iota(jnp.int32, (size, size), 1)
    eye = (row == col).astype(jnp.float32)
    member = table[2]

    def block(sector, kind):
        return pieces[(sector // own) ^ member, sector % own, kind]

    square = jnp.zeros((size, size), jnp.float32)
    for j in range(total):
        value = states[(j // own) ^ member, j % own]
        square = square + value * value
    norm = jnp.sqrt(jnp.full((8, size), jnp.sum(square), jnp.float32))[0:1]

    for j in range(total):
        target = table[HEAD + 2 * total + j]
        vec_out[j] = states[(target // own) ^ member, target % own] / norm
        diagonal_out[j] = jnp.where(target // own == member, onsite[target % own], 0.0)
        left = jnp.where(table[0] == 1, eye, block(table[HEAD + j], 0))
        right = jnp.where(table[1] == 1, eye, block(table[HEAD + total + j], 1))
        left_out[j] = split_left(left)
        right_out[j] = split_right(right)
        back_out[j, 0] = jnp.transpose(left)
        back_out[j, 1] = jnp.transpose(right)
    for i in range(own):
        mine_out[i] = states[0, i] / norm
    for j in range(total):
        plain_out[j] = inward(vec_out[j], left_out[j], right_out[j])


def chooser(flags, got0, got1, sent0, sent1, terms, size):
    flag = lambda k: jnp.broadcast_to(flags[k, 0:1] != 0, (size, size))
    first, last, swap = flag(0), flag(1), flag(2)

    def chosen(s, m, end, sent_a, sent_b, got_a, got_b):
        at = slice((s * terms + m) * size, (s * terms + m + 1) * size)
        there = jnp.where(swap, got_b[at], got_a[at])
        return jnp.where(end, jnp.where(swap, sent_b[at], sent_a[at]), there)

    left_of = lambda s, m: chosen(s, m, first, sent1, sent0, got0, got1)
    right_of = lambda s, m: chosen(s, m, last, sent0, sent1, got1, got0)
    return left_of, right_of


def spread(s, slot, bond, env_out, mixed_out, left_of, right_of):
    terms, size = bond.shape[0], bond.shape[-1]

    def weighted(m, k, block):
        tiles = block.reshape(size // 8, 8, size)
        return (tiles * bond[m, k][None]).reshape(size, size)

    rows = lambda m: slice(m * size, (m + 1) * size)
    for m in range(terms):
        env_out[slot, rows(m)] = split_left(left_of(s, m))
    blocks = [right_of(s, m) for m in range(terms)]
    for m in range(terms):
        total = weighted(m, 0, blocks[0])
        for k in range(1, terms):
            total = total + weighted(m, k, blocks[k])
        mixed_out[slot, rows(m)] = split_left(total)


def image_of(j, env, mixed, terms, plain, vec, back, diagonal):
    core = core_of(env, mixed, split_right(plain[j]), terms)
    return product(product(back[j, 0], core), back[j, 1]) + diagonal[j] * vec[j]


def either(before, after, slot):
    count = before.shape[0]
    late = slot >= count
    return jnp.where(
        late, after[jnp.maximum(slot - count, 0)], before[jnp.minimum(slot, count - 1)]
    )


def split_kernel(flags, bond, got0, got1, sent0, sent1, env_out, mixed_out):
    terms, size = bond.shape[0], bond.shape[-1]
    left_of, right_of = chooser(flags, got0, got1, sent0, sent1, terms, size)
    for s in range(env_out.shape[0]):
        spread(s, s, bond, env_out, mixed_out, left_of, right_of)


def first_kernel(
    begin, flags, bond, got0, got1, sent0, sent1, plain, vec, back, diagonal,
    env_out, mixed_out, part_out,
):
    terms, size = bond.shape[0], bond.shape[-1]
    left_of, right_of = chooser(flags, got0, got1, sent0, sent1, terms, size)
    for s in range(part_out.shape[0]):
        spread(s, s, bond, env_out, mixed_out, left_of, right_of)
        part_out[s] = image_of(
            begin + s, env_out[s], mixed_out[s], terms, plain, vec, back, diagonal
        )


def paired_kernel(
    slots, flags, bond, got0, got1, sent0, sent1, env_before, mixed_before,
    plain, vec, back, diagonal, env_out, mixed_out, part_out,
):
    terms, size = bond.shape[0], bond.shape[-1]
    total = vec.shape[0]
    left_of, right_of = chooser(flags, got0, got1, sent0, sent1, terms, size)
    for s in range(env_out.shape[0]):
        spread(s, s, bond, env_out, mixed_out, left_of, right_of)
    for j in range(part_out.shape[0]):
        env = either(env_before, env_out, slots[j])
        mixed = either(mixed_before, mixed_out, slots[total + j])
        part_out[j] = image_of(j, env, mixed, terms, plain, vec, back, diagonal)


def early_kernel(
    begin, slots, image, part, vec, middle, left, right, diagonal, env, mixed, *refs
):
    before, (resid_out, stat_out, moved, cores) = refs[:-4], refs[-4:]
    width, size = image.shape[0], image.shape[1]
    terms = mixed.shape[1] // size
    zero = jnp.zeros((size, size), jnp.float32)
    tile = lambda value: jnp.full((8, 128), value, jnp.float32)

    along, norm = zero, zero
    for i in range(width):
        along = along + vec[begin + i] * image[i]
        norm = norm + vec[begin + i] * vec[begin + i]
    along, norm = jnp.sum(along), jnp.sum(norm)
    guess = jnp.where(norm > 0, along / jnp.where(norm > 0, norm, 1.0), 0.0)
    left_over, square = zero, zero
    for i in range(width):
        resid = image[i] - guess * vec[begin + i]
        resid_out[i] = resid
        left_over = left_over + resid * vec[begin + i]
        square = square + resid * resid
    square = tile(jnp.sum(square))
    length = jnp.sqrt(square + 1e-06)
    scale = (1.0 / length)[0:1]
    stat_out[0] = tile(guess)
    stat_out[1] = tile(norm)
    stat_out[2] = tile(jnp.sum(left_over))
    stat_out[3] = square
    stat_out[4] = length

    for i in range(width):
        resid = resid_out[i] * scale
        resid_out[i] = resid
        moved[i] = inward(resid, left[begin + i], right[begin + i])
    for i in range(width):
        if slots is None:
            sides = env[i], mixed[i]
        else:
            sides = (
                either(before[0], env, slots[i]),
                either(before[1], mixed, slots[vec.shape[0] + i]),
            )
        cores[i] = core_of(*sides, split_right(moved[i]), terms)
    shares = lambda i: diagonal[begin + i]
    both = zero
    for i in range(width):
        resid = resid_out[i]
        both = both + moved[i] * cores[i] + (shares(i) * resid) * resid
    stat_out[5] = tile(jnp.sum(both))
    cross = zero
    for i in range(width):
        resid = resid_out[i]
        cross = cross + middle[begin + i] * cores[i]
        cross = cross + resid * (part[i] + shares(i) * vec[begin + i])
    stat_out[6] = tile(jnp.sum(cross))
    plain = zero
    for i in range(width):
        plain = plain + vec[begin + i] * part[i]
    stat_out[7] = tile(jnp.sum(plain))


def second_kernel(
    own, widths, flags, part0, part1, vec, left, right, diagonal, env, mixed, *refs
):
    count = len(widths)
    resids, stats = refs[:count], refs[count : 2 * count]
    second_out, share_out, work = refs[2 * count :]
    total, size, late = vec.shape[0], vec.shape[1], part0.shape[0]
    early = total - late
    terms = mixed.shape[1] // size
    zero = jnp.zeros((size, size), jnp.float32)
    tile = lambda value: jnp.full((8, 128), value, jnp.float32)

    images = [part0[i] + part1[i] for i in range(late)]
    along = zero
    for i in range(late):
        along = along + vec[early + i] * images[i]
    alpha1 = tile(jnp.sum(along))
    for stat in stats:
        alpha1 = alpha1 + (stat[0] * stat[1] + stat[2])
    rest = zero
    for i in range(late):
        images[i] = images[i] - alpha1[0:1] * vec[early + i]
        rest = rest + images[i] * images[i]
    square = tile(jnp.sum(rest)) + 1e-06
    for stat in stats:
        away = alpha1 - stat[0]
        square = square + jnp.maximum(
            stat[3] - 2.0 * away * stat[2] + away * (away * stat[1]), 0.0
        )
    beta = jnp.sqrt(square)
    scale = (1.0 / beta)[0:1]
    share = zero
    for i in range(late):
        j = early + i
        value = images[i] * scale
        work[j] = value
        moved = inward(value, left[j], right[j])
        core = core_of(env[i], mixed[i], split_right(moved), terms)
        share = share + moved * core + (diagonal[j] * value) * value
    begin = 0
    sums = zero[:8]
    for resid, stat, width in zip(resids, stats, widths):
        long, off = stat[4] / beta, (alpha1 - stat[0]) / beta
        sums = sums + long * (long * stat[5]) - off * (long * stat[6]) + off * (off * stat[7])
        for i in range(width):
            work[begin + i] = long[0:1] * resid[i] - off[0:1] * vec[begin + i]
        begin += width
    share_out[0] = tile(jnp.sum(share)) + sums
    share_out[1] = alpha1
    share_out[2] = beta
    for i in range(own):
        mine = work[0]
        for j in range(1, total):
            mine = jnp.where(flags[3 + i * total + j, 0:1] != 0, work[j], mine)
        second_out[i] = mine


def final_kernel(count, share0, share1, share2, share3, mine, second, out, energy_out):
    alpha2 = (share0[0] + share1[0]) + (share2[0] + share3[0])
    alpha1, beta = share0[1], share0[2]
    energy = (alpha1 + alpha2) / 2.0 - jnp.sqrt(((alpha1 - alpha2) / 2.0) ** 2 + beta * beta)
    height = jnp.sqrt(beta * beta + (energy - alpha1) ** 2)
    scale = math.sqrt(count)
    weight1 = (scale * (beta / height))[0:1]
    weight2 = (scale * ((energy - alpha1) / height))[0:1]
    for i in range(out.shape[0]):
        out[i] = weight1 * mine[i] + weight2 * second[i]
    energy_out[0] = energy[0, 0]


def on_device(
    state, left_tensor, right_tensor, onsite, left_env, right_env, mpo_bond, sectors, flow
):
    parts = lax.axis_size("sites") // GROUP
    own, size = state.shape[0], state.shape[1]
    terms, total = left_env.shape[0], left_env.shape[1]
    f32, bf16 = jnp.float32, jnp.bfloat16
    begins = [sum(CHUNKS[:c]) for c in range(len(CHUNKS))]

    smem = pl.BlockSpec(memory_space=pltpu.SMEM)
    vmem = pl.BlockSpec(memory_space=pltpu.VMEM)
    hbm = pl.BlockSpec(memory_space=pltpu.HBM)
    shape = jax.ShapeDtypeStruct
    dma = pltpu.SemaphoreType.DMA
    params = lambda mib: pltpu.CompilerParams(vmem_limit_bytes=mib * MIB)

    small_cost = pl.CostEstimate(flops=1, bytes_accessed=1, transcendentals=0)

    rows = lambda width: width * terms * size
    chunk = lambda c: (rows(CHUNKS[c]) + (own * size + terms if c == 0 else 0), size)
    chunks = lambda some: [pltpu.VMEM(chunk(c), f32) for c in some for _ in range(2)]
    in_hbm = lambda *values: [
        pltpu.with_memory_space_constraint(value, pltpu.HBM) for value in values
    ]
    opened = pl.pallas_call(
        functools.partial(open_kernel, CHUNKS[0], parts),
        in_specs=[hbm] * 5,
        out_specs=[vmem] * 2,
        out_shape=chunks([0]),
        scratch_shapes=[
            pltpu.VMEM(mpo_bond.shape, f32),
            dma((2, CHUNKS[0])),
            dma((2, own)),
            dma((1,)),
        ],
        cost_estimate=small_cost,
        compiler_params=params(4),
        name="open",
    )(*in_hbm(mpo_bond, left_tensor, right_tensor, left_env, right_env))
    later = range(1, len(CHUNKS))
    table, *picked = pl.pallas_call(
        functools.partial(pick_kernel, CHUNKS, parts),
        in_specs=[hbm] * 4,
        out_specs=[smem] + [vmem] * (2 * len(later)),
        out_shape=[shape((HEAD + 7 * total,), jnp.int32)] + chunks(later),
        scratch_shapes=[
            pltpu.SMEM(sectors.shape, jnp.int32),
            pltpu.SMEM(flow.shape, jnp.int32),
            pltpu.SMEM((2 * total,), jnp.int32),
            pltpu.SMEM((3 * 7 * (total + 1),), jnp.int32),
            dma((2, total)),
            dma((2,)),
        ],
        cost_estimate=small_cost,
        compiler_params=params(4),
        name="pick",
    )(*in_hbm(sectors, flow, left_env, right_env))
    opened = list(opened) + picked
    sent = [tuple(opened[2 * c : 2 * c + 2]) for c in range(len(CHUNKS))]
    states = gather(state)
    got = [tuple(hand_over(block, side) for side, block in enumerate(pair)) for pair in sent]

    tail = [block[rows(CHUNKS[0]) :] for block in got[0]]
    swap = table[3] == 1
    from_left, from_right = jnp.where(swap, tail[1], tail[0]), jnp.where(swap, tail[0], tail[1])
    small = jnp.eye(terms, dtype=f32)
    bond_left = jnp.where(table[0] == 1, small, from_left[own * size :, : mpo_bond.shape[1]])
    bond_right = jnp.where(table[1] == 1, small, from_right[own * size :, : mpo_bond.shape[1]])
    bond = jnp.sum(bond_left[:, None, :] * bond_right[None, :, :], axis=2)
    bond = jnp.broadcast_to(bond[:, :, None, None], (terms, terms, 8, size))
    flags = jnp.concatenate(
        [
            table[0:2],
            table[3:4],
            (
                table[HEAD + 2 * total : HEAD + 3 * total][None, :]
                == table[2] * own + jnp.arange(own, dtype=jnp.int32)[:, None]
            ).astype(jnp.int32).reshape(-1),
        ]
    )
    flags = jnp.broadcast_to(flags[:, None, None], (3 + own * total, 8, size))
    tensors = lambda block: block[: own * size].reshape(own, size, size)
    pieces = gather(jnp.stack([tensors(from_left), tensors(from_right)], 1))

    vec, plain, left, right, back, diagonal, mine = pl.pallas_call(
        functools.partial(prepare_kernel, own),
        in_specs=[smem] + [vmem] * 3,
        out_specs=[vmem] * 7,
        out_shape=[
            shape((total, size, size), f32),
            shape((total, size, size), f32),
            shape((total, size, 2 * size), bf16),
            shape((total, 2 * size, 2 * size), bf16),
            shape((total, 2, size, size), f32),
            shape((total, size, size), f32),
            shape((own, size, size), f32),
        ],
        cost_estimate=small_cost,
        compiler_params=params(12),
        name="prepare",
    )(table, states, pieces, onsite)

    def early(begin, width, image, part, env, mixed, after):
        image, _ = lax.optimization_barrier((image, after))
        return pl.pallas_call(
            functools.partial(early_kernel, begin) if begin == 0 else functools.partial(
                early_kernel, begin, None
            ),
            in_specs=([smem] + [vmem] * 2 if begin == 0 else []) + [vmem] * 9,
            out_specs=[vmem] * 2,
            out_shape=[shape((width, size, size), f32), shape((8, 8, 128), f32)],
            scratch_shapes=[pltpu.VMEM((width, size, size), f32)] * 2,
            cost_estimate=small_cost,
            compiler_params=params(12),
            name="early_second_matvec",
        )(*([slots] if begin == 0 else []), image, part, vec, plain, left, right, diagonal, env, mixed, *(before if begin == 0 else []))

    resids, stats, waits, held = [], [], [], None
    slots = table[HEAD + 5 * total : HEAD + 7 * total]
    groups = (CHUNKS[0] + CHUNKS[1],) + CHUNKS[2:]
    for c, (begin, width) in enumerate(zip([0] + begins[2:], groups)):
        if c > 0:
            got[c + 1], _ = lax.optimization_barrier((got[c + 1], waits[c - 1]))
            kernel, ahead = functools.partial(first_kernel, begin), [vmem] * 6
            operands = (flags, bond, *got[c + 1], *sent[c + 1])
        else:
            split = shape((CHUNKS[0], rows(1), 2 * size), bf16)
            kernel, ahead = paired_kernel, [smem] + [vmem] * 8
            before = pl.pallas_call(
                split_kernel,
                in_specs=[vmem] * 6,
                out_specs=[vmem] * 2,
                out_shape=[split, split],
                cost_estimate=small_cost,
                compiler_params=params(12),
                name="split",
            )(flags, bond, *got[0], *sent[0])
            operands = (slots, flags, bond, *got[1], *sent[1], *before)
        env, mixed, part = pl.pallas_call(
            kernel,
            in_specs=ahead + [vmem] * 4,
            out_specs=[vmem] * 3,
            out_shape=[
                shape((CHUNKS[c + 1], rows(1), 2 * size), bf16),
                shape((CHUNKS[c + 1], rows(1), 2 * size), bf16),
                shape((width, size, size), f32),
            ],
            cost_estimate=small_cost,
            compiler_params=params(12),
            name=f"first_matvec{c}",
        )(*operands, plain, vec, back, diagonal)
        if held is not None:
            resid, stat = early(*held, after=part)
            resids.append(resid)
            stats.append(stat)
        if c < len(groups) - 1:
            near, far = (2, 1) if c == 0 else (1, 2)
            beside = part + partner(part, near)
            image = beside + partner(beside, far)
            held = (begin, width, image, part, env, mixed)
            waits.append([beside if c == len(groups) - 2 else image] + stats[-1:])

    beside = part + partner(part, 1)
    parts = [beside, partner(beside, 2)]
    second, share = pl.pallas_call(
        functools.partial(second_kernel, own, groups[:-1]),
        in_specs=[vmem] * (9 + 2 * (len(groups) - 1)),
        out_specs=[vmem] * 2,
        out_shape=[shape((own, size, size), f32), shape((3, 8, 128), f32)],
        scratch_shapes=[pltpu.VMEM((total, size, size), f32)],
        cost_estimate=small_cost,
        compiler_params=params(12),
        name="second_matvec",
    )(flags, *parts, vec, left, right, diagonal, env, mixed, *resids, *stats)

    shares = [share] + [partner(share[:1], mask) for mask in (1, 2, 3)]
    new_state, energy = pl.pallas_call(
        functools.partial(final_kernel, total * size * size),
        in_specs=[vmem] * 6,
        out_specs=[vmem, smem],
        out_shape=[shape((own, size, size), f32), shape((1,), f32)],
        cost_estimate=small_cost,
        compiler_params=params(4),
        name="ritz_update",
    )(*shares, mine, second)
    return (new_state, energy)


def solution(mesh):
    return jax.shard_map(
        on_device,
        mesh=mesh,
        in_specs=(
            P(("groups", "sites"), None, None),
            P(("groups", "sites"), None, None),
            P(("groups", "sites"), None, None),
            P(("groups", "sites"), None, None),
            P(("groups", "sites"), None, None, None),
            P(("groups", "sites"), None, None, None),
            P(("groups", "sites"), None),
            P("groups", None),
            P("groups", None),
        ),
        out_specs=(P(("groups", "sites"), None, None), P(("groups", "sites"))),
        check_vma=False,
    )
```
